32 devices in a mesh: tm: 16 (over z, y, core), space: 2 (over x).
Axes of the slice: x: 2, y: 2, z: 4, core: 2. Of those that a mesh axis runs over, the one named last changes fastest.
Arguments:
- c_points: float32 [32, 3, 64, 512], P('tm', None, 'space'), may hold values from -0.45 to 1.3, as said below
Outputs:
- updated: float32 [32, 3, 64, 512], P('tm', None, 'space')
- coarse_residual: float32 [32, 3, 2, 32, 512], P(None, None, 'space', 'tm')
The draws below stay inside these ranges and needn't reach their ends.
Inputs may be any that keep to these rules, and one draw needn't show every extreme that they name: `c_points`: the first field (height) lies in 0.7 to 1.3, the other two (momenta) in -0.45 to 0.45.
All inputs are finite; a program needn't handle non-finite values.
Results may differ from the reference program's by a relative error of at most 0.000028.
Values sent between devices are 32-bit elements; how exact they have to be, the bound alone decides.
No kernel may reach another device: no remote copies, remote signals or barrier semaphores. Data moves between devices by JAX's collectives and lax.ppermute only.
A program may use at most 64 MiB of HBM per device.

```python
import jax
import jax.numpy as jnp
from jax import lax

FACTOR = 8
STRIP_ROWS = 32
COLUMNS = 512
COARSE = 32
GRID_ROWS = 64
N_SPACE = 2


def draw_c_points(key, part):
    keys = jax.random.split(key, 3)
    shape = (COARSE, GRID_ROWS, COLUMNS)
    height = 1.0 + 0.3 * jax.random.uniform(keys[0], shape, jnp.float32, -1.0, 1.0)
    east_flow = jnp.clip(0.15 * jax.random.normal(keys[1], shape, jnp.float32), -0.45, 0.45)
    north_flow = jnp.clip(0.15 * jax.random.normal(keys[2], shape, jnp.float32), -0.45, 0.45)
    return jnp.stack([height, east_flow, north_flow], axis=1).astype(jnp.float32)


def setup_inputs(seed: int = 0) -> dict:
    key_of = jax.random.split(jax.random.key(seed), 2)
    c_points = draw_c_points(jax.random.fold_in(key_of[1], 71), 0)
    return dict(c_points=c_points)


gravity = 1.0
half_ratio = 0.1


def column_flux(state):
    height = state[..., 0, :, :]
    east_flow = state[..., 1, :, :]
    north_flow = state[..., 2, :, :]
    velocity = east_flow / height
    return jnp.stack([east_flow, east_flow * velocity + 0.5 * gravity * height * height, north_flow * velocity], axis=-3)


def row_flux(state):
    height = state[..., 0, :, :]
    east_flow = state[..., 1, :, :]
    north_flow = state[..., 2, :, :]
    velocity = north_flow / height
    return jnp.stack([north_flow, east_flow * velocity, north_flow * velocity + 0.5 * gravity * height * height], axis=-3)


def flux_step(extended):
    center = extended[..., 1:-1, :]
    upper_row = extended[..., 2:, :]
    lower_row = extended[..., :-2, :]
    right_cells = jnp.roll(center, -1, axis=-1)
    left_cells = jnp.roll(center, 1, axis=-1)
    average = 0.25 * (upper_row + lower_row + right_cells + left_cells)
    return average - half_ratio * (column_flux(right_cells) - column_flux(left_cells)) - half_ratio * (row_flux(upper_row) - row_flux(lower_row))


def propagate(state):
    for step in range(FACTOR):
        extended = jnp.concatenate([state[:, -1:, :], state, state[:, :1, :]], axis=1)
        state = flux_step(extended)
    return state


def reference(c_points):
    advanced = lax.map(propagate, c_points)
    updated = jnp.concatenate([c_points[:1], advanced[:-1]], axis=0)
    pushed = lax.map(propagate, updated)
    residual = (pushed - advanced).reshape(COARSE, 3, N_SPACE, STRIP_ROWS, COLUMNS)
    return updated, residual
```

```python
import functools

import jax
import jax.numpy as jnp
from jax import lax
from jax.experimental import pallas as pl
from jax.experimental.pallas import tpu as pltpu
from jax.sharding import PartitionSpec as P

FACTOR = 8
LANES = 128
SUB = 8

MOMENTUM = 0.4
PRESSURE = 0.08


def reciprocal(x):
    r = pl.reciprocal(x, approx=True)
    return r * (2.0 - x * r)


def row_terms(read, chunks, factor, lane):
    north, south, east, west = [], [], [], []
    for c in range(chunks):
        h, p, q = read(0, c), read(1, c), read(2, c)
        r = reciprocal(h)
        u = p * r
        pressure = h * h * factor
        a = p * u + pressure
        b = q * u
        d = q * (q * r) + pressure
        east.append((h - p, p - a, q - b))
        west.append((h + p, p + a, q + b))
        north.append((h - q, p - b, q - d))
        south.append((h + q, p + b, q + d))
    level = []
    for c in range(chunks):
        after, before = (c + 1) % chunks, (c - 1) % chunks
        fields = []
        for f in range(3):
            e = jnp.where(lane == 0, east[after][f], east[c][f])
            w = jnp.where(lane == LANES - 1, west[before][f], west[c][f])
            fields.append(pltpu.roll(e, LANES - 1, 1) + pltpu.roll(w, 1, 1))
        level.append(tuple(fields))
    return north, south, level


def step(src, dst, held, points, depth, chunks, factor):
    lane = lax.broadcasted_iota(jnp.int32, (SUB, LANES), 1)
    cells = [(f, c) for f in range(3) for c in range(chunks)]
    for k in range(points):
        partial = south_before = None
        for i in range(depth):
            north, south, level = row_terms(
                lambda f, c: src[k, f, i, c], chunks, factor, lane
            )
            for f, c in cells:
                if i == 0:
                    held[k, f, c] = pltpu.roll(north[c][f], SUB - 1, 0)
                else:
                    dst[k, f, i - 1, c] = partial[c][f] + north[c][f]
            if i == 0:
                partial = level
            else:
                partial = [
                    tuple(level[c][f] + south_before[c][f] for f in range(3)) for c in range(chunks)
                ]
            south_before = south
        for f, c in cells:
            dst[k, f, depth - 1, c] = partial[c][f] + held[k, f, c]
            dst[k, f, 0, c] = dst[k, f, 0, c] + pltpu.roll(south_before[c][f], 1, 0)


def fill(ext, points, chunks, pieces):
    for k in range(points):
        start = 0
        for piece in pieces[k]:
            rows = piece.shape[1]
            for f in range(3):
                for c in range(chunks):
                    ext[k, f, c, start : start + rows, :] = piece[f, :, c * LANES : (c + 1) * LANES]
            start += rows


def propagate(ext, state, held, points, chunks):
    depth = ext.shape[3] // SUB
    cells = [(k, f, c, i) for k in range(points) for f in range(3) for c in range(chunks) for i in range(depth)]
    for k, f, c, i in cells:
        value = ext.at[k, f, c][pl.ds(i, SUB, stride=depth), :]
        state[0, k, f, i, c] = value if f == 0 else MOMENTUM * value

    def two(_, factor):
        step(state.at[0], state.at[1], held, points, depth, chunks, factor)
        factor = factor * 0.25
        step(state.at[1], state.at[0], held, points, depth, chunks, factor)
        return factor * 0.25

    lax.fori_loop(0, FACTOR // 2, two, jnp.float32(PRESSURE))
    shrink = 0.25**FACTOR
    for k, f, c, i in cells:
        value = state[0, k, f, i, c] * (shrink if f == 0 else shrink / MOMENTUM)
        ext.at[k, f, c][pl.ds(i, SUB, stride=depth), :] = value


def advance_kernel(points, chunks, own, low, high, out, ext, state, held):
    fill(ext, points, chunks, [(low.at[k], own.at[k], high.at[k]) for k in range(points)])
    propagate(ext, state, held, points, chunks)
    rows = own.shape[2]
    for k in range(points):
        for f in range(3):
            for c in range(chunks):
                out[k, f, :, c * LANES : (c + 1) * LANES] = ext[k, f, c, FACTOR : FACTOR + rows, :]


def residual_kernel(points, chunks, own, low, high, advanced, out, ext, state, held):
    fill(ext, points, chunks, [(low.at[k], own.at[k], high.at[k]) for k in range(points)])
    propagate(ext, state, held, points, chunks)
    rows = own.shape[2]
    for k in range(points):
        for f in range(3):
            for c in range(chunks):
                span = slice(c * LANES, (c + 1) * LANES)
                out[k, f, :, span] = ext[k, f, c, FACTOR : FACTOR + rows, :] - advanced[k, f, :, span]


def call(kernel, own, *others):
    points, fields, rows, columns = own.shape
    chunks = columns // LANES
    extended = rows + 2 * FACTOR
    cost = pl.CostEstimate(
        flops=points * extended * columns * FACTOR * 45,
        bytes_accessed=4 * points * fields * extended * columns * 2,
        transcendentals=points * extended * columns * FACTOR,
    )
    return pl.pallas_call(
        functools.partial(kernel, points, chunks),
        out_shape=jax.ShapeDtypeStruct(own.shape, own.dtype),
        in_specs=[pl.BlockSpec(memory_space=pltpu.VMEM)] * (1 + len(others)),
        out_specs=pl.BlockSpec(memory_space=pltpu.VMEM),
        scratch_shapes=[
            pltpu.VMEM((points, fields, chunks, extended, LANES), jnp.float32),
            pltpu.VMEM((2, points, fields, extended // SUB, chunks, SUB, LANES), jnp.float32),
            pltpu.VMEM((points, fields, chunks, SUB, LANES), jnp.float32),
        ],
        compiler_params=pltpu.CompilerParams(vmem_limit_bytes=24 * 2**20),
        cost_estimate=cost,
    )(own, *others)


def halos(block):
    count = lax.axis_size("space")
    forward = [(i, (i + 1) % count) for i in range(count)]
    backward = [(target, source) for source, target in forward]
    last, first = block[..., -FACTOR:, :], block[..., :FACTOR, :]
    return lax.ppermute(last, "space", forward), lax.ppermute(first, "space", backward)


def from_behind(block, axis, distance):
    devices = range(lax.axis_size(axis))
    route = [(i - distance, i) for i in devices if i - distance in devices]
    return lax.ppermute(block, axis, route)


def on_device(c_points):
    leading = lax.axis_index("tm") == 0
    low, high = halos(c_points)
    advanced = call(advance_kernel, c_points, low, high)
    incoming = from_behind(advanced[-1], "tm", 1)
    opening = jnp.where(leading, c_points[0], incoming)
    updated = jnp.concatenate([opening[None], advanced[:-1]], axis=0)
    low, high = halos(updated)
    residual = call(residual_kernel, updated, low, high, advanced)
    coarse = lax.all_to_all(residual, "tm", split_axis=2, concat_axis=0, tiled=True)
    return (updated, coarse[:, :, None])


def solution(mesh):
    in_specs = (P("tm", None, "space", None),)
    out_specs = (P("tm", None, "space", None), P(None, None, "space", "tm", None))
    return jax.shard_map(
        on_device, mesh=mesh, in_specs=in_specs, out_specs=out_specs, check_vma=False
    )
```

```python
import functools

import jax
import jax.numpy as jnp
from jax import lax
from jax.experimental import pallas as pl
from jax.experimental.pallas import tpu as pltpu
from jax.sharding import PartitionSpec as P

FACTOR = 8
LANES = 128
SUB = 8

MOMENTUM = 0.4
PRESSURE = 0.08


def reciprocal(x):
    r = pl.reciprocal(x, approx=True)
    return r * (2.0 - x * r)


def row_terms(read, chunks, factor, lane):
    north, south, east, west = [], [], [], []
    for c in range(chunks):
        h, p, q = read(0, c), read(1, c), read(2, c)
        r = reciprocal(h)
        u = p * r
        pressure = h * h * factor
        a = p * u + pressure
        b = q * u
        d = q * (q * r) + pressure
        east.append((h - p, p - a, q - b))
        west.append((h + p, p + a, q + b))
        north.append((h - q, p - b, q - d))
        south.append((h + q, p + b, q + d))
    level = []
    for c in range(chunks):
        after, before = (c + 1) % chunks, (c - 1) % chunks
        fields = []
        for f in range(3):
            e = jnp.where(lane == 0, east[after][f], east[c][f])
            w = jnp.where(lane == LANES - 1, west[before][f], west[c][f])
            fields.append(pltpu.roll(e, LANES - 1, 1) + pltpu.roll(w, 1, 1))
        level.append(tuple(fields))
    return north, south, level


def step(src, dst, held, points, depth, chunks, factor):
    lane = lax.broadcasted_iota(jnp.int32, (SUB, LANES), 1)
    cells = [(f, c) for f in range(3) for c in range(chunks)]
    for k in range(points):
        partial = south_before = None
        for i in range(depth):
            north, south, level = row_terms(
                lambda f, c: src[k, f, i, c], chunks, factor, lane
            )
            for f, c in cells:
                if i == 0:
                    held[k, f, c] = pltpu.roll(north[c][f], SUB - 1, 0)
                else:
                    dst[k, f, i - 1, c] = partial[c][f] + north[c][f]
            if i == 0:
                partial = level
            else:
                partial = [
                    tuple(level[c][f] + south_before[c][f] for f in range(3)) for c in range(chunks)
                ]
            south_before = south
        for f, c in cells:
            dst[k, f, depth - 1, c] = partial[c][f] + held[k, f, c]
            dst[k, f, 0, c] = dst[k, f, 0, c] + pltpu.roll(south_before[c][f], 1, 0)


def fill(ext, points, chunks, pieces):
    for k in range(points):
        start = 0
        for piece in pieces[k]:
            rows = piece.shape[1]
            for f in range(3):
                for c in range(chunks):
                    ext[k, f, c, start : start + rows, :] = piece[f, :, c * LANES : (c + 1) * LANES]
            start += rows


def propagate(ext, state, held, points, chunks):
    depth = ext.shape[3] // SUB
    cells = [(k, f, c, i) for k in range(points) for f in range(3) for c in range(chunks) for i in range(depth)]
    for k, f, c, i in cells:
        value = ext.at[k, f, c][pl.ds(i, SUB, stride=depth), :]
        state[0, k, f, i, c] = value if f == 0 else MOMENTUM * value

    def two(_, factor):
        step(state.at[0], state.at[1], held, points, depth, chunks, factor)
        factor = factor * 0.25
        step(state.at[1], state.at[0], held, points, depth, chunks, factor)
        return factor * 0.25

    lax.fori_loop(0, FACTOR // 2, two, jnp.float32(PRESSURE))
    shrink = 0.25**FACTOR
    for k, f, c, i in cells:
        value = state[0, k, f, i, c] * (shrink if f == 0 else shrink / MOMENTUM)
        ext.at[k, f, c][pl.ds(i, SUB, stride=depth), :] = value


def edges_of(block):
    return jnp.stack([block[..., -FACTOR:, :], block[..., :FACTOR, :]])


def spans(chunks):
    return [slice(c * LANES, (c + 1) * LANES) for c in range(chunks)]


def advance_kernel(points, chunks, own, halo, out, last, near, far, ext, state, held):
    fill(ext, points, chunks, [(halo.at[0, k], own.at[k], halo.at[1, k]) for k in range(points)])
    propagate(ext, state, held, points, chunks)
    rows = own.shape[2]
    for k in range(points):
        target, edge = (last, far) if k == points - 1 else (out.at[k], near.at[:, k])
        for f in range(3):
            for c, span in enumerate(spans(chunks)):
                target[f, :, span] = ext[k, f, c, FACTOR : FACTOR + rows, :]
                edge[0, f, :, span] = ext[k, f, c, rows : FACTOR + rows, :]
                edge[1, f, :, span] = ext[k, f, c, FACTOR : 2 * FACTOR, :]


def residual_kernel(
    points, chunks, groups, start, start_halo, incoming, incoming_halo, advanced, near, last, *rest
):
    messages, (ext, state, held, packed) = rest[:-4], rest[-4:]
    me = lax.axis_index("tm")

    @pl.when(me == 0)
    def _():
        fill(ext, 1, chunks, [(start_halo.at[0, 0], start.at[0], start_halo.at[1, 0])])

    @pl.when(me > 0)
    def _():
        fill(ext, 1, chunks, [(incoming_halo.at[0], incoming, incoming_halo.at[1])])

    fill(
        ext.at[pl.ds(1, points - 1)],
        points - 1,
        chunks,
        [(near.at[0, k], advanced.at[k], near.at[1, k]) for k in range(points - 1)],
    )
    propagate(ext, state, held, points, chunks)
    rows = last.shape[1]
    share = rows // groups
    for k in range(points):
        before = last if k == points - 1 else advanced.at[k]
        for f in range(3):
            for c, span in enumerate(spans(chunks)):
                value = ext[k, f, c, FACTOR : FACTOR + rows, :] - before[f, :, span]
                ext[k, f, c, FACTOR : FACTOR + rows, :] = value
                for g in range(groups):
                    base = FACTOR + g * share
                    packed[g, k, f, :, span] = ext[k, f, c, base : base + share, :]
    for d, message in enumerate(messages):
        message[...] = packed[target_of(me, d, groups)]


def target_of(i, d, count):
    return i ^ d if count & (count - 1) == 0 else (i + d) % count


def source_of(i, d, count):
    return i ^ d if count & (count - 1) == 0 else (i - d) % count


def gather_kernel(points, groups, *refs):
    messages, out, sems = refs[:-2], refs[-2], refs[-1]
    me = lax.axis_index("tm")
    copies = []
    for d, message in enumerate(messages):
        place = source_of(me, d, groups) * points
        copies.append(
            pltpu.make_async_copy(message, out.at[pl.ds(place, points), :, 0], sems.at[d])
        )
    for copy in copies:
        copy.start()
    for copy in copies:
        copy.wait()


VMEM = pl.BlockSpec(memory_space=pltpu.VMEM)


def call(kernel, shapes, points, rows, columns, operands, extra=()):
    chunks = columns // LANES
    extended = rows + 2 * FACTOR
    cost = pl.CostEstimate(
        flops=points * extended * columns * FACTOR * 45,
        bytes_accessed=4 * points * 3 * extended * columns * 2,
        transcendentals=points * extended * columns * FACTOR,
    )
    return pl.pallas_call(
        functools.partial(kernel, points, chunks),
        out_shape=[jax.ShapeDtypeStruct(shape, jnp.float32) for shape in shapes],
        in_specs=[VMEM] * len(operands),
        out_specs=[VMEM] * len(shapes),
        scratch_shapes=[
            pltpu.VMEM((points, 3, chunks, extended, LANES), jnp.float32),
            pltpu.VMEM((2, points, 3, extended // SUB, chunks, SUB, LANES), jnp.float32),
            pltpu.VMEM((points, 3, chunks, SUB, LANES), jnp.float32),
            *extra,
        ],
        compiler_params=pltpu.CompilerParams(vmem_limit_bytes=24 * 2**20),
        cost_estimate=cost,
    )(*operands)


def exchange(edges, shift):
    groups, strips = lax.axis_size("tm"), lax.axis_size("space")

    def route(move):
        return [
            (t * strips + s, (t + shift) * strips + (s + move) % strips)
            for t in range(groups - shift)
            for s in range(strips)
        ]

    both = ("tm", "space")
    if strips == 2:
        return lax.ppermute(edges, both, route(1))
    return jnp.stack(
        [lax.ppermute(edges[0], both, route(1)), lax.ppermute(edges[1], both, route(-1))]
    )


def on_device(c_points):
    points, fields, rows, columns = c_points.shape
    groups = lax.axis_size("tm")
    share = rows // groups
    start_halo = exchange(edges_of(c_points), 0)
    advanced, last, near, far = call(
        advance_kernel,
        [
            (points - 1, fields, rows, columns),
            (fields, rows, columns),
            (2, points - 1, fields, FACTOR, columns),
            (2, fields, FACTOR, columns),
        ],
        points,
        rows,
        columns,
        (c_points, start_halo),
    )
    incoming_halo = exchange(far, 1)
    incoming = lax.ppermute(last, "tm", [(i, i + 1) for i in range(groups - 1)])
    near = exchange(near, 0)
    opening = jnp.where(lax.axis_index("tm") == 0, c_points[0], incoming)
    updated = jnp.concatenate([opening[None], advanced], axis=0)
    packet = (points, fields, share, columns)
    messages = call(
        lambda p, c, *refs: residual_kernel(p, c, groups, *refs),
        [packet] * groups,
        points,
        rows,
        columns,
        (c_points, start_halo, incoming, incoming_halo, advanced, near, last),
        extra=[pltpu.VMEM((groups, *packet), jnp.float32)],
    )
    arrived = [messages[0]]
    for d in range(1, groups):
        route = [(i, target_of(i, d, groups)) for i in range(groups)]
        arrived.append(lax.ppermute(messages[d], "tm", route))
    coarse = pl.pallas_call(
        functools.partial(gather_kernel, points, groups),
        out_shape=jax.ShapeDtypeStruct((groups * points, fields, 1, share, columns), jnp.float32),
        in_specs=[VMEM] * groups,
        out_specs=pl.BlockSpec(memory_space=pl.ANY),
        scratch_shapes=[pltpu.SemaphoreType.DMA((groups,))],
    )(*arrived)
    return (updated, coarse)


def solution(mesh):
    in_specs = (P("tm", None, "space", None),)
    out_specs = (P("tm", None, "space", None), P(None, None, "space", "tm", None))
    return jax.shard_map(
        on_device, mesh=mesh, in_specs=in_specs, out_specs=out_specs, check_vma=False
    )
```

```python
import functools

import jax
import jax.numpy as jnp
from jax import lax
from jax.experimental import pallas as pl
from jax.experimental.pallas import tpu as pltpu
from jax.sharding import PartitionSpec as P

FACTOR = 8
LANES = 128
SUB = 8

MOMENTUM = 0.4
PRESSURE = 0.08


def reciprocal(x):
    r = pl.reciprocal(x, approx=True)
    return r * (2.0 - x * r)


def row_terms(read, chunks, factor, lane):
    north, south, east, west = [], [], [], []
    for c in range(chunks):
        h, p, q = read(0, c), read(1, c), read(2, c)
        r = reciprocal(h)
        u = p * r
        pressure = h * h * factor
        a = p * u + pressure
        b = q * u
        d = q * (q * r) + pressure
        east.append((h - p, p - a, q - b))
        west.append((h + p, p + a, q + b))
        north.append((h - q, p - b, q - d))
        south.append((h + q, p + b, q + d))
    level = []
    for c in range(chunks):
        after, before = (c + 1) % chunks, (c - 1) % chunks
        fields = []
        for f in range(3):
            e = jnp.where(lane == 0, east[after][f], east[c][f])
            w = jnp.where(lane == LANES - 1, west[before][f], west[c][f])
            fields.append(pltpu.roll(e, LANES - 1, 1) + pltpu.roll(w, 1, 1))
        level.append(tuple(fields))
    return north, south, level


def step(src, dst, held, depth, chunks, factor):
    lane = lax.broadcasted_iota(jnp.int32, (SUB, LANES), 1)
    cells = [(f, c) for f in range(3) for c in range(chunks)]
    partial = south_before = None
    for i in range(depth):
        north, south, level = row_terms(lambda f, c: src[f, i, c], chunks, factor, lane)
        for f, c in cells:
            if i == 0:
                held[f, c] = pltpu.roll(north[c][f], SUB - 1, 0)
            else:
                dst[f, i - 1, c] = partial[c][f] + north[c][f]
        if i == 0:
            partial = level
        else:
            partial = [
                tuple(level[c][f] + south_before[c][f] for f in range(3)) for c in range(chunks)
            ]
        south_before = south
    for f, c in cells:
        dst[f, depth - 1, c] = partial[c][f] + held[f, c]
        dst[f, 0, c] = dst[f, 0, c] + pltpu.roll(south_before[c][f], 1, 0)


def spans(chunks):
    return [slice(c * LANES, (c + 1) * LANES) for c in range(chunks)]


def fill(ext, base, chunks, pieces):
    for piece in pieces:
        rows = piece.shape[1]
        for f in range(3):
            for c, span in enumerate(spans(chunks)):
                ext[f, c, base : base + rows, :] = piece[f, :, span]
        base += rows


def propagate(scratch, base, rows, chunks):
    ext, state, held = scratch
    depth = rows // SUB
    cells = [(f, c, i) for f in range(3) for c in range(chunks) for i in range(depth)]
    for f, c, i in cells:
        value = ext.at[f, c][pl.ds(base + i, SUB, stride=depth), :]
        state[0, f, i, c] = value if f == 0 else MOMENTUM * value

    def two(_, factor):
        step(state.at[0], state.at[1], held, depth, chunks, factor)
        factor = factor * 0.25
        step(state.at[1], state.at[0], held, depth, chunks, factor)
        return factor * 0.25

    lax.fori_loop(0, FACTOR // 2, two, jnp.float32(PRESSURE))
    shrink = 0.25**FACTOR
    for f, c, i in cells:
        value = state[0, f, i, c] * (shrink if f == 0 else shrink / MOMENTUM)
        ext.at[f, c][pl.ds(base + i, SUB, stride=depth), :] = value


def take(target, ext, rows, chunks):
    for f in range(3):
        for c, span in enumerate(spans(chunks)):
            target[f, :, span] = ext[f, c, 2 * FACTOR : 2 * FACTOR + rows, :]


def own_kernel(chunks, own, halo, advanced, pushed, *scratch):
    rows, ext = own.shape[2], scratch[0]
    for k in range(advanced.shape[0]):
        fill(ext, 0, chunks, [halo.at[0, k], own.at[k], halo.at[1, k]])
        propagate(scratch, 0, rows + 4 * FACTOR, chunks)
        take(advanced.at[k], ext, rows, chunks)
        propagate(scratch, FACTOR, rows + 2 * FACTOR, chunks)
        take(pushed.at[k], ext, rows, chunks)


def edge_kernel(
    chunks, groups, own, halo, behind, behind_halo, last_halo, advanced, pushed, updated, packed, *scratch
):
    points, _, rows, _ = own.shape
    share = rows // groups
    ext = scratch[0]

    def pack(k, difference):
        for f in range(3):
            for c, span in enumerate(spans(chunks)):
                ext[f, c, 2 * FACTOR : 2 * FACTOR + rows, :] = difference(
                    ext[f, c, 2 * FACTOR : 2 * FACTOR + rows, :], f, span
                )
                for g in range(groups):
                    start = 2 * FACTOR + g * share
                    packed[g, k, f, :, span] = ext[f, c, start : start + share, :]

    fill(ext, 0, chunks, [behind_halo.at[0], behind, behind_halo.at[1]])
    propagate(scratch, 0, rows + 4 * FACTOR, chunks)

    @pl.when(lax.axis_index("tm") == 0)
    def _():
        fill(ext, 0, chunks, [halo.at[0, 0], own.at[0], halo.at[1, 0]])

    take(updated.at[0], ext, rows, chunks)
    for k in range(points - 1):
        updated[k + 1] = advanced[k]
    propagate(scratch, FACTOR, rows + 2 * FACTOR, chunks)
    pack(0, lambda value, f, span: value - advanced[0, f, :, span])
    for k in range(1, points - 1):
        pack(k, lambda _, f, span: pushed[k - 1, f, :, span] - advanced[k, f, :, span])
    fill(ext, FACTOR, chunks, [last_halo.at[0], own.at[points - 1], last_halo.at[1]])
    propagate(scratch, FACTOR, rows + 2 * FACTOR, chunks)
    pack(points - 1, lambda value, f, span: pushed[points - 2, f, :, span] - value)


VMEM = pl.BlockSpec(memory_space=pltpu.VMEM)


def call(kernel, shapes, work, rows, columns, operands):
    chunks = columns // LANES
    extended = rows + 4 * FACTOR
    cost = pl.CostEstimate(
        flops=work * extended * columns * FACTOR * 45,
        bytes_accessed=4 * work * 3 * extended * columns,
        transcendentals=work * extended * columns * FACTOR,
    )
    return pl.pallas_call(
        functools.partial(kernel, chunks),
        out_shape=[jax.ShapeDtypeStruct(shape, jnp.float32) for shape in shapes],
        in_specs=[VMEM] * len(operands),
        out_specs=[VMEM] * len(shapes),
        scratch_shapes=[
            pltpu.VMEM((3, chunks, extended, LANES), jnp.float32),
            pltpu.VMEM((2, 3, extended // SUB, chunks, SUB, LANES), jnp.float32),
            pltpu.VMEM((3, chunks, SUB, LANES), jnp.float32),
        ],
        compiler_params=pltpu.CompilerParams(vmem_limit_bytes=24 * 2**20),
        cost_estimate=cost,
    )(*operands)


def edges_of(block, width):
    return jnp.stack([block[..., -width:, :], block[..., :width, :]])


def route(shift, move):
    groups, strips = lax.axis_size("tm"), lax.axis_size("space")
    return [
        (t * strips + s, (t + shift) % groups * strips + (s + move) % strips)
        for t in range(groups)
        for s in range(strips)
    ]


def exchange(edges, shift):
    both = ("tm", "space")
    if lax.axis_size("space") == 2:
        return lax.ppermute(edges, both, route(shift, 1))
    return jnp.stack(
        [
            lax.ppermute(edges[0], both, route(shift, 1)),
            lax.ppermute(edges[1], both, route(shift, -1)),
        ]
    )


def on_device(c_points):
    points, fields, rows, columns = c_points.shape
    groups = lax.axis_size("tm")
    last = c_points[-1]
    halo = exchange(edges_of(c_points[:-1], 2 * FACTOR), 0)
    behind_halo = exchange(edges_of(last, 2 * FACTOR), 1)
    behind = lax.ppermute(last, ("tm", "space"), route(1, 0))
    last_halo = exchange(edges_of(last, FACTOR), 0)
    inner = (points - 1, fields, rows, columns)
    advanced, pushed = call(
        own_kernel, [inner, inner], 2 * (points - 1), rows, columns, (c_points, halo)
    )
    updated, packed = call(
        lambda chunks, *refs: edge_kernel(chunks, groups, *refs),
        [c_points.shape, (groups, points, fields, rows // groups, columns)],
        3,
        rows,
        columns,
        (c_points, halo, behind, behind_halo, last_halo, advanced, pushed),
    )
    coarse = lax.all_to_all(packed, "tm", split_axis=0, concat_axis=0, tiled=True)
    return (updated, coarse.reshape(groups * points, fields, 1, rows // groups, columns))


def solution(mesh):
    in_specs = (P("tm", None, "space", None),)
    out_specs = (P("tm", None, "space", None), P(None, None, "space", "tm", None))
    return jax.shard_map(
        on_device, mesh=mesh, in_specs=in_specs, out_specs=out_specs, check_vma=False
    )
```

```python
import functools

import jax
import jax.numpy as jnp
from jax import lax
from jax.experimental import pallas as pl
from jax.experimental.pallas import tpu as pltpu
from jax.sharding import PartitionSpec as P

FACTOR = 8
LANES = 128
SUB = 8

MOMENTUM = 0.4
PRESSURE = 0.08


def reciprocal(x):
    r = pl.reciprocal(x, approx=True)
    return r * (2.0 - x * r)


def row_terms(read, chunks, factor, lane):
    north, south, east, west = [], [], [], []
    for c in range(chunks):
        h, p, q = read(0, c), read(1, c), read(2, c)
        r = reciprocal(h)
        u = p * r
        pressure = h * h * factor
        a = p * u + pressure
        b = q * u
        d = q * (q * r) + pressure
        east.append((h - p, p - a, q - b))
        west.append((h + p, p + a, q + b))
        north.append((h - q, p - b, q - d))
        south.append((h + q, p + b, q + d))
    level = []
    for c in range(chunks):
        after, before = (c + 1) % chunks, (c - 1) % chunks
        fields = []
        for f in range(3):
            e = jnp.where(lane == 0, east[after][f], east[c][f])
            w = jnp.where(lane == LANES - 1, west[before][f], west[c][f])
            fields.append(pltpu.roll(e, LANES - 1, 1) + pltpu.roll(w, 1, 1))
        level.append(tuple(fields))
    return north, south, level


def step(src, dst, held, first, depth, chunks, factor):
    lane = lax.broadcasted_iota(jnp.int32, (SUB, LANES), 1)
    cells = [(f, c) for f in range(3) for c in range(chunks)]
    partial = south_before = None
    for n in range(depth):
        i, before = (first + n) % depth, (first + n - 1) % depth
        north, south, level = row_terms(lambda f, c: src[f, i, c], chunks, factor, lane)
        if i == 0:
            wrapped = [tuple(pltpu.roll(t, SUB - 1, 0) for t in terms) for terms in north]
        else:
            wrapped = north
        for f, c in cells:
            if n == 0:
                held[f, c] = wrapped[c][f]
            else:
                dst[f, before, c] = partial[c][f] + wrapped[c][f]
        partial = level
        if n > 0:
            partial = [
                tuple(level[c][f] + south_before[c][f] for f in range(3)) for c in range(chunks)
            ]
        south_before = south
        if i == depth - 1:
            south_before = [tuple(pltpu.roll(t, 1, 0) for t in terms) for terms in south]
    last = (first - 1) % depth
    for f, c in cells:
        if depth == 1:
            dst[f, 0, c] = partial[c][f] + held[f, c] + south_before[c][f]
        else:
            dst[f, last, c] = partial[c][f] + held[f, c]
            dst[f, first, c] = dst[f, first, c] + south_before[c][f]


def spans(chunks):
    return [slice(c * LANES, (c + 1) * LANES) for c in range(chunks)]


class Rows:
    def __init__(self, count, chunks):
        self.depth, self.chunks = count // SUB, chunks
        self.pitch = self.depth | 1

    def cells(self):
        return [
            (f, c, i) for f in range(3) for c in range(self.chunks) for i in range(self.depth)
        ]

    def pieces(self, start, count):
        found, at = [], 0
        while at < count:
            block, offset = divmod(start + at, self.depth)
            length = min(count - at, self.depth - offset)
            found.append((at, block * self.pitch + offset, length))
            at += length
        return found

    def fill(self, ext, arrays):
        start = 0
        for array in arrays:
            rows = array.shape[1]
            for at, place, length in self.pieces(start, rows):
                for f in range(3):
                    for c, span in enumerate(spans(self.chunks)):
                        ext[f, c, place : place + length, :] = array[f, at : at + length, span]
            start += rows

    def load(self, ext, state):
        for f, c, i in self.cells():
            value = ext.at[f, c][pl.ds(i, SUB, stride=self.pitch), :]
            state[0, f, i, c] = value if f == 0 else MOMENTUM * value

    def store(self, ext, state, steps):
        shrink = 0.25**steps
        for f, c, i in self.cells():
            value = state[0, f, i, c] * (shrink if f == 0 else shrink / MOMENTUM)
            ext.at[f, c][pl.ds(i, SUB, stride=self.pitch), :] = value

    def propagate(self, state, held, steps):
        depth = self.depth

        def two(_, factor):
            step(state.at[0], state.at[1], held, 0, depth, self.chunks, factor)
            factor = factor * 0.25
            step(state.at[1], state.at[0], held, 1 % depth, depth, self.chunks, factor)
            return factor * 0.25

        lax.fori_loop(0, FACTOR // 2, two, jnp.float32(PRESSURE * 0.25**steps))

    def take(self, ext, start, count, use):
        for at, place, length in self.pieces(start, count):
            for f in range(3):
                for c, span in enumerate(spans(self.chunks)):
                    use(f, span, at, length, ext[f, c, place : place + length, :])


def put(target):
    def use(f, span, at, length, value):
        target[f, at : at + length, span] = value

    return use


def own_kernel(chunks, own, halo, advanced, pushed, ext, state, held):
    rows = own.shape[2]
    wide = Rows(rows + 4 * FACTOR, chunks)
    for k in range(advanced.shape[0]):
        wide.fill(ext, [halo.at[0, k], own.at[k], halo.at[1, k]])
        wide.load(ext, state)
        wide.propagate(state, held, 0)
        wide.store(ext, state, FACTOR)
        wide.take(ext, 2 * FACTOR, rows, put(advanced.at[k]))
        wide.propagate(state, held, FACTOR)
        wide.store(ext, state, 2 * FACTOR)
        wide.take(ext, 2 * FACTOR, rows, put(pushed.at[k]))


def last_kernel(chunks, own, halo, advanced, pushed, residual, ext, state, held):
    points, _, rows, _ = own.shape
    narrow = Rows(rows + 2 * FACTOR, chunks)
    narrow.fill(ext, [halo.at[0], own.at[points - 1], halo.at[1]])
    narrow.load(ext, state)
    narrow.propagate(state, held, 0)
    narrow.store(ext, state, FACTOR)

    def use(f, span, at, length, value):
        part = slice(at, at + length)
        residual[points - 2, f, part, span] = pushed[points - 2, f, part, span] - value

    narrow.take(ext, FACTOR, rows, use)
    for k in range(points - 2):
        residual[k] = pushed[k] - advanced[k + 1]


def first_kernel(
    chunks, groups, own, halo, behind, behind_halo, advanced, residual,
    updated, packed, ext, state, held, first, sems,
):
    points, _, rows, _ = own.shape
    share = rows // groups
    wide = Rows(rows + 4 * FACTOR, chunks)
    copies = [
        pltpu.make_async_copy(advanced, updated.at[pl.ds(1, points - 1)], sems.at[0]),
        pltpu.make_async_copy(first, updated.at[0], sems.at[1]),
    ]
    copies[0].start()
    wide.fill(ext, [behind_halo.at[0], behind, behind_halo.at[1]])
    wide.load(ext, state)
    wide.propagate(state, held, 0)
    wide.store(ext, state, FACTOR)
    wide.take(ext, 2 * FACTOR, rows, put(first))
    shrink = 0.25**FACTOR

    @pl.when(lax.axis_index("tm") == 0)
    def _():
        wide.fill(ext, [halo.at[0, 0], own.at[0], halo.at[1, 0]])
        wide.load(ext, state)
        for f, c, i in wide.cells():
            state[0, f, i, c] = state[0, f, i, c] * (1 / shrink)
        first[...] = own[0]

    copies[1].start()
    wide.propagate(state, held, FACTOR)
    wide.store(ext, state, 2 * FACTOR)
    for at, place, length in wide.pieces(2 * FACTOR, rows):
        for f in range(3):
            for c, span in enumerate(spans(chunks)):
                part = slice(place, place + length)
                ext[f, c, part, :] = ext[f, c, part, :] - advanced[0, f, at : at + length, span]
    for g in range(groups):
        for f in range(3):
            for c, span in enumerate(spans(chunks)):
                for at, place, length in wide.pieces(2 * FACTOR + g * share, share):
                    packed[g * points, f, 0, at : at + length, span] = ext[
                        f, c, place : place + length, :
                    ]
                for k in range(1, points):
                    packed[g * points + k, f, 0, :, span] = residual[
                        k - 1, f, g * share : (g + 1) * share, span
                    ]
    for copy in copies:
        copy.wait()


VMEM = pl.BlockSpec(memory_space=pltpu.VMEM)


def call(kernel, shapes, work, rows, columns, operands, out_specs=None, extra=()):
    chunks = columns // LANES
    extended = rows + 4 * FACTOR
    cost = pl.CostEstimate(
        flops=work * extended * columns * FACTOR * 45,
        bytes_accessed=4 * work * 3 * extended * columns,
        transcendentals=work * extended * columns * FACTOR,
    )
    return pl.pallas_call(
        functools.partial(kernel, chunks),
        out_shape=[jax.ShapeDtypeStruct(shape, jnp.float32) for shape in shapes],
        in_specs=[VMEM] * len(operands),
        out_specs=out_specs or [VMEM] * len(shapes),
        scratch_shapes=[
            pltpu.VMEM((3, chunks, extended + SUB, LANES), jnp.float32),
            pltpu.VMEM((2, 3, extended // SUB, chunks, SUB, LANES), jnp.float32),
            pltpu.VMEM((3, chunks, SUB, LANES), jnp.float32),
            *extra,
        ],
        compiler_params=pltpu.CompilerParams(vmem_limit_bytes=24 * 2**20),
        cost_estimate=cost,
    )(*operands)


def edges_of(block, width):
    return jnp.stack([block[..., -width:, :], block[..., :width, :]])


def route(shift, move):
    groups, strips = lax.axis_size("tm"), lax.axis_size("space")
    return [
        (t * strips + s, (t + shift) % groups * strips + (s + move) % strips)
        for t in range(groups)
        for s in range(strips)
    ]


def exchange(edges, shift):
    both = ("tm", "space")
    if lax.axis_size("space") == 2:
        return lax.ppermute(edges, both, route(shift, 1))
    return jnp.stack(
        [
            lax.ppermute(edges[0], both, route(shift, 1)),
            lax.ppermute(edges[1], both, route(shift, -1)),
        ]
    )


def on_device(c_points):
    points, fields, rows, columns = c_points.shape
    groups = lax.axis_size("tm")
    last = c_points[-1]
    halo = exchange(edges_of(c_points[:-1], 2 * FACTOR), 0)
    last_halo = exchange(edges_of(last, FACTOR), 0)
    behind_halo = exchange(edges_of(last, 2 * FACTOR), 1)
    behind = lax.ppermute(last, ("tm", "space"), route(1, 0))
    inner = (points - 1, fields, rows, columns)
    advanced, pushed = call(
        own_kernel, [inner, inner], 2 * (points - 1), rows, columns, (c_points, halo)
    )
    (residual,) = call(
        last_kernel, [inner], 1, rows, columns, (c_points, last_halo, advanced, pushed)
    )
    updated, packed = call(
        lambda chunks, *refs: first_kernel(chunks, groups, *refs),
        [c_points.shape, (groups * points, fields, 1, rows // groups, columns)],
        2,
        rows,
        columns,
        (c_points, halo, behind, behind_halo, advanced, residual),
        out_specs=[pl.BlockSpec(memory_space=pl.ANY), VMEM],
        extra=[pltpu.VMEM((fields, rows, columns), jnp.float32), pltpu.SemaphoreType.DMA((2,))],
    )
    return (updated, lax.all_to_all(packed, "tm", split_axis=0, concat_axis=0, tiled=True))


def solution(mesh):
    in_specs = (P("tm", None, "space", None),)
    out_specs = (P("tm", None, "space", None), P(None, None, "space", "tm", None))
    return jax.shard_map(
        on_device, mesh=mesh, in_specs=in_specs, out_specs=out_specs, check_vma=False
    )
```

```python
import functools

import jax
import jax.numpy as jnp
from jax import lax
from jax.experimental import pallas as pl
from jax.experimental.pallas import tpu as pltpu
from jax.sharding import PartitionSpec as P

FACTOR = 8
LANES = 128
SUB = 8

MOMENTUM = 0.4
PRESSURE = 0.08


def reciprocal(x):
    r = pl.reciprocal(x, approx=True)
    return r * (2.0 - x * r)


def row_terms(read, chunks, factor, lane):
    north, south, east, west = [], [], [], []
    for c in range(chunks):
        h, p, q = read(0, c), read(1, c), read(2, c)
        r = reciprocal(h)
        u = p * r
        pressure = h * h * factor
        a = p * u + pressure
        b = q * u
        d = q * (q * r) + pressure
        east.append((h - p, p - a, q - b))
        west.append((h + p, p + a, q + b))
        north.append((h - q, p - b, q - d))
        south.append((h + q, p + b, q + d))
    level = []
    for c in range(chunks):
        after, before = (c + 1) % chunks, (c - 1) % chunks
        fields = []
        for f in range(3):
            e = jnp.where(lane == 0, east[after][f], east[c][f])
            w = jnp.where(lane == LANES - 1, west[before][f], west[c][f])
            fields.append(pltpu.roll(e, LANES - 1, 1) + pltpu.roll(w, 1, 1))
        level.append(tuple(fields))
    return north, south, level


def step(src, dst, held, first, depth, chunks, factor):
    lane = lax.broadcasted_iota(jnp.int32, (SUB, LANES), 1)
    cells = [(f, c) for f in range(3) for c in range(chunks)]
    partial = south_before = None
    for n in range(depth):
        i, before = (first + n) % depth, (first + n - 1) % depth
        north, south, level = row_terms(lambda f, c: src[f, i, c], chunks, factor, lane)
        if i == 0:
            wrapped = [tuple(pltpu.roll(t, SUB - 1, 0) for t in terms) for terms in north]
        else:
            wrapped = north
        for f, c in cells:
            if n == 0:
                held[f, c] = wrapped[c][f]
            else:
                dst[f, before, c] = partial[c][f] + wrapped[c][f]
        partial = level
        if n > 0:
            partial = [
                tuple(level[c][f] + south_before[c][f] for f in range(3)) for c in range(chunks)
            ]
        south_before = south
        if i == depth - 1:
            south_before = [tuple(pltpu.roll(t, 1, 0) for t in terms) for terms in south]
    last = (first - 1) % depth
    for f, c in cells:
        if depth == 1:
            dst[f, 0, c] = partial[c][f] + held[f, c] + south_before[c][f]
        else:
            dst[f, last, c] = partial[c][f] + held[f, c]
            dst[f, first, c] = dst[f, first, c] + south_before[c][f]


def spans(chunks):
    return [slice(c * LANES, (c + 1) * LANES) for c in range(chunks)]


class Rows:
    def __init__(self, count, chunks):
        self.depth, self.chunks = count // SUB, chunks
        self.pitch = self.depth | 1

    def cells(self):
        return [
            (f, c, i) for f in range(3) for c in range(self.chunks) for i in range(self.depth)
        ]

    def pieces(self, start, count):
        found, at = [], 0
        while at < count:
            block, offset = divmod(start + at, self.depth)
            length = min(count - at, self.depth - offset)
            found.append((at, block * self.pitch + offset, length))
            at += length
        return found

    def fill(self, ext, arrays):
        start = 0
        for array in arrays:
            rows = array.shape[1]
            for at, place, length in self.pieces(start, rows):
                for f in range(3):
                    for c, span in enumerate(spans(self.chunks)):
                        ext[f, c, place : place + length, :] = array[f, at : at + length, span]
            start += rows

    def load(self, ext, state):
        for f, c, i in self.cells():
            value = ext.at[f, c][pl.ds(i, SUB, stride=self.pitch), :]
            state[0, f, i, c] = value if f == 0 else MOMENTUM * value

    def store(self, ext, state, steps):
        shrink = 0.25**steps
        for f, c, i in self.cells():
            value = state[0, f, i, c] * (shrink if f == 0 else shrink / MOMENTUM)
            ext.at[f, c][pl.ds(i, SUB, stride=self.pitch), :] = value

    def propagate(self, state, held, steps):
        depth = self.depth

        def two(_, factor):
            step(state.at[0], state.at[1], held, 0, depth, self.chunks, factor)
            factor = factor * 0.25
            step(state.at[1], state.at[0], held, 1 % depth, depth, self.chunks, factor)
            return factor * 0.25

        lax.fori_loop(0, FACTOR // 2, two, jnp.float32(PRESSURE * 0.25**steps))

    def take(self, ext, start, count, use):
        for at, place, length in self.pieces(start, count):
            for f in range(3):
                for c, span in enumerate(spans(self.chunks)):
                    use(f, span, at, length, ext[f, c, place : place + length, :])


def put(target):
    def use(f, span, at, length, value):
        target[f, at : at + length, span] = value

    return use


def own_kernel(chunks, own, halo, advanced, pushed, ext, state, held):
    rows = own.shape[2]
    wide = Rows(rows + 4 * FACTOR, chunks)
    for k in range(advanced.shape[0]):
        wide.fill(ext, [halo.at[0, k], own.at[k], halo.at[1, k]])
        wide.load(ext, state)
        wide.propagate(state, held, 0)
        wide.store(ext, state, FACTOR)
        wide.take(ext, 2 * FACTOR, rows, put(advanced.at[k]))
        wide.propagate(state, held, FACTOR)
        wide.store(ext, state, 2 * FACTOR)
        wide.take(ext, 2 * FACTOR, rows, put(pushed.at[k]))


def last_kernel(chunks, own, halo, advanced, pushed, residual, ext, state, held):
    points, _, rows, _ = own.shape
    narrow = Rows(rows + 2 * FACTOR, chunks)
    narrow.fill(ext, [halo.at[0], own.at[points - 1], halo.at[1]])
    narrow.load(ext, state)
    narrow.propagate(state, held, 0)
    narrow.store(ext, state, FACTOR)

    def use(f, span, at, length, value):
        part = slice(at, at + length)
        residual[points - 2, f, part, span] = pushed[points - 2, f, part, span] - value

    narrow.take(ext, FACTOR, rows, use)
    for k in range(points - 2):
        residual[k] = pushed[k] - advanced[k + 1]


def first_kernel(
    chunks, groups, own, halo, behind, behind_halo, advanced, residual,
    updated, packed, ext, state, held, first, sems,
):
    points, _, rows, _ = own.shape
    share = rows // groups
    wide = Rows(rows + 4 * FACTOR, chunks)
    copies = [
        pltpu.make_async_copy(advanced, updated.at[pl.ds(1, points - 1)], sems.at[0]),
        pltpu.make_async_copy(first, updated.at[0], sems.at[1]),
    ]
    copies[0].start()
    wide.fill(ext, [behind_halo.at[0], behind, behind_halo.at[1]])
    wide.load(ext, state)
    wide.propagate(state, held, 0)
    wide.store(ext, state, FACTOR)
    wide.take(ext, 2 * FACTOR, rows, put(first))
    shrink = 0.25**FACTOR

    @pl.when(lax.axis_index("tm") == 0)
    def _():
        wide.fill(ext, [halo.at[0, 0], own.at[0], halo.at[1, 0]])
        wide.load(ext, state)
        for f, c, i in wide.cells():
            state[0, f, i, c] = state[0, f, i, c] * (1 / shrink)
        first[...] = own[0]

    copies[1].start()
    wide.propagate(state, held, FACTOR)
    wide.store(ext, state, 2 * FACTOR)
    for at, place, length in wide.pieces(2 * FACTOR, rows):
        for f in range(3):
            for c, span in enumerate(spans(chunks)):
                part = slice(place, place + length)
                ext[f, c, part, :] = ext[f, c, part, :] - advanced[0, f, at : at + length, span]
    for g in range(groups):
        for f in range(3):
            for c, span in enumerate(spans(chunks)):
                for at, place, length in wide.pieces(2 * FACTOR + g * share, share):
                    packed[g * points, f, 0, at : at + length, span] = ext[
                        f, c, place : place + length, :
                    ]
                for k in range(1, points):
                    packed[g * points + k, f, 0, :, span] = residual[
                        k - 1, f, g * share : (g + 1) * share, span
                    ]
    for copy in copies:
        copy.wait()


VMEM = pl.BlockSpec(memory_space=pltpu.VMEM)


def call(kernel, shapes, work, rows, columns, operands, out_specs=None, extra=()):
    chunks = columns // LANES
    extended = rows + 4 * FACTOR
    cost = pl.CostEstimate(
        flops=work * extended * columns * FACTOR * 45,
        bytes_accessed=4 * work * 3 * extended * columns,
        transcendentals=work * extended * columns * FACTOR,
    )
    return pl.pallas_call(
        functools.partial(kernel, chunks),
        out_shape=[jax.ShapeDtypeStruct(shape, jnp.float32) for shape in shapes],
        in_specs=[VMEM] * len(operands),
        out_specs=out_specs or [VMEM] * len(shapes),
        scratch_shapes=[
            pltpu.VMEM((3, chunks, extended + SUB, LANES), jnp.float32),
            pltpu.VMEM((2, 3, extended // SUB, chunks, SUB, LANES), jnp.float32),
            pltpu.VMEM((3, chunks, SUB, LANES), jnp.float32),
            *extra,
        ],
        compiler_params=pltpu.CompilerParams(vmem_limit_bytes=24 * 2**20),
        cost_estimate=cost,
    )(*operands)


def edges_of(block, width):
    return jnp.stack([block[..., -width:, :], block[..., :width, :]])


def route(shift, move):
    groups, strips = lax.axis_size("tm"), lax.axis_size("space")
    return [
        (t * strips + s, (t + shift) % groups * strips + (s + move) % strips)
        for t in range(groups)
        for s in range(strips)
    ]


def exchange(edges, shift):
    both = ("tm", "space")
    if lax.axis_size("space") == 2:
        return lax.ppermute(edges, both, route(shift, 1))
    return jnp.stack(
        [
            lax.ppermute(edges[0], both, route(shift, 1)),
            lax.ppermute(edges[1], both, route(shift, -1)),
        ]
    )


def on_device(c_points):
    points, fields, rows, columns = c_points.shape
    groups = lax.axis_size("tm")
    last = c_points[-1]
    halo = exchange(edges_of(c_points[:-1], 2 * FACTOR), 0)
    last_halo = exchange(edges_of(last, FACTOR), 0)
    halo, last_edges = lax.optimization_barrier((halo, edges_of(last, 2 * FACTOR)))
    behind_halo = exchange(last_edges, 1)
    behind = lax.ppermute(last, ("tm", "space"), route(1, 0))
    inner = (points - 1, fields, rows, columns)
    advanced, pushed = call(
        own_kernel, [inner, inner], 2 * (points - 1), rows, columns, (c_points, halo)
    )
    (residual,) = call(
        last_kernel, [inner], 1, rows, columns, (c_points, last_halo, advanced, pushed)
    )
    updated, packed = call(
        lambda chunks, *refs: first_kernel(chunks, groups, *refs),
        [c_points.shape, (groups * points, fields, 1, rows // groups, columns)],
        2,
        rows,
        columns,
        (c_points, halo, behind, behind_halo, advanced, residual),
        out_specs=[pl.BlockSpec(memory_space=pl.ANY), VMEM],
        extra=[pltpu.VMEM((fields, rows, columns), jnp.float32), pltpu.SemaphoreType.DMA((2,))],
    )
    return (updated, lax.all_to_all(packed, "tm", split_axis=0, concat_axis=0, tiled=True))


def solution(mesh):
    in_specs = (P("tm", None, "space", None),)
    out_specs = (P("tm", None, "space", None), P(None, None, "space", "tm", None))
    return jax.shard_map(
        on_device, mesh=mesh, in_specs=in_specs, out_specs=out_specs, check_vma=False
    )
```

```python
import functools

import jax
import jax.numpy as jnp
from jax import lax
from jax.experimental import pallas as pl
from jax.experimental.pallas import tpu as pltpu
from jax.sharding import PartitionSpec as P

FACTOR = 8
LANES = 128
SUB = 8

MOMENTUM = 0.4
PRESSURE = 0.08


def reciprocal(x):
    r = pl.reciprocal(x, approx=True)
    return r * (2.0 - x * r)


def row_terms(read, chunks, factor, lane):
    north, south, east, west = [], [], [], []
    for c in range(chunks):
        h, p, q = read(0, c), read(1, c), read(2, c)
        r = reciprocal(h)
        u = p * r
        pressure = h * h * factor
        a = p * u + pressure
        b = q * u
        d = q * (q * r) + pressure
        east.append((h - p, p - a, q - b))
        west.append((h + p, p + a, q + b))
        north.append((h - q, p - b, q - d))
        south.append((h + q, p + b, q + d))
    level = []
    for c in range(chunks):
        after, before = (c + 1) % chunks, (c - 1) % chunks
        fields = []
        for f in range(3):
            e = jnp.where(lane == 0, east[after][f], east[c][f])
            w = jnp.where(lane == LANES - 1, west[before][f], west[c][f])
            fields.append(pltpu.roll(e, LANES - 1, 1) + pltpu.roll(w, 1, 1))
        level.append(tuple(fields))
    return north, south, level


def step(src, dst, held, first, depth, chunks, factor):
    lane = lax.broadcasted_iota(jnp.int32, (SUB, LANES), 1)
    cells = [(f, c) for f in range(3) for c in range(chunks)]
    partial = south_before = None
    for n in range(depth):
        i, before = (first + n) % depth, (first + n - 1) % depth
        north, south, level = row_terms(lambda f, c: src[f, i, c], chunks, factor, lane)
        if i == 0:
            wrapped = [tuple(pltpu.roll(t, SUB - 1, 0) for t in terms) for terms in north]
        else:
            wrapped = north
        for f, c in cells:
            if n == 0:
                held[f, c] = wrapped[c][f]
            else:
                dst[f, before, c] = partial[c][f] + wrapped[c][f]
        partial = level
        if n > 0:
            partial = [
                tuple(level[c][f] + south_before[c][f] for f in range(3)) for c in range(chunks)
            ]
        south_before = south
        if i == depth - 1:
            south_before = [tuple(pltpu.roll(t, 1, 0) for t in terms) for terms in south]
    last = (first - 1) % depth
    for f, c in cells:
        if depth == 1:
            dst[f, 0, c] = partial[c][f] + held[f, c] + south_before[c][f]
        else:
            dst[f, last, c] = partial[c][f] + held[f, c]
            dst[f, first, c] = dst[f, first, c] + south_before[c][f]


def spans(chunks):
    return [slice(c * LANES, (c + 1) * LANES) for c in range(chunks)]


class Rows:
    def __init__(self, count, chunks):
        self.depth, self.chunks = count // SUB, chunks
        self.pitch = self.depth | 1

    def cells(self):
        return [
            (f, c, i) for f in range(3) for c in range(self.chunks) for i in range(self.depth)
        ]

    def pieces(self, start, count):
        found, at = [], 0
        while at < count:
            block, offset = divmod(start + at, self.depth)
            length = min(count - at, self.depth - offset)
            found.append((at, block * self.pitch + offset, length))
            at += length
        return found

    def fill(self, ext, arrays):
        start = 0
        for array in arrays:
            rows = array.shape[1]
            for at, place, length in self.pieces(start, rows):
                for f in range(3):
                    for c, span in enumerate(spans(self.chunks)):
                        ext[f, c, place : place + length, :] = array[f, at : at + length, span]
            start += rows

    def load(self, ext, state):
        for f, c, i in self.cells():
            value = ext.at[f, c][pl.ds(i, SUB, stride=self.pitch), :]
            state[0, f, i, c] = value if f == 0 else MOMENTUM * value

    def store(self, ext, state, steps):
        shrink = 0.25**steps
        for f, c, i in self.cells():
            value = state[0, f, i, c] * (shrink if f == 0 else shrink / MOMENTUM)
            ext.at[f, c][pl.ds(i, SUB, stride=self.pitch), :] = value

    def propagate(self, state, held, steps):
        depth = self.depth

        def two(_, factor):
            step(state.at[0], state.at[1], held, 0, depth, self.chunks, factor)
            factor = factor * 0.25
            step(state.at[1], state.at[0], held, 1 % depth, depth, self.chunks, factor)
            return factor * 0.25

        lax.fori_loop(0, FACTOR // 2, two, jnp.float32(PRESSURE * 0.25**steps))

    def take(self, ext, start, count, use):
        for at, place, length in self.pieces(start, count):
            for f in range(3):
                for c, span in enumerate(spans(self.chunks)):
                    use(f, span, at, length, ext[f, c, place : place + length, :])


def put(target):
    def use(f, span, at, length, value):
        target[f, at : at + length, span] = value

    return use


def pack(ext, layout, start, rows, groups, packed, k):
    share = rows // groups
    for g in range(groups):
        for at, place, length in layout.pieces(start + g * share, share):
            for f in range(3):
                for c, span in enumerate(spans(layout.chunks)):
                    packed[g, k, f, 0, at : at + length, span] = ext[f, c, place : place + length, :]


def subtract(ext, layout, start, rows, difference):
    for at, place, length in layout.pieces(start, rows):
        for f in range(3):
            for c, span in enumerate(spans(layout.chunks)):
                part = slice(place, place + length)
                ext[f, c, part, :] = difference(ext[f, c, part, :], f, slice(at, at + length), span)


def last_kernel(chunks, own, halo, advanced, ext, state, held):
    points, _, rows, _ = own.shape
    narrow = Rows(rows + 2 * FACTOR, chunks)
    narrow.fill(ext, [halo.at[0], own.at[points - 1], halo.at[1]])
    narrow.load(ext, state)
    narrow.propagate(state, held, 0)
    narrow.store(ext, state, FACTOR)
    narrow.take(ext, FACTOR, rows, put(advanced))


def own_kernel(chunks, groups, own, halo, last, advanced, packed, ext, state, held):
    rows = own.shape[2]
    wide = Rows(rows + 4 * FACTOR, chunks)
    following = last
    for k in reversed(range(advanced.shape[0])):
        wide.fill(ext, [halo.at[0, k], own.at[k], halo.at[1, k]])
        wide.load(ext, state)
        wide.propagate(state, held, 0)
        wide.store(ext, state, FACTOR)
        wide.take(ext, 2 * FACTOR, rows, put(advanced.at[k]))
        wide.propagate(state, held, FACTOR)
        wide.store(ext, state, 2 * FACTOR)
        subtract(
            ext, wide, 2 * FACTOR, rows, lambda v, f, part, span: v - following[f, part, span]
        )
        pack(ext, wide, 2 * FACTOR, rows, groups, packed, k)
        following = advanced.at[k]


def first_kernel(
    chunks, groups, own, halo, behind, behind_halo, advanced,
    updated, packed, ext, state, held, first, sems,
):
    points, _, rows, _ = own.shape
    wide = Rows(rows + 4 * FACTOR, chunks)
    copies = [
        pltpu.make_async_copy(advanced, updated.at[pl.ds(1, points - 1)], sems.at[0]),
        pltpu.make_async_copy(first, updated.at[0], sems.at[1]),
    ]
    copies[0].start()
    wide.fill(ext, [behind_halo.at[0], behind, behind_halo.at[1]])
    wide.load(ext, state)
    wide.propagate(state, held, 0)
    wide.store(ext, state, FACTOR)
    wide.take(ext, 2 * FACTOR, rows, put(first))
    shrink = 0.25**FACTOR

    @pl.when(lax.axis_index("tm") == 0)
    def _():
        wide.fill(ext, [halo.at[0, 0], own.at[0], halo.at[1, 0]])
        wide.load(ext, state)
        for f, c, i in wide.cells():
            state[0, f, i, c] = state[0, f, i, c] * (1 / shrink)
        first[...] = own[0]

    copies[1].start()
    wide.propagate(state, held, FACTOR)
    wide.store(ext, state, 2 * FACTOR)
    subtract(ext, wide, 2 * FACTOR, rows, lambda v, f, part, span: v - advanced[0, f, part, span])
    pack(ext, wide, 2 * FACTOR, rows, groups, packed, 0)
    for copy in copies:
        copy.wait()


def join_kernel(opening, others, out, sems):
    inner = others.shape[1]
    copies = [
        pltpu.make_async_copy(others, out.at[:, pl.ds(1, inner)], sems.at[0]),
        pltpu.make_async_copy(opening, out.at[:, pl.ds(0, 1)], sems.at[1]),
    ]
    for copy in copies:
        copy.start()
    for copy in copies:
        copy.wait()


VMEM = pl.BlockSpec(memory_space=pltpu.VMEM)


def call(kernel, shapes, work, rows, columns, operands, out_specs=None, extra=()):
    chunks = columns // LANES
    extended = rows + 4 * FACTOR
    cost = pl.CostEstimate(
        flops=work * extended * columns * FACTOR * 45,
        bytes_accessed=4 * work * 3 * extended * columns,
        transcendentals=work * extended * columns * FACTOR,
    )
    return pl.pallas_call(
        functools.partial(kernel, chunks),
        out_shape=[jax.ShapeDtypeStruct(shape, jnp.float32) for shape in shapes],
        in_specs=[VMEM] * len(operands),
        out_specs=out_specs or [VMEM] * len(shapes),
        scratch_shapes=[
            pltpu.VMEM((3, chunks, extended + SUB, LANES), jnp.float32),
            pltpu.VMEM((2, 3, extended // SUB, chunks, SUB, LANES), jnp.float32),
            pltpu.VMEM((3, chunks, SUB, LANES), jnp.float32),
            *extra,
        ],
        compiler_params=pltpu.CompilerParams(vmem_limit_bytes=24 * 2**20),
        cost_estimate=cost,
    )(*operands)


def edges_of(block, width):
    return jnp.stack([block[..., -width:, :], block[..., :width, :]])


def route(shift, move):
    groups, strips = lax.axis_size("tm"), lax.axis_size("space")
    return [
        (t * strips + s, (t + shift) % groups * strips + (s + move) % strips)
        for t in range(groups)
        for s in range(strips)
    ]


def exchange(edges, shift):
    both = ("tm", "space")
    if lax.axis_size("space") == 2:
        return lax.ppermute(edges, both, route(shift, 1))
    return jnp.stack(
        [
            lax.ppermute(edges[0], both, route(shift, 1)),
            lax.ppermute(edges[1], both, route(shift, -1)),
        ]
    )


def on_device(c_points):
    points, fields, rows, columns = c_points.shape
    groups = lax.axis_size("tm")
    last = c_points[-1]
    last_halo = exchange(edges_of(last, FACTOR), 0)
    halo = exchange(edges_of(c_points[:-1], 2 * FACTOR), 0)
    halo, last_edges, last = lax.optimization_barrier((halo, edges_of(last, 2 * FACTOR), last))
    behind_halo = exchange(last_edges, 1)
    behind = lax.ppermute(last, ("tm", "space"), route(1, 0))
    inner = (points - 1, fields, rows, columns)
    packet = (fields, 1, rows // groups, columns)
    (advanced_last,) = call(
        last_kernel, [last.shape], 1, rows, columns, (c_points, last_halo)
    )
    advanced, packed = call(
        lambda chunks, *refs: own_kernel(chunks, groups, *refs),
        [inner, (groups, points - 1, *packet)],
        2 * (points - 1),
        rows,
        columns,
        (c_points, halo, advanced_last),
    )
    others = lax.all_to_all(packed, "tm", split_axis=0, concat_axis=0, tiled=True)
    updated, packed = call(
        lambda chunks, *refs: first_kernel(chunks, groups, *refs),
        [c_points.shape, (groups, 1, *packet)],
        2,
        rows,
        columns,
        (c_points, halo, behind, behind_halo, advanced),
        out_specs=[pl.BlockSpec(memory_space=pl.ANY), VMEM],
        extra=[pltpu.VMEM((fields, rows, columns), jnp.float32), pltpu.SemaphoreType.DMA((2,))],
    )
    opening = lax.all_to_all(packed, "tm", split_axis=0, concat_axis=0, tiled=True)
    coarse = pl.pallas_call(
        join_kernel,
        out_shape=jax.ShapeDtypeStruct((groups, points, *packet), jnp.float32),
        in_specs=[VMEM] * 2,
        out_specs=pl.BlockSpec(memory_space=pl.ANY),
        scratch_shapes=[pltpu.SemaphoreType.DMA((2,))],
    )(opening, others)
    return (updated, coarse.reshape(groups * points, *packet))


def solution(mesh):
    in_specs = (P("tm", None, "space", None),)
    out_specs = (P("tm", None, "space", None), P(None, None, "space", "tm", None))
    return jax.shard_map(
        on_device, mesh=mesh, in_specs=in_specs, out_specs=out_specs, check_vma=False
    )
```

```python
import functools

import jax
import jax.numpy as jnp
from jax import lax
from jax.experimental import pallas as pl
from jax.experimental.pallas import tpu as pltpu
from jax.sharding import PartitionSpec as P

FACTOR = 8
LANES = 128
SUB = 8

MOMENTUM = 0.4
PRESSURE = 0.08


def reciprocal(x):
    r = pl.reciprocal(x, approx=True)
    return r * (2.0 - x * r)


def row_terms(read, chunks, factor, lane):
    north, south, east, west = [], [], [], []
    for c in range(chunks):
        h, p, q = read(0, c), read(1, c), read(2, c)
        r = reciprocal(h)
        u = p * r
        pressure = h * h * factor
        a = p * u + pressure
        b = q * u
        d = q * (q * r) + pressure
        east.append((h - p, p - a, q - b))
        west.append((h + p, p + a, q + b))
        north.append((h - q, p - b, q - d))
        south.append((h + q, p + b, q + d))
    level = []
    for c in range(chunks):
        after, before = (c + 1) % chunks, (c - 1) % chunks
        fields = []
        for f in range(3):
            e = jnp.where(lane == 0, east[after][f], east[c][f])
            w = jnp.where(lane == LANES - 1, west[before][f], west[c][f])
            fields.append(pltpu.roll(e, LANES - 1, 1) + pltpu.roll(w, 1, 1))
        level.append(tuple(fields))
    return north, south, level


def step(src, dst, held, first, depth, chunks, factor):
    lane = lax.broadcasted_iota(jnp.int32, (SUB, LANES), 1)
    cells = [(f, c) for f in range(3) for c in range(chunks)]
    partial = south_before = None
    for n in range(depth):
        i, before = (first + n) % depth, (first + n - 1) % depth
        north, south, level = row_terms(lambda f, c: src[f, i, c], chunks, factor, lane)
        if i == 0:
            wrapped = [tuple(pltpu.roll(t, SUB - 1, 0) for t in terms) for terms in north]
        else:
            wrapped = north
        for f, c in cells:
            if n == 0:
                held[f, c] = wrapped[c][f]
            else:
                dst[f, before, c] = partial[c][f] + wrapped[c][f]
        partial = level
        if n > 0:
            partial = [
                tuple(level[c][f] + south_before[c][f] for f in range(3)) for c in range(chunks)
            ]
        south_before = south
        if i == depth - 1:
            south_before = [tuple(pltpu.roll(t, 1, 0) for t in terms) for terms in south]
    last = (first - 1) % depth
    for f, c in cells:
        if depth == 1:
            dst[f, 0, c] = partial[c][f] + held[f, c] + south_before[c][f]
        else:
            dst[f, last, c] = partial[c][f] + held[f, c]
            dst[f, first, c] = dst[f, first, c] + south_before[c][f]


def spans(chunks):
    return [slice(c * LANES, (c + 1) * LANES) for c in range(chunks)]


class Rows:
    def __init__(self, count, chunks):
        self.depth, self.chunks = count // SUB, chunks
        self.pitch = self.depth | 1

    def cells(self):
        return [
            (f, c, i) for f in range(3) for c in range(self.chunks) for i in range(self.depth)
        ]

    def pieces(self, start, count):
        found, at = [], 0
        while at < count:
            block, offset = divmod(start + at, self.depth)
            length = min(count - at, self.depth - offset)
            found.append((at, block * self.pitch + offset, length))
            at += length
        return found

    def fill(self, ext, arrays):
        start = 0
        for array in arrays:
            rows = array.shape[1]
            for at, place, length in self.pieces(start, rows):
                for f in range(3):
                    for c, span in enumerate(spans(self.chunks)):
                        ext[f, c, place : place + length, :] = array[f, at : at + length, span]
            start += rows

    def load(self, ext, state):
        for f, c, i in self.cells():
            value = ext.at[f, c][pl.ds(i, SUB, stride=self.pitch), :]
            state[0, f, i, c] = value if f == 0 else MOMENTUM * value

    def store(self, ext, state, steps):
        shrink = 0.25**steps
        for f, c, i in self.cells():
            value = state[0, f, i, c] * (shrink if f == 0 else shrink / MOMENTUM)
            ext.at[f, c][pl.ds(i, SUB, stride=self.pitch), :] = value

    def propagate(self, state, held, steps):
        depth = self.depth

        def two(_, factor):
            step(state.at[0], state.at[1], held, 0, depth, self.chunks, factor)
            factor = factor * 0.25
            step(state.at[1], state.at[0], held, 1 % depth, depth, self.chunks, factor)
            return factor * 0.25

        lax.fori_loop(0, FACTOR // 2, two, jnp.float32(PRESSURE * 0.25**steps))

    def take(self, ext, start, count, use):
        for at, place, length in self.pieces(start, count):
            for f in range(3):
                for c, span in enumerate(spans(self.chunks)):
                    use(f, span, at, length, ext[f, c, place : place + length, :])


def put(target):
    def use(f, span, at, length, value):
        target[f, at : at + length, span] = value

    return use


def chain_kernel(chunks, point, own, halo, advanced, pushed, ext, state, held):
    rows = own.shape[2]
    wide = Rows(rows + 4 * FACTOR, chunks)
    wide.fill(ext, [halo.at[0], own.at[point], halo.at[1]])
    wide.load(ext, state)
    wide.propagate(state, held, 0)
    wide.store(ext, state, FACTOR)
    wide.take(ext, 2 * FACTOR, rows, put(advanced))
    wide.propagate(state, held, FACTOR)
    wide.store(ext, state, 2 * FACTOR)
    wide.take(ext, 2 * FACTOR, rows, put(pushed))


def pack_kernel(points, groups, pair, *refs):
    following, pushed, outs = refs[:points], refs[points : 2 * points], refs[2 * points : -1]
    difference = refs[-1]
    me = lax.axis_index("tm")
    rows = difference.shape[2]
    share = rows // groups
    for k in range(points):
        difference[k] = pushed[k][...] - following[k][...]

    @pl.when(me == groups - 1)
    def _():
        first = following[points - 1]
        difference[points - 1] = first[...] - first[...]

    def sort(side):
        for g in range(groups):
            target = outs[(g % pair) ^ side]
            part = slice(g * share, (g + 1) * share)
            for k in range(points):
                for f in range(3):
                    target[g // pair, k, f, 0] = difference[k, f, part, :]

    for side in range(pair):
        pl.when(me % pair == side)(functools.partial(sort, side))


VMEM = pl.BlockSpec(memory_space=pltpu.VMEM)


def call(kernel, shapes, work, rows, columns, operands):
    chunks = columns // LANES
    extended = rows + 4 * FACTOR
    cost = pl.CostEstimate(
        flops=work * extended * columns * FACTOR * 45,
        bytes_accessed=4 * work * 3 * extended * columns,
        transcendentals=work * extended * columns * FACTOR,
    )
    return pl.pallas_call(
        functools.partial(kernel, chunks),
        out_shape=[jax.ShapeDtypeStruct(shape, jnp.float32) for shape in shapes],
        in_specs=[VMEM] * len(operands),
        out_specs=[VMEM] * len(shapes),
        scratch_shapes=[
            pltpu.VMEM((3, chunks, extended + SUB, LANES), jnp.float32),
            pltpu.VMEM((2, 3, extended // SUB, chunks, SUB, LANES), jnp.float32),
            pltpu.VMEM((3, chunks, SUB, LANES), jnp.float32),
        ],
        compiler_params=pltpu.CompilerParams(vmem_limit_bytes=24 * 2**20),
        cost_estimate=cost,
    )(*operands)


def chain(point, c_points, halo):
    _, fields, rows, columns = c_points.shape
    shape = (fields, rows, columns)
    return call(
        lambda chunks, *refs: chain_kernel(chunks, point, *refs),
        [shape, shape],
        2,
        rows,
        columns,
        (c_points, halo),
    )


def edges_of(block, width):
    return jnp.stack([block[..., -width:, :], block[..., :width, :]])


def route(shift, move):
    groups, strips = lax.axis_size("tm"), lax.axis_size("space")
    return [
        (t * strips + s, (t + shift) % groups * strips + (s + move) % strips)
        for t in range(groups)
        for s in range(strips)
    ]


def exchange(edges, shift):
    both = ("tm", "space")
    if lax.axis_size("space") == 2:
        return lax.ppermute(edges, both, route(shift, 1))
    return jnp.stack(
        [
            lax.ppermute(edges[0], both, route(shift, 1)),
            lax.ppermute(edges[1], both, route(shift, -1)),
        ]
    )


def pack(following, pushed, groups, pair):
    points, (fields, rows, columns) = len(pushed), pushed[0].shape
    packet = (groups // pair, points, fields, 1, rows // groups, columns)
    size = 4 * points * fields * rows * columns
    return pl.pallas_call(
        functools.partial(pack_kernel, points, groups, pair),
        out_shape=[jax.ShapeDtypeStruct(packet, jnp.float32)] * pair,
        in_specs=[VMEM] * (2 * points),
        out_specs=[VMEM] * pair,
        scratch_shapes=[pltpu.VMEM((points, fields, rows, columns), jnp.float32)],
        compiler_params=pltpu.CompilerParams(vmem_limit_bytes=24 * 2**20),
        cost_estimate=pl.CostEstimate(flops=size, bytes_accessed=3 * size, transcendentals=0),
    )(*following, *pushed)


def on_device(c_points):
    points = c_points.shape[0]
    groups = lax.axis_size("tm")
    me = lax.axis_index("tm")
    pair = 2 if groups % 2 == 0 else 1
    both = ("tm", "space")
    halos = [exchange(edges_of(c_points[k], 2 * FACTOR), 0) for k in range(points)]
    advanced, pushed = zip(*[chain(k, c_points, halos[k]) for k in range(points)])
    next_first = lax.ppermute(advanced[0], both, route(-1, 0))
    sides = pack([*advanced[1:], next_first], pushed, groups, pair)
    if pair == 2:
        other = lax.ppermute(sides[1], "tm", [(i, i ^ 1) for i in range(groups)])
        even = jnp.where(me & 1 == 0, sides[0], other)
        odd = jnp.where(me & 1 == 0, other, sides[0])
        sides = [even, odd]
    coarse = lax.all_to_all(
        jnp.stack(sides, axis=1),
        "tm",
        split_axis=0,
        concat_axis=0,
        axis_index_groups=[list(range(side, groups, pair)) for side in range(pair)],
        tiled=True,
    )
    coarse = coarse.reshape(groups * points, *coarse.shape[3:])
    coarse = jnp.concatenate([coarse[-1:], coarse[:-1]], axis=0)
    incoming = lax.ppermute(advanced[-1], both, route(1, 0))
    opening = jnp.where(me == 0, c_points[0], incoming)
    return (jnp.stack([opening, *advanced[:-1]]), coarse)


def solution(mesh):
    in_specs = (P("tm", None, "space", None),)
    out_specs = (P("tm", None, "space", None), P(None, None, "space", "tm", None))
    return jax.shard_map(
        on_device, mesh=mesh, in_specs=in_specs, out_specs=out_specs, check_vma=False
    )
```

```python
import functools

import jax
import jax.numpy as jnp
from jax import lax
from jax.experimental import pallas as pl
from jax.experimental.pallas import tpu as pltpu
from jax.sharding import PartitionSpec as P

FACTOR = 8
LANES = 128
SUB = 8

MOMENTUM = 0.4
PRESSURE = 0.08


def reciprocal(x):
    r = pl.reciprocal(x, approx=True)
    return r * (2.0 - x * r)


def row_terms(read, chunks, factor, lane):
    north, south, east, west = [], [], [], []
    for c in range(chunks):
        h, p, q = read(0, c), read(1, c), read(2, c)
        r = reciprocal(h)
        u = p * r
        pressure = h * h * factor
        a = p * u + pressure
        b = q * u
        d = q * (q * r) + pressure
        east.append((h - p, p - a, q - b))
        west.append((h + p, p + a, q + b))
        north.append((h - q, p - b, q - d))
        south.append((h + q, p + b, q + d))
    level = []
    for c in range(chunks):
        after, before = (c + 1) % chunks, (c - 1) % chunks
        fields = []
        for f in range(3):
            e = jnp.where(lane == 0, east[after][f], east[c][f])
            w = jnp.where(lane == LANES - 1, west[before][f], west[c][f])
            fields.append(pltpu.roll(e, LANES - 1, 1) + pltpu.roll(w, 1, 1))
        level.append(tuple(fields))
    return north, south, level


def step(src, dst, held, first, depth, chunks, factor):
    lane = lax.broadcasted_iota(jnp.int32, (SUB, LANES), 1)
    cells = [(f, c) for f in range(3) for c in range(chunks)]
    partial = south_before = None
    for n in range(depth):
        i, before = (first + n) % depth, (first + n - 1) % depth
        north, south, level = row_terms(lambda f, c: src[f, i, c], chunks, factor, lane)
        if i == 0:
            wrapped = [tuple(pltpu.roll(t, SUB - 1, 0) for t in terms) for terms in north]
        else:
            wrapped = north
        for f, c in cells:
            if n == 0:
                held[f, c] = wrapped[c][f]
            else:
                dst[f, before, c] = partial[c][f] + wrapped[c][f]
        partial = level
        if n > 0:
            partial = [
                tuple(level[c][f] + south_before[c][f] for f in range(3)) for c in range(chunks)
            ]
        south_before = south
        if i == depth - 1:
            south_before = [tuple(pltpu.roll(t, 1, 0) for t in terms) for terms in south]
    last = (first - 1) % depth
    for f, c in cells:
        if depth == 1:
            dst[f, 0, c] = partial[c][f] + held[f, c] + south_before[c][f]
        else:
            dst[f, last, c] = partial[c][f] + held[f, c]
            dst[f, first, c] = dst[f, first, c] + south_before[c][f]


def spans(chunks):
    return [slice(c * LANES, (c + 1) * LANES) for c in range(chunks)]


class Rows:
    def __init__(self, count, chunks):
        self.depth, self.chunks = count // SUB, chunks
        self.pitch = self.depth | 1

    def cells(self):
        return [
            (f, c, i) for f in range(3) for c in range(self.chunks) for i in range(self.depth)
        ]

    def pieces(self, start, count):
        found, at = [], 0
        while at < count:
            block, offset = divmod(start + at, self.depth)
            length = min(count - at, self.depth - offset)
            found.append((at, block * self.pitch + offset, length))
            at += length
        return found

    def fill(self, ext, arrays):
        start = 0
        for array in arrays:
            rows = array.shape[1]
            for at, place, length in self.pieces(start, rows):
                for f in range(3):
                    for c, span in enumerate(spans(self.chunks)):
                        ext[f, c, place : place + length, :] = array[f, at : at + length, span]
            start += rows

    def load(self, ext, state):
        for f, c, i in self.cells():
            value = ext.at[f, c][pl.ds(i, SUB, stride=self.pitch), :]
            state[0, f, i, c] = value if f == 0 else MOMENTUM * value

    def store(self, ext, state, steps):
        shrink = 0.25**steps
        for f, c, i in self.cells():
            value = state[0, f, i, c] * (shrink if f == 0 else shrink / MOMENTUM)
            ext.at[f, c][pl.ds(i, SUB, stride=self.pitch), :] = value

    def propagate(self, state, held, steps):
        depth = self.depth

        def two(_, factor):
            step(state.at[0], state.at[1], held, 0, depth, self.chunks, factor)
            factor = factor * 0.25
            step(state.at[1], state.at[0], held, 1 % depth, depth, self.chunks, factor)
            return factor * 0.25

        lax.fori_loop(0, FACTOR // 2, two, jnp.float32(PRESSURE * 0.25**steps))

    def take(self, ext, start, count, use):
        for at, place, length in self.pieces(start, count):
            for f in range(3):
                for c, span in enumerate(spans(self.chunks)):
                    use(f, span, at, length, ext[f, c, place : place + length, :])


def put(target):
    def use(f, span, at, length, value):
        target[f, at : at + length, span] = value

    return use


def behind_kernel(chunks, own, halo, advanced, pushed, ext, state, held):
    rows = own.shape[1]
    wide = Rows(rows + 4 * FACTOR, chunks)
    wide.fill(ext, [halo.at[0], own, halo.at[1]])
    wide.load(ext, state)
    wide.propagate(state, held, 0)
    wide.store(ext, state, FACTOR)
    wide.take(ext, 2 * FACTOR, rows, put(advanced))
    wide.propagate(state, held, FACTOR)
    wide.store(ext, state, 2 * FACTOR)
    wide.take(ext, 2 * FACTOR, rows, put(pushed))


def own_kernel(chunks, own, halo, behind, advanced, pushed, updated, ext, state, held, sems):
    inner, _, rows, _ = advanced.shape
    wide = Rows(rows + 4 * FACTOR, chunks)
    leading = lax.axis_index("tm") == 0
    start = pltpu.make_async_copy(own.at[0], updated.at[0], sems.at[0])
    opening = pltpu.make_async_copy(behind, updated.at[0], sems.at[0])
    pl.when(leading)(start.start)
    pl.when(jnp.logical_not(leading))(opening.start)
    copies = []
    for k in range(inner):
        wide.fill(ext, [halo.at[0, k], own.at[k], halo.at[1, k]])
        wide.load(ext, state)
        wide.propagate(state, held, 0)
        wide.store(ext, state, FACTOR)
        wide.take(ext, 2 * FACTOR, rows, put(advanced.at[k]))
        copies.append(pltpu.make_async_copy(advanced.at[k], updated.at[k + 1], sems.at[k + 1]))
        copies[-1].start()
        wide.propagate(state, held, FACTOR)
        wide.store(ext, state, 2 * FACTOR)
        wide.take(ext, 2 * FACTOR, rows, put(pushed.at[k]))
    opening.wait()
    for copy in copies:
        copy.wait()


def pack_kernel(points, groups, opening, advanced, pushed, following, packed, difference):
    rows = difference.shape[2]
    share = rows // groups
    for k in range(points):
        before = opening[...] if k == 0 else pushed[k - 1]
        difference[k] = before - (following[...] if k == points - 1 else advanced[k])

    @pl.when(lax.axis_index("tm") == 0)
    def _():
        difference[0] = advanced[0] - advanced[0]

    for g in range(groups):
        part = slice(g * share, (g + 1) * share)
        for k in range(points):
            for f in range(3):
                packed[g * points + k, f, 0] = difference[k, f, part, :]


VMEM = pl.BlockSpec(memory_space=pltpu.VMEM)


def call(kernel, shapes, work, rows, columns, operands, out_specs=None, extra=()):
    chunks = columns // LANES
    extended = rows + 4 * FACTOR
    cost = pl.CostEstimate(
        flops=work * extended * columns * FACTOR * 45,
        bytes_accessed=4 * work * 3 * extended * columns,
        transcendentals=work * extended * columns * FACTOR,
    )
    return pl.pallas_call(
        functools.partial(kernel, chunks),
        out_shape=[jax.ShapeDtypeStruct(shape, jnp.float32) for shape in shapes],
        in_specs=[VMEM] * len(operands),
        out_specs=out_specs or [VMEM] * len(shapes),
        scratch_shapes=[
            pltpu.VMEM((3, chunks, extended + SUB, LANES), jnp.float32),
            pltpu.VMEM((2, 3, extended // SUB, chunks, SUB, LANES), jnp.float32),
            pltpu.VMEM((3, chunks, SUB, LANES), jnp.float32),
            *extra,
        ],
        compiler_params=pltpu.CompilerParams(vmem_limit_bytes=24 * 2**20),
        cost_estimate=cost,
    )(*operands)


def edges_of(block, width):
    return jnp.stack([block[..., -width:, :], block[..., :width, :]])


def route(shift, move):
    groups, strips = lax.axis_size("tm"), lax.axis_size("space")
    return [
        (t * strips + s, (t + shift) % groups * strips + (s + move) % strips)
        for t in range(groups)
        for s in range(strips)
    ]


def exchange(edges, shift):
    both = ("tm", "space")
    if lax.axis_size("space") == 2:
        return lax.ppermute(edges, both, route(shift, 1))
    return jnp.stack(
        [
            lax.ppermute(edges[0], both, route(shift, 1)),
            lax.ppermute(edges[1], both, route(shift, -1)),
        ]
    )


def pack(opening, advanced, pushed, following, groups):
    points, (fields, rows, columns) = pushed.shape[0] + 1, opening.shape
    packet = (groups * points, fields, 1, rows // groups, columns)
    size = points * fields * rows * columns
    return pl.pallas_call(
        functools.partial(pack_kernel, points, groups),
        out_shape=jax.ShapeDtypeStruct(packet, jnp.float32),
        in_specs=[VMEM] * 4,
        out_specs=VMEM,
        scratch_shapes=[pltpu.VMEM((points, fields, rows, columns), jnp.float32)],
        compiler_params=pltpu.CompilerParams(vmem_limit_bytes=24 * 2**20),
        cost_estimate=pl.CostEstimate(flops=size, bytes_accessed=12 * size, transcendentals=0),
    )(opening, advanced, pushed, following)


def on_device(c_points):
    points, fields, rows, columns = c_points.shape
    groups = lax.axis_size("tm")
    both = ("tm", "space")
    last = c_points[-1]
    behind_halo = exchange(edges_of(last, 2 * FACTOR), 1)
    behind = lax.ppermute(last, both, route(1, 0))
    halo = exchange(edges_of(c_points[:-1], 2 * FACTOR), 0)
    opening, first_pushed = call(
        behind_kernel, [last.shape] * 2, 2, rows, columns, (behind, behind_halo)
    )
    following = lax.ppermute(opening, both, route(-1, 0))
    inner = (points - 1, fields, rows, columns)
    advanced, pushed, updated = call(
        own_kernel,
        [inner, inner, c_points.shape],
        2 * (points - 1),
        rows,
        columns,
        (c_points, halo, opening),
        out_specs=[VMEM, VMEM, pl.BlockSpec(memory_space=pl.ANY)],
        extra=[pltpu.SemaphoreType.DMA((points,))],
    )
    packed = pack(first_pushed, advanced, pushed, following, groups)
    return (updated, lax.all_to_all(packed, "tm", split_axis=0, concat_axis=0, tiled=True))


def solution(mesh):
    in_specs = (P("tm", None, "space", None),)
    out_specs = (P("tm", None, "space", None), P(None, None, "space", "tm", None))
    return jax.shard_map(
        on_device, mesh=mesh, in_specs=in_specs, out_specs=out_specs, check_vma=False
    )
```

```python
import functools

import jax
import jax.numpy as jnp
from jax import lax
from jax.experimental import pallas as pl
from jax.experimental.pallas import tpu as pltpu
from jax.sharding import PartitionSpec as P

FACTOR = 8
LANES = 128
SUB = 8

MOMENTUM = 0.4
PRESSURE = 0.08


def reciprocal(x):
    r = pl.reciprocal(x, approx=True)
    return r * (2.0 - x * r)


def row_terms(read, chunks, factor, lane):
    north, south, east, west = [], [], [], []
    for c in range(chunks):
        h, p, q = read(0, c), read(1, c), read(2, c)
        r = reciprocal(h)
        u = p * r
        pressure = h * h * factor
        a = p * u + pressure
        b = q * u
        d = q * (q * r) + pressure
        east.append((h - p, p - a, q - b))
        west.append((h + p, p + a, q + b))
        north.append((h - q, p - b, q - d))
        south.append((h + q, p + b, q + d))
    level = []
    for c in range(chunks):
        after, before = (c + 1) % chunks, (c - 1) % chunks
        fields = []
        for f in range(3):
            e = jnp.where(lane == 0, east[after][f], east[c][f])
            w = jnp.where(lane == LANES - 1, west[before][f], west[c][f])
            fields.append(pltpu.roll(e, LANES - 1, 1) + pltpu.roll(w, 1, 1))
        level.append(tuple(fields))
    return north, south, level


def step(src, dst, held, first, depth, chunks, factor):
    lane = lax.broadcasted_iota(jnp.int32, (SUB, LANES), 1)
    cells = [(f, c) for f in range(3) for c in range(chunks)]
    partial = south_before = None
    for n in range(depth):
        i, before = (first + n) % depth, (first + n - 1) % depth
        north, south, level = row_terms(lambda f, c: src[f, i, c], chunks, factor, lane)
        if i == 0:
            wrapped = [tuple(pltpu.roll(t, SUB - 1, 0) for t in terms) for terms in north]
        else:
            wrapped = north
        for f, c in cells:
            if n == 0:
                held[f, c] = wrapped[c][f]
            else:
                dst[f, before, c] = partial[c][f] + wrapped[c][f]
        partial = level
        if n > 0:
            partial = [
                tuple(level[c][f] + south_before[c][f] for f in range(3)) for c in range(chunks)
            ]
        south_before = south
        if i == depth - 1:
            south_before = [tuple(pltpu.roll(t, 1, 0) for t in terms) for terms in south]
    last = (first - 1) % depth
    for f, c in cells:
        if depth == 1:
            dst[f, 0, c] = partial[c][f] + held[f, c] + south_before[c][f]
        else:
            dst[f, last, c] = partial[c][f] + held[f, c]
            dst[f, first, c] = dst[f, first, c] + south_before[c][f]


def spans(chunks):
    return [slice(c * LANES, (c + 1) * LANES) for c in range(chunks)]


class Rows:
    def __init__(self, count, chunks):
        self.depth, self.chunks = count // SUB, chunks
        self.pitch = self.depth | 1

    def cells(self):
        return [
            (f, c, i) for f in range(3) for c in range(self.chunks) for i in range(self.depth)
        ]

    def pieces(self, start, count):
        found, at = [], 0
        while at < count:
            block, offset = divmod(start + at, self.depth)
            length = min(count - at, self.depth - offset)
            found.append((at, block * self.pitch + offset, length))
            at += length
        return found

    def fill(self, ext, arrays):
        start = 0
        for array in arrays:
            rows = array.shape[1]
            for at, place, length in self.pieces(start, rows):
                for f in range(3):
                    for c, span in enumerate(spans(self.chunks)):
                        ext[f, c, place : place + length, :] = array[f, at : at + length, span]
            start += rows

    def load(self, ext, state):
        for f, c, i in self.cells():
            value = ext.at[f, c][pl.ds(i, SUB, stride=self.pitch), :]
            state[0, f, i, c] = value if f == 0 else MOMENTUM * value

    def store(self, ext, state, steps):
        shrink = 0.25**steps
        for f, c, i in self.cells():
            value = state[0, f, i, c] * (shrink if f == 0 else shrink / MOMENTUM)
            ext.at[f, c][pl.ds(i, SUB, stride=self.pitch), :] = value

    def propagate(self, state, held, steps):
        depth = self.depth

        def two(_, factor):
            step(state.at[0], state.at[1], held, 0, depth, self.chunks, factor)
            factor = factor * 0.25
            step(state.at[1], state.at[0], held, 1 % depth, depth, self.chunks, factor)
            return factor * 0.25

        lax.fori_loop(0, FACTOR // 2, two, jnp.float32(PRESSURE * 0.25**steps))

    def take(self, ext, start, count, use):
        for at, place, length in self.pieces(start, count):
            for f in range(3):
                for c, span in enumerate(spans(self.chunks)):
                    use(f, span, at, length, ext[f, c, place : place + length, :])


def put(target):
    def use(f, span, at, length, value):
        target[f, at : at + length, span] = value

    return use


def chain_kernel(chunks, point, own, halo, advanced, pushed, ext, state, held):
    rows = own.shape[2]
    wide = Rows(rows + 4 * FACTOR, chunks)
    wide.fill(ext, [halo.at[0], own.at[point], halo.at[1]])
    wide.load(ext, state)
    wide.propagate(state, held, 0)
    wide.store(ext, state, FACTOR)
    wide.take(ext, 2 * FACTOR, rows, put(advanced))
    wide.propagate(state, held, FACTOR)
    wide.store(ext, state, 2 * FACTOR)
    wide.take(ext, 2 * FACTOR, rows, put(pushed))


def pack_kernel(points, groups, *refs):
    following, pushed, (packed, difference) = refs[:points], refs[points:-2], refs[-2:]
    rows = difference.shape[2]
    share = rows // groups
    for k in range(points):
        difference[k] = pushed[k][...] - following[k][...]

    @pl.when(lax.axis_index("tm") == groups - 1)
    def _():
        first = following[points - 1]
        difference[points - 1] = first[...] - first[...]

    for g in range(groups):
        part = slice(g * share, (g + 1) * share)
        for k in range(points):
            for f in range(3):
                packed[g * points + k, f, 0] = difference[k, f, part, :]


VMEM = pl.BlockSpec(memory_space=pltpu.VMEM)


def call(kernel, shapes, work, rows, columns, operands):
    chunks = columns // LANES
    extended = rows + 4 * FACTOR
    cost = pl.CostEstimate(
        flops=work * extended * columns * FACTOR * 45,
        bytes_accessed=4 * work * 3 * extended * columns,
        transcendentals=work * extended * columns * FACTOR,
    )
    return pl.pallas_call(
        functools.partial(kernel, chunks),
        out_shape=[jax.ShapeDtypeStruct(shape, jnp.float32) for shape in shapes],
        in_specs=[VMEM] * len(operands),
        out_specs=[VMEM] * len(shapes),
        scratch_shapes=[
            pltpu.VMEM((3, chunks, extended + SUB, LANES), jnp.float32),
            pltpu.VMEM((2, 3, extended // SUB, chunks, SUB, LANES), jnp.float32),
            pltpu.VMEM((3, chunks, SUB, LANES), jnp.float32),
        ],
        compiler_params=pltpu.CompilerParams(vmem_limit_bytes=24 * 2**20),
        cost_estimate=cost,
    )(*operands)


def chain(point, c_points, halo):
    _, fields, rows, columns = c_points.shape
    shape = (fields, rows, columns)
    return call(
        lambda chunks, *refs: chain_kernel(chunks, point, *refs),
        [shape, shape],
        2,
        rows,
        columns,
        (c_points, halo),
    )


def edges_of(block, width):
    return jnp.stack([block[..., -width:, :], block[..., :width, :]])


def route(shift, move):
    groups, strips = lax.axis_size("tm"), lax.axis_size("space")
    return [
        (t * strips + s, (t + shift) % groups * strips + (s + move) % strips)
        for t in range(groups)
        for s in range(strips)
    ]


def exchange(edges, shift):
    both = ("tm", "space")
    if lax.axis_size("space") == 2:
        return lax.ppermute(edges, both, route(shift, 1))
    return jnp.stack(
        [
            lax.ppermute(edges[0], both, route(shift, 1)),
            lax.ppermute(edges[1], both, route(shift, -1)),
        ]
    )


def pack(following, pushed, groups):
    points, (fields, rows, columns) = len(pushed), pushed[0].shape
    packet = (groups * points, fields, 1, rows // groups, columns)
    size = points * fields * rows * columns
    return pl.pallas_call(
        functools.partial(pack_kernel, points, groups),
        out_shape=jax.ShapeDtypeStruct(packet, jnp.float32),
        in_specs=[VMEM] * (2 * points),
        out_specs=VMEM,
        scratch_shapes=[pltpu.VMEM((points, fields, rows, columns), jnp.float32)],
        compiler_params=pltpu.CompilerParams(vmem_limit_bytes=24 * 2**20),
        cost_estimate=pl.CostEstimate(flops=size, bytes_accessed=12 * size, transcendentals=0),
    )(*following, *pushed)


def on_device(c_points):
    points = c_points.shape[0]
    groups = lax.axis_size("tm")
    halos = [exchange(edges_of(c_points[k], 2 * FACTOR), 0) for k in range(points)]
    advanced, pushed = zip(*[chain(k, c_points, halos[k]) for k in range(points)])
    next_first = lax.ppermute(advanced[0], ("tm", "space"), route(-1, 0))
    packed = pack([*advanced[1:], next_first], pushed, groups)
    coarse = lax.all_to_all(packed, "tm", split_axis=0, concat_axis=0, tiled=True)
    coarse = jnp.concatenate([coarse[-1:], coarse[:-1]], axis=0)
    incoming = lax.ppermute(advanced[-1], "tm", [(i, i + 1) for i in range(groups - 1)])
    opening = jnp.where(lax.axis_index("tm") == 0, c_points[0], incoming)
    return (jnp.stack([opening, *advanced[:-1]]), coarse)


def solution(mesh):
    in_specs = (P("tm", None, "space", None),)
    out_specs = (P("tm", None, "space", None), P(None, None, "space", "tm", None))
    return jax.shard_map(
        on_device, mesh=mesh, in_specs=in_specs, out_specs=out_specs, check_vma=False
    )
```

```python
import functools

import jax
import jax.numpy as jnp
from jax import lax
from jax.experimental import pallas as pl
from jax.experimental.pallas import tpu as pltpu
from jax.sharding import PartitionSpec as P

FACTOR = 8
LANES = 128
SUB = 8

MOMENTUM = 0.4
PRESSURE = 0.08


def reciprocal(x):
    r = pl.reciprocal(x, approx=True)
    return r * (2.0 - x * r)


def row_terms(read, chunks, factor, lane):
    north, south, east, west = [], [], [], []
    for c in range(chunks):
        h, p, q = read(0, c), read(1, c), read(2, c)
        r = reciprocal(h)
        u = p * r
        pressure = h * h * factor
        a = p * u + pressure
        b = q * u
        d = q * (q * r) + pressure
        east.append((h - p, p - a, q - b))
        west.append((h + p, p + a, q + b))
        north.append((h - q, p - b, q - d))
        south.append((h + q, p + b, q + d))
    level = []
    for c in range(chunks):
        after, before = (c + 1) % chunks, (c - 1) % chunks
        fields = []
        for f in range(3):
            e = jnp.where(lane == 0, east[after][f], east[c][f])
            w = jnp.where(lane == LANES - 1, west[before][f], west[c][f])
            fields.append(pltpu.roll(e, LANES - 1, 1) + pltpu.roll(w, 1, 1))
        level.append(tuple(fields))
    return north, south, level


def step(src, dst, held, first, depth, chunks, factor):
    lane = lax.broadcasted_iota(jnp.int32, (SUB, LANES), 1)
    cells = [(f, c) for f in range(3) for c in range(chunks)]
    partial = south_before = None
    for n in range(depth):
        i, before = (first + n) % depth, (first + n - 1) % depth
        north, south, level = row_terms(lambda f, c: src[f, i, c], chunks, factor, lane)
        if i == 0:
            wrapped = [tuple(pltpu.roll(t, SUB - 1, 0) for t in terms) for terms in north]
        else:
            wrapped = north
        for f, c in cells:
            if n == 0:
                held[f, c] = wrapped[c][f]
            else:
                dst[f, before, c] = partial[c][f] + wrapped[c][f]
        partial = level
        if n > 0:
            partial = [
                tuple(level[c][f] + south_before[c][f] for f in range(3)) for c in range(chunks)
            ]
        south_before = south
        if i == depth - 1:
            south_before = [tuple(pltpu.roll(t, 1, 0) for t in terms) for terms in south]
    last = (first - 1) % depth
    for f, c in cells:
        if depth == 1:
            dst[f, 0, c] = partial[c][f] + held[f, c] + south_before[c][f]
        else:
            dst[f, last, c] = partial[c][f] + held[f, c]
            dst[f, first, c] = dst[f, first, c] + south_before[c][f]


def spans(chunks):
    return [slice(c * LANES, (c + 1) * LANES) for c in range(chunks)]


class Rows:
    def __init__(self, count, chunks):
        self.depth, self.chunks = count // SUB, chunks
        self.pitch = self.depth | 1

    def cells(self):
        return [
            (f, c, i) for f in range(3) for c in range(self.chunks) for i in range(self.depth)
        ]

    def pieces(self, start, count):
        found, at = [], 0
        while at < count:
            block, offset = divmod(start + at, self.depth)
            length = min(count - at, self.depth - offset)
            found.append((at, block * self.pitch + offset, length))
            at += length
        return found

    def fill(self, ext, arrays):
        start = 0
        for array in arrays:
            rows = array.shape[1]
            for at, place, length in self.pieces(start, rows):
                for f in range(3):
                    for c, span in enumerate(spans(self.chunks)):
                        ext[f, c, place : place + length, :] = array[f, at : at + length, span]
            start += rows

    def load(self, ext, state):
        for f, c, i in self.cells():
            value = ext.at[f, c][pl.ds(i, SUB, stride=self.pitch), :]
            state[0, f, i, c] = value if f == 0 else MOMENTUM * value

    def store(self, ext, state, steps):
        shrink = 0.25**steps
        for f, c, i in self.cells():
            value = state[0, f, i, c] * (shrink if f == 0 else shrink / MOMENTUM)
            ext.at[f, c][pl.ds(i, SUB, stride=self.pitch), :] = value

    def propagate(self, state, held, steps):
        depth = self.depth

        def two(_, factor):
            step(state.at[0], state.at[1], held, 0, depth, self.chunks, factor)
            factor = factor * 0.25
            step(state.at[1], state.at[0], held, 1 % depth, depth, self.chunks, factor)
            return factor * 0.25

        lax.fori_loop(0, FACTOR // 2, two, jnp.float32(PRESSURE * 0.25**steps))

    def take(self, ext, start, count, use):
        for at, place, length in self.pieces(start, count):
            for f in range(3):
                for c, span in enumerate(spans(self.chunks)):
                    use(f, span, at, length, ext[f, c, place : place + length, :])


def put(target):
    def use(f, span, at, length, value):
        target[f, at : at + length, span] = value

    return use


def chain_kernel(chunks, point, own, halo, advanced, pushed, ext, state, held):
    rows = own.shape[2]
    wide = Rows(rows + 4 * FACTOR, chunks)
    wide.fill(ext, [halo.at[0], own.at[point], halo.at[1]])
    wide.load(ext, state)
    wide.propagate(state, held, 0)
    wide.store(ext, state, FACTOR)
    wide.take(ext, 2 * FACTOR, rows, put(advanced))
    wide.propagate(state, held, FACTOR)
    wide.store(ext, state, 2 * FACTOR)
    wide.take(ext, 2 * FACTOR, rows, put(pushed))


def half_kernel(chunks, own, halo, advanced, ext, state, held):
    rows = own.shape[1]
    narrow = Rows(rows + 2 * FACTOR, chunks)
    narrow.fill(ext, [halo.at[0], own, halo.at[1]])
    narrow.load(ext, state)
    narrow.propagate(state, held, 0)
    narrow.store(ext, state, FACTOR)
    narrow.take(ext, FACTOR, rows, put(advanced))


def pack_kernel(points, groups, *refs):
    following, pushed, (packed, difference) = refs[:points], refs[points:-2], refs[-2:]
    _, _, rows, columns = difference.shape
    share = rows // groups
    for k in range(points):
        difference[k] = pushed[k][...] - following[k][...]

    @pl.when(lax.axis_index("tm") == groups - 1)
    def _():
        first = following[points - 1]
        difference[points - 1] = first[...] - first[...]

    for g in range(groups):
        part = slice(g * share, (g + 1) * share)
        for k in range(points):
            for f in range(3):
                for span in spans(columns // LANES):
                    packed[g * points + k, f, 0, :, span] = difference[k, f, part, span]


VMEM = pl.BlockSpec(memory_space=pltpu.VMEM)


def call(kernel, shapes, work, rows, columns, operands):
    chunks = columns // LANES
    extended = rows + 4 * FACTOR
    cost = pl.CostEstimate(
        flops=work * extended * columns * FACTOR * 45,
        bytes_accessed=4 * work * 3 * extended * columns,
        transcendentals=work * extended * columns * FACTOR,
    )
    return pl.pallas_call(
        functools.partial(kernel, chunks),
        out_shape=[jax.ShapeDtypeStruct(shape, jnp.float32) for shape in shapes],
        in_specs=[VMEM] * len(operands),
        out_specs=[VMEM] * len(shapes),
        scratch_shapes=[
            pltpu.VMEM((3, chunks, extended + SUB, LANES), jnp.float32),
            pltpu.VMEM((2, 3, extended // SUB, chunks, SUB, LANES), jnp.float32),
            pltpu.VMEM((3, chunks, SUB, LANES), jnp.float32),
        ],
        compiler_params=pltpu.CompilerParams(vmem_limit_bytes=24 * 2**20),
        cost_estimate=cost,
    )(*operands)


def chain(point, c_points, halo):
    _, fields, rows, columns = c_points.shape
    shape = (fields, rows, columns)
    return call(
        lambda chunks, *refs: chain_kernel(chunks, point, *refs),
        [shape, shape],
        2,
        rows,
        columns,
        (c_points, halo),
    )


def edges_of(block, width):
    return jnp.stack([block[..., -width:, :], block[..., :width, :]])


def route(shift, move):
    groups, strips = lax.axis_size("tm"), lax.axis_size("space")
    return [
        (t * strips + s, (t + shift) % groups * strips + (s + move) % strips)
        for t in range(groups)
        for s in range(strips)
    ]


def exchange(edges, shift):
    both = ("tm", "space")
    if lax.axis_size("space") == 2:
        return lax.ppermute(edges, both, route(shift, 1))
    return jnp.stack(
        [
            lax.ppermute(edges[0], both, route(shift, 1)),
            lax.ppermute(edges[1], both, route(shift, -1)),
        ]
    )


def pack(following, pushed, groups):
    points, (fields, rows, columns) = len(pushed), pushed[0].shape
    packet = (groups * points, fields, 1, rows // groups, columns)
    size = points * fields * rows * columns
    return pl.pallas_call(
        functools.partial(pack_kernel, points, groups),
        out_shape=jax.ShapeDtypeStruct(packet, jnp.float32),
        in_specs=[VMEM] * (2 * points),
        out_specs=VMEM,
        scratch_shapes=[pltpu.VMEM((points, fields, rows, columns), jnp.float32)],
        compiler_params=pltpu.CompilerParams(vmem_limit_bytes=24 * 2**20),
        cost_estimate=pl.CostEstimate(flops=size, bytes_accessed=12 * size, transcendentals=0),
    )(*following, *pushed)


def on_device(c_points):
    points = c_points.shape[0]
    groups = lax.axis_size("tm")
    both = ("tm", "space")
    last = c_points[-1]
    halos = [exchange(edges_of(c_points[k], 2 * FACTOR), 0) for k in range(points)]
    behind = lax.ppermute(last, both, route(1, 0))
    behind_halo = exchange(edges_of(last, FACTOR), 1)
    advanced, pushed = zip(*[chain(k, c_points, halos[k]) for k in range(points)])
    next_first = lax.ppermute(advanced[0], both, route(-1, 0))
    packed = pack([*advanced[1:], next_first], pushed, groups)
    coarse = lax.all_to_all(packed, "tm", split_axis=0, concat_axis=0, tiled=True)
    coarse = jnp.concatenate([coarse[-1:], coarse[:-1]], axis=0)
    behind, behind_halo, _ = lax.optimization_barrier((behind, behind_halo, packed))
    (before,) = call(half_kernel, [last.shape], 1, *last.shape[1:], (behind, behind_halo))
    opening = jnp.where(lax.axis_index("tm") == 0, c_points[0], before)
    return (jnp.stack([opening, *advanced[:-1]]), coarse)


def solution(mesh):
    in_specs = (P("tm", None, "space", None),)
    out_specs = (P("tm", None, "space", None), P(None, None, "space", "tm", None))
    return jax.shard_map(
        on_device, mesh=mesh, in_specs=in_specs, out_specs=out_specs, check_vma=False
    )
```

```python
import functools

import jax
import jax.numpy as jnp
from jax import lax
from jax.experimental import pallas as pl
from jax.experimental.pallas import tpu as pltpu
from jax.sharding import PartitionSpec as P

FACTOR = 8
LANES = 128
SUB = 8

MOMENTUM = 0.4
PRESSURE = 0.08


def reciprocal(x):
    r = pl.reciprocal(x, approx=True)
    return r * (2.0 - x * r)


def cell_terms(h, p, q, factor):
    r = reciprocal(h)
    u = p * r
    pressure = h * h * factor
    a = p * u + pressure
    b = q * u
    d = q * (q * r) + pressure
    return (h - q, p - b, q - d), (h + q, p + b, q + d), (h - p, p - a, q - b), (h + p, p + a, q + b)


def added(x, y):
    return y if x is None else [a + b for a, b in zip(x, y)]


def step(src, dst, first, depth, chunks, factor):
    lane = lax.broadcasted_iota(jnp.int32, (SUB, LANES), 1)
    fields, last = range(3), chunks - 1
    below = [None] * chunks

    def from_east(mine, after):
        return [pltpu.roll(jnp.where(lane == 0, a, m), LANES - 1, 1) for m, a in zip(mine, after)]

    def from_west(mine, before):
        return [pltpu.roll(jnp.where(lane == last_lane, b, m), 1, 1) for m, b in zip(mine, before)]

    last_lane = LANES - 1
    for n in range(depth):
        i, before = (first + n) % depth, (first + n - 1) % depth

        def keep(c, total):
            for f in fields:
                dst[f, i, c] = dst[f, i, c] + total[f] if n == depth - 1 else total[f]

        to_west, to_east, total = [None] * chunks, [None] * chunks, below
        below = [None] * chunks
        for c in range(chunks):
            to_south, to_north, to_west[c], to_east[c] = cell_terms(
                src[0, i, c], src[1, i, c], src[2, i, c], factor
            )
            if i == 0:
                to_south = [pltpu.roll(t, SUB - 1, 0) for t in to_south]
            if i == depth - 1:
                to_north = [pltpu.roll(t, 1, 0) for t in to_north]
            for f in fields:
                dst[f, before, c] = to_south[f] if n == 0 else dst[f, before, c] + to_south[f]
            below[c] = to_north
            if c > 0:
                total[c] = added(total[c], from_west(to_east[c], to_east[c - 1]))
                total[c - 1] = added(total[c - 1], from_east(to_west[c - 1], to_west[c]))
                if c > 1:
                    keep(c - 1, total[c - 1])
        total[0] = added(total[0], from_west(to_east[0], to_east[last]))
        total[last] = added(total[last], from_east(to_west[last], to_west[0]))
        for c in sorted({0, last}):
            keep(c, total[c])
    for c in range(chunks):
        for f in fields:
            dst[f, first, c] = dst[f, first, c] + below[c][f]


def spans(chunks):
    return [slice(c * LANES, (c + 1) * LANES) for c in range(chunks)]


class Rows:
    def __init__(self, count, chunks):
        self.depth, self.chunks = count // SUB, chunks
        self.pitch = self.depth | 1

    def cells(self):
        return [
            (f, c, i) for f in range(3) for c in range(self.chunks) for i in range(self.depth)
        ]

    def pieces(self, start, count):
        found, at = [], 0
        while at < count:
            block, offset = divmod(start + at, self.depth)
            length = min(count - at, self.depth - offset)
            found.append((at, block * self.pitch + offset, length))
            at += length
        return found

    def fill(self, ext, arrays):
        start = 0
        for array in arrays:
            rows = array.shape[1]
            for at, place, length in self.pieces(start, rows):
                for f in range(3):
                    for c, span in enumerate(spans(self.chunks)):
                        ext[f, c, place : place + length, :] = array[f, at : at + length, span]
            start += rows

    def load(self, ext, state):
        for f, c, i in self.cells():
            value = ext.at[f, c][pl.ds(i, SUB, stride=self.pitch), :]
            state[0, f, i, c] = value if f == 0 else MOMENTUM * value

    def store(self, ext, state, steps):
        shrink = 0.25**steps
        for f, c, i in self.cells():
            value = state[0, f, i, c] * (shrink if f == 0 else shrink / MOMENTUM)
            ext.at[f, c][pl.ds(i, SUB, stride=self.pitch), :] = value

    def propagate(self, state, steps):
        depth = self.depth

        def two(_, factor):
            step(state.at[0], state.at[1], 0, depth, self.chunks, factor)
            factor = factor * 0.25
            step(state.at[1], state.at[0], 1 % depth, depth, self.chunks, factor)
            return factor * 0.25

        lax.fori_loop(0, FACTOR // 2, two, jnp.float32(PRESSURE * 0.25**steps))

    def take(self, ext, start, count, use):
        for at, place, length in self.pieces(start, count):
            for f in range(3):
                for c, span in enumerate(spans(self.chunks)):
                    use(f, span, at, length, ext[f, c, place : place + length, :])


def put(target):
    def use(f, span, at, length, value):
        target[f, at : at + length, span] = value

    return use


def chain_kernel(chunks, point, own, halo, advanced, pushed, ext, state):
    rows = own.shape[2]
    wide = Rows(rows + 4 * FACTOR, chunks)
    wide.fill(ext, [halo.at[0], own.at[point], halo.at[1]])
    wide.load(ext, state)
    wide.propagate(state, 0)
    wide.store(ext, state, FACTOR)
    wide.take(ext, 2 * FACTOR, rows, put(advanced))
    wide.propagate(state, FACTOR)
    wide.store(ext, state, 2 * FACTOR)
    wide.take(ext, 2 * FACTOR, rows, put(pushed))


VMEM = pl.BlockSpec(memory_space=pltpu.VMEM)


def call(kernel, shapes, work, rows, columns, operands):
    chunks = columns // LANES
    extended = rows + 4 * FACTOR
    cost = pl.CostEstimate(
        flops=work * extended * columns * FACTOR * 45,
        bytes_accessed=4 * work * 3 * extended * columns,
        transcendentals=work * extended * columns * FACTOR,
    )
    return pl.pallas_call(
        functools.partial(kernel, chunks),
        out_shape=[jax.ShapeDtypeStruct(shape, jnp.float32) for shape in shapes],
        in_specs=[VMEM] * len(operands),
        out_specs=[VMEM] * len(shapes),
        scratch_shapes=[
            pltpu.VMEM((3, chunks, extended + SUB, LANES), jnp.float32),
            pltpu.VMEM((2, 3, extended // SUB, chunks, SUB, LANES), jnp.float32),
        ],
        compiler_params=pltpu.CompilerParams(vmem_limit_bytes=24 * 2**20),
        cost_estimate=cost,
    )(*operands)


def chain(point, c_points, halo):
    _, fields, rows, columns = c_points.shape
    shape = (fields, rows, columns)
    return call(
        lambda chunks, *refs: chain_kernel(chunks, point, *refs),
        [shape, shape],
        2,
        rows,
        columns,
        (c_points, halo),
    )


def edges_of(block, width):
    return jnp.stack([block[..., -width:, :], block[..., :width, :]])


def route(shift, move):
    groups, strips = lax.axis_size("tm"), lax.axis_size("space")
    return [
        (t * strips + s, (t + shift) % groups * strips + (s + move) % strips)
        for t in range(groups)
        for s in range(strips)
    ]


def exchange(edges, shift):
    both = ("tm", "space")
    if lax.axis_size("space") == 2:
        return lax.ppermute(edges, both, route(shift, 1))
    return jnp.stack(
        [
            lax.ppermute(edges[0], both, route(shift, 1)),
            lax.ppermute(edges[1], both, route(shift, -1)),
        ]
    )


def on_device(c_points):
    points = c_points.shape[0]
    groups = lax.axis_size("tm")
    halos = [exchange(edges_of(c_points[k], 2 * FACTOR), 0) for k in range(points)]
    advanced, pushed = zip(*[chain(k, c_points, halos[k]) for k in range(points)])
    next_first = lax.ppermute(advanced[0], ("tm", "space"), route(-1, 0))
    me = lax.axis_index("tm")
    wrapped = jnp.where(me == groups - 1, next_first, pushed[-1])
    residual = jnp.stack(
        [after - now for after, now in zip([*pushed[:-1], wrapped], [*advanced[1:], next_first])]
    )
    points, fields, rows, columns = c_points.shape
    shares = residual.reshape(points, fields, groups, rows // groups, columns)
    packed = shares.transpose(2, 0, 1, 3, 4).reshape(-1, fields, 1, rows // groups, columns)
    coarse = lax.all_to_all(packed, "tm", split_axis=0, concat_axis=0, tiled=True)
    coarse = jnp.concatenate([coarse[-1:], coarse[:-1]], axis=0)
    incoming = lax.ppermute(advanced[-1], "tm", [(i, i + 1) for i in range(groups - 1)])
    opening = jnp.where(me == 0, c_points[0], incoming)
    return (jnp.stack([opening, *advanced[:-1]]), coarse)


def solution(mesh):
    in_specs = (P("tm", None, "space", None),)
    out_specs = (P("tm", None, "space", None), P(None, None, "space", "tm", None))
    return jax.shard_map(
        on_device, mesh=mesh, in_specs=in_specs, out_specs=out_specs, check_vma=False
    )
```

```python
import functools

import jax
import jax.numpy as jnp
from jax import lax
from jax.experimental import pallas as pl
from jax.experimental.pallas import tpu as pltpu
from jax.sharding import PartitionSpec as P

FACTOR = 8
LANES = 128
SUB = 8

MOMENTUM = 0.4
PRESSURE = 0.08


def reciprocal(x):
    r = pl.reciprocal(x, approx=True)
    return r * (2.0 - x * r)


def row_terms(read, chunks, factor, lane):
    north, south, east, west = [], [], [], []
    for c in range(chunks):
        h, p, q = read(0, c), read(1, c), read(2, c)
        r = reciprocal(h)
        u = p * r
        pressure = h * h * factor
        a = p * u + pressure
        b = q * u
        d = q * (q * r) + pressure
        east.append((h - p, p - a, q - b))
        west.append((h + p, p + a, q + b))
        north.append((h - q, p - b, q - d))
        south.append((h + q, p + b, q + d))
    level = []
    for c in range(chunks):
        after, before = (c + 1) % chunks, (c - 1) % chunks
        fields = []
        for f in range(3):
            e = jnp.where(lane == 0, east[after][f], east[c][f])
            w = jnp.where(lane == LANES - 1, west[before][f], west[c][f])
            fields.append(pltpu.roll(e, LANES - 1, 1) + pltpu.roll(w, 1, 1))
        level.append(tuple(fields))
    return north, south, level


def step(src, dst, held, first, depth, chunks, factor):
    lane = lax.broadcasted_iota(jnp.int32, (SUB, LANES), 1)
    cells = [(f, c) for f in range(3) for c in range(chunks)]
    partial = south_before = None
    for n in range(depth):
        i, before = (first + n) % depth, (first + n - 1) % depth
        north, south, level = row_terms(lambda f, c: src[f, i, c], chunks, factor, lane)
        if i == 0:
            wrapped = [tuple(pltpu.roll(t, SUB - 1, 0) for t in terms) for terms in north]
        else:
            wrapped = north
        for f, c in cells:
            if n == 0:
                held[f, c] = wrapped[c][f]
            else:
                dst[f, before, c] = partial[c][f] + wrapped[c][f]
        partial = level
        if n > 0:
            partial = [
                tuple(level[c][f] + south_before[c][f] for f in range(3)) for c in range(chunks)
            ]
        south_before = south
        if i == depth - 1:
            south_before = [tuple(pltpu.roll(t, 1, 0) for t in terms) for terms in south]
    last = (first - 1) % depth
    for f, c in cells:
        if depth == 1:
            dst[f, 0, c] = partial[c][f] + held[f, c] + south_before[c][f]
        else:
            dst[f, last, c] = partial[c][f] + held[f, c]
            dst[f, first, c] = dst[f, first, c] + south_before[c][f]


def spans(chunks):
    return [slice(c * LANES, (c + 1) * LANES) for c in range(chunks)]


class Rows:
    def __init__(self, count, chunks):
        self.depth, self.chunks = count // SUB, chunks
        self.pitch = self.depth | 1

    def cells(self):
        return [
            (f, c, i) for f in range(3) for c in range(self.chunks) for i in range(self.depth)
        ]

    def pieces(self, start, count):
        found, at = [], 0
        while at < count:
            block, offset = divmod(start + at, self.depth)
            length = min(count - at, self.depth - offset)
            found.append((at, block * self.pitch + offset, length))
            at += length
        return found

    def fill(self, ext, arrays):
        start = 0
        for array in arrays:
            rows = array.shape[1]
            for at, place, length in self.pieces(start, rows):
                for f in range(3):
                    for c, span in enumerate(spans(self.chunks)):
                        ext[f, c, place : place + length, :] = array[f, at : at + length, span]
            start += rows

    def load(self, ext, state):
        for f, c, i in self.cells():
            value = ext.at[f, c][pl.ds(i, SUB, stride=self.pitch), :]
            state[0, f, i, c] = value if f == 0 else MOMENTUM * value

    def store(self, ext, state, steps):
        shrink = 0.25**steps
        for f, c, i in self.cells():
            value = state[0, f, i, c] * (shrink if f == 0 else shrink / MOMENTUM)
            ext.at[f, c][pl.ds(i, SUB, stride=self.pitch), :] = value

    def propagate(self, state, held, steps):
        depth = self.depth

        def two(_, factor):
            step(state.at[0], state.at[1], held, 0, depth, self.chunks, factor)
            factor = factor * 0.25
            step(state.at[1], state.at[0], held, 1 % depth, depth, self.chunks, factor)
            return factor * 0.25

        lax.fori_loop(0, FACTOR // 2, two, jnp.float32(PRESSURE * 0.25**steps))

    def take(self, ext, start, count, use):
        for at, place, length in self.pieces(start, count):
            for f in range(3):
                for c, span in enumerate(spans(self.chunks)):
                    use(f, span, at, length, ext[f, c, place : place + length, :])


def put(target):
    def use(f, span, at, length, value):
        target[f, at : at + length, span] = value

    return use


def chain_kernel(chunks, point, own, halo, advanced, pushed, ext, state, held):
    rows = own.shape[2]
    wide = Rows(rows + 4 * FACTOR, chunks)
    wide.fill(ext, [halo.at[0], own.at[point], halo.at[1]])
    wide.load(ext, state)
    wide.propagate(state, held, 0)
    wide.store(ext, state, FACTOR)
    wide.take(ext, 2 * FACTOR, rows, put(advanced))
    wide.propagate(state, held, FACTOR)
    wide.store(ext, state, 2 * FACTOR)
    wide.take(ext, 2 * FACTOR, rows, put(pushed))


def pack_kernel(points, groups, *refs):
    following, pushed, (packed, difference) = refs[:points], refs[points:-2], refs[-2:]
    rows = difference.shape[2]
    share = rows // groups
    for k in range(points):
        difference[k] = pushed[k][...] - following[k][...]

    @pl.when(lax.axis_index("tm") == groups - 1)
    def _():
        first = following[points - 1]
        difference[points - 1] = first[...] - first[...]

    for g in range(groups):
        part = slice(g * share, (g + 1) * share)
        for k in range(points):
            for f in range(3):
                packed[(groups - 1 - g) * points + k, f, 0] = difference[k, f, part, :]


VMEM = pl.BlockSpec(memory_space=pltpu.VMEM)


def call(kernel, shapes, work, rows, columns, operands):
    chunks = columns // LANES
    extended = rows + 4 * FACTOR
    cost = pl.CostEstimate(
        flops=work * extended * columns * FACTOR * 45,
        bytes_accessed=4 * work * 3 * extended * columns,
        transcendentals=work * extended * columns * FACTOR,
    )
    return pl.pallas_call(
        functools.partial(kernel, chunks),
        out_shape=[jax.ShapeDtypeStruct(shape, jnp.float32) for shape in shapes],
        in_specs=[VMEM] * len(operands),
        out_specs=[VMEM] * len(shapes),
        scratch_shapes=[
            pltpu.VMEM((3, chunks, extended + SUB, LANES), jnp.float32),
            pltpu.VMEM((2, 3, extended // SUB, chunks, SUB, LANES), jnp.float32),
            pltpu.VMEM((3, chunks, SUB, LANES), jnp.float32),
        ],
        compiler_params=pltpu.CompilerParams(vmem_limit_bytes=24 * 2**20),
        cost_estimate=cost,
    )(*operands)


def chain(point, c_points, halo):
    _, fields, rows, columns = c_points.shape
    shape = (fields, rows, columns)
    return call(
        lambda chunks, *refs: chain_kernel(chunks, point, *refs),
        [shape, shape],
        2,
        rows,
        columns,
        (c_points, halo),
    )


def edges_of(block, width):
    return jnp.stack([block[..., -width:, :], block[..., :width, :]])


def route(shift, move):
    groups, strips = lax.axis_size("tm"), lax.axis_size("space")
    return [
        (t * strips + s, (t + shift) % groups * strips + (s + move) % strips)
        for t in range(groups)
        for s in range(strips)
    ]


def exchange(edges, shift):
    both = ("tm", "space")
    if lax.axis_size("space") == 2:
        return lax.ppermute(edges, both, route(shift, 1))
    return jnp.stack(
        [
            lax.ppermute(edges[0], both, route(shift, 1)),
            lax.ppermute(edges[1], both, route(shift, -1)),
        ]
    )


def pack(following, pushed, groups):
    points, (fields, rows, columns) = len(pushed), pushed[0].shape
    packet = (groups * points, fields, 1, rows // groups, columns)
    size = points * fields * rows * columns
    return pl.pallas_call(
        functools.partial(pack_kernel, points, groups),
        out_shape=jax.ShapeDtypeStruct(packet, jnp.float32),
        in_specs=[VMEM] * (2 * points),
        out_specs=VMEM,
        scratch_shapes=[pltpu.VMEM((points, fields, rows, columns), jnp.float32)],
        compiler_params=pltpu.CompilerParams(vmem_limit_bytes=24 * 2**20),
        cost_estimate=pl.CostEstimate(flops=size, bytes_accessed=12 * size, transcendentals=0),
    )(*following, *pushed)


def on_device(c_points):
    points = c_points.shape[0]
    groups = lax.axis_size("tm")
    halos = [exchange(edges_of(c_points[k], 2 * FACTOR), 0) for k in range(points)]
    advanced, pushed = zip(*[chain(k, c_points, halos[k]) for k in range(points)])
    next_first = lax.ppermute(advanced[0], ("tm", "space"), route(-1, 0))
    packed = pack([*advanced[1:], next_first], pushed, groups)
    members = [list(reversed(range(groups)))]
    coarse = lax.all_to_all(
        packed, "tm", split_axis=0, concat_axis=0, axis_index_groups=members, tiled=True
    )
    coarse = coarse.reshape(groups, points, *coarse.shape[1:])[::-1].reshape(coarse.shape)
    coarse = jnp.concatenate([coarse[-1:], coarse[:-1]], axis=0)
    incoming = lax.ppermute(advanced[-1], "tm", [(i, i + 1) for i in range(groups - 1)])
    opening = jnp.where(lax.axis_index("tm") == 0, c_points[0], incoming)
    return (jnp.stack([opening, *advanced[:-1]]), coarse)


def solution(mesh):
    in_specs = (P("tm", None, "space", None),)
    out_specs = (P("tm", None, "space", None), P(None, None, "space", "tm", None))
    return jax.shard_map(
        on_device, mesh=mesh, in_specs=in_specs, out_specs=out_specs, check_vma=False
    )
```

```python
import functools

import jax
import jax.numpy as jnp
from jax import lax
from jax.experimental import pallas as pl
from jax.experimental.pallas import tpu as pltpu
from jax.sharding import PartitionSpec as P

FACTOR = 8
LANES = 128
SUB = 8

MOMENTUM = 0.4
PRESSURE = 0.08


def reciprocal(x):
    r = pl.reciprocal(x, approx=True)
    return r * (2.0 - x * r)


def row_terms(read, chunks, factor, lane):
    north, south, east, west = [], [], [], []
    for c in range(chunks):
        h, p, q = read(0, c), read(1, c), read(2, c)
        r = reciprocal(h)
        u = p * r
        pressure = h * h * factor
        a = p * u + pressure
        b = q * u
        d = q * (q * r) + pressure
        east.append((h - p, p - a, q - b))
        west.append((h + p, p + a, q + b))
        north.append((h - q, p - b, q - d))
        south.append((h + q, p + b, q + d))
    level = []
    for c in range(chunks):
        after, before = (c + 1) % chunks, (c - 1) % chunks
        fields = []
        for f in range(3):
            e = jnp.where(lane == 0, east[after][f], east[c][f])
            w = jnp.where(lane == LANES - 1, west[before][f], west[c][f])
            fields.append(pltpu.roll(e, LANES - 1, 1) + pltpu.roll(w, 1, 1))
        level.append(tuple(fields))
    return north, south, level


def step(src, dst, held, first, depth, chunks, factor):
    lane = lax.broadcasted_iota(jnp.int32, (SUB, LANES), 1)
    cells = [(f, c) for f in range(3) for c in range(chunks)]
    partial = south_before = None
    for n in range(depth):
        i, before = (first + n) % depth, (first + n - 1) % depth
        north, south, level = row_terms(lambda f, c: src[f, i, c], chunks, factor, lane)
        if i == 0:
            wrapped = [tuple(pltpu.roll(t, SUB - 1, 0) for t in terms) for terms in north]
        else:
            wrapped = north
        for f, c in cells:
            if n == 0:
                held[f, c] = wrapped[c][f]
            else:
                dst[f, before, c] = partial[c][f] + wrapped[c][f]
        partial = level
        if n > 0:
            partial = [
                tuple(level[c][f] + south_before[c][f] for f in range(3)) for c in range(chunks)
            ]
        south_before = south
        if i == depth - 1:
            south_before = [tuple(pltpu.roll(t, 1, 0) for t in terms) for terms in south]
    last = (first - 1) % depth
    for f, c in cells:
        if depth == 1:
            dst[f, 0, c] = partial[c][f] + held[f, c] + south_before[c][f]
        else:
            dst[f, last, c] = partial[c][f] + held[f, c]
            dst[f, first, c] = dst[f, first, c] + south_before[c][f]


def spans(chunks):
    return [slice(c * LANES, (c + 1) * LANES) for c in range(chunks)]


class Rows:
    def __init__(self, count, chunks):
        self.depth, self.chunks = count // SUB, chunks
        self.pitch = self.depth | 1

    def cells(self):
        return [
            (f, c, i) for f in range(3) for c in range(self.chunks) for i in range(self.depth)
        ]

    def pieces(self, start, count):
        found, at = [], 0
        while at < count:
            block, offset = divmod(start + at, self.depth)
            length = min(count - at, self.depth - offset)
            found.append((at, block * self.pitch + offset, length))
            at += length
        return found

    def fill(self, ext, arrays):
        start = 0
        for array in arrays:
            rows = array.shape[1]
            for at, place, length in self.pieces(start, rows):
                for f in range(3):
                    for c, span in enumerate(spans(self.chunks)):
                        ext[f, c, place : place + length, :] = array[f, at : at + length, span]
            start += rows

    def load(self, ext, state):
        for f, c, i in self.cells():
            value = ext.at[f, c][pl.ds(i, SUB, stride=self.pitch), :]
            state[0, f, i, c] = value if f == 0 else MOMENTUM * value

    def store(self, ext, state, steps):
        shrink = 0.25**steps
        for f, c, i in self.cells():
            value = state[0, f, i, c] * (shrink if f == 0 else shrink / MOMENTUM)
            ext.at[f, c][pl.ds(i, SUB, stride=self.pitch), :] = value

    def propagate(self, state, held, steps):
        depth = self.depth

        def two(_, factor):
            step(state.at[0], state.at[1], held, 0, depth, self.chunks, factor)
            factor = factor * 0.25
            step(state.at[1], state.at[0], held, 1 % depth, depth, self.chunks, factor)
            return factor * 0.25

        lax.fori_loop(0, FACTOR // 2, two, jnp.float32(PRESSURE * 0.25**steps))

    def take(self, ext, start, count, use):
        for at, place, length in self.pieces(start, count):
            for f in range(3):
                for c, span in enumerate(spans(self.chunks)):
                    use(f, span, at, length, ext[f, c, place : place + length, :])


def put(target):
    def use(f, span, at, length, value):
        target[f, at : at + length, span] = value

    return use


def chain_kernel(chunks, point, own, halo, advanced, pushed, ext, state, held):
    rows = own.shape[2]
    wide = Rows(rows + 4 * FACTOR, chunks)
    wide.fill(ext, [halo.at[0], own.at[point], halo.at[1]])
    wide.load(ext, state)
    wide.propagate(state, held, 0)
    wide.store(ext, state, FACTOR)
    wide.take(ext, 2 * FACTOR, rows, put(advanced))
    wide.propagate(state, held, FACTOR)
    wide.store(ext, state, 2 * FACTOR)
    wide.take(ext, 2 * FACTOR, rows, put(pushed))


def head_kernel(chunks, point, own, halo, advanced, carried, ext, state, held):
    rows = own.shape[2]
    wide = Rows(rows + 4 * FACTOR, chunks)
    wide.fill(ext, [halo.at[0], own.at[point], halo.at[1]])
    wide.load(ext, state)
    wide.propagate(state, held, 0)
    wide.store(ext, state, FACTOR)
    wide.take(ext, 2 * FACTOR, rows, put(advanced))
    carried[...] = state[0]


def finish_kernel(chunks, carried, pushed, ext, state, held):
    rows = pushed.shape[1]
    wide = Rows(rows + 4 * FACTOR, chunks)
    state[0] = carried[...]
    wide.propagate(state, held, FACTOR)
    wide.store(ext, state, 2 * FACTOR)
    wide.take(ext, 2 * FACTOR, rows, put(pushed))


def pack_kernel(points, groups, *refs):
    following, pushed, (packed, difference) = refs[:points], refs[points:-2], refs[-2:]
    rows = difference.shape[2]
    share = rows // groups
    for k in range(points):
        difference[k] = pushed[k][...] - following[k][...]

    @pl.when(lax.axis_index("tm") == groups - 1)
    def _():
        first = following[points - 1]
        difference[points - 1] = first[...] - first[...]

    for g in range(groups):
        part = slice(g * share, (g + 1) * share)
        for k in range(points):
            for f in range(3):
                packed[(g - groups // 2) % groups * points + k, f, 0] = difference[k, f, part, :]


VMEM = pl.BlockSpec(memory_space=pltpu.VMEM)


def call(kernel, shapes, work, rows, columns, operands):
    chunks = columns // LANES
    extended = rows + 4 * FACTOR
    cost = pl.CostEstimate(
        flops=work * extended * columns * FACTOR * 45,
        bytes_accessed=4 * work * 3 * extended * columns,
        transcendentals=work * extended * columns * FACTOR,
    )
    return pl.pallas_call(
        functools.partial(kernel, chunks),
        out_shape=[jax.ShapeDtypeStruct(shape, jnp.float32) for shape in shapes],
        in_specs=[VMEM] * len(operands),
        out_specs=[VMEM] * len(shapes),
        scratch_shapes=[
            pltpu.VMEM((3, chunks, extended + SUB, LANES), jnp.float32),
            pltpu.VMEM((2, 3, extended // SUB, chunks, SUB, LANES), jnp.float32),
            pltpu.VMEM((3, chunks, SUB, LANES), jnp.float32),
        ],
        compiler_params=pltpu.CompilerParams(vmem_limit_bytes=24 * 2**20),
        cost_estimate=cost,
    )(*operands)


def chain(point, c_points, halo):
    _, fields, rows, columns = c_points.shape
    shape = (fields, rows, columns)
    return call(
        lambda chunks, *refs: chain_kernel(chunks, point, *refs),
        [shape, shape],
        2,
        rows,
        columns,
        (c_points, halo),
    )


def head(point, c_points, halo):
    _, fields, rows, columns = c_points.shape
    vectors = (fields, (rows + 4 * FACTOR) // SUB, columns // LANES, SUB, LANES)
    return call(
        lambda chunks, *refs: head_kernel(chunks, point, *refs),
        [(fields, rows, columns), vectors],
        1,
        rows,
        columns,
        (c_points, halo),
    )


def finish(carried, shape):
    _, rows, columns = shape
    return call(finish_kernel, [shape], 1, rows, columns, (carried,))[0]


def edges_of(block, width):
    return jnp.stack([block[..., -width:, :], block[..., :width, :]])


def route(shift, move):
    groups, strips = lax.axis_size("tm"), lax.axis_size("space")
    return [
        (t * strips + s, (t + shift) % groups * strips + (s + move) % strips)
        for t in range(groups)
        for s in range(strips)
    ]


def exchange(edges, shift):
    both = ("tm", "space")
    if lax.axis_size("space") == 2:
        return lax.ppermute(edges, both, route(shift, 1))
    return jnp.stack(
        [
            lax.ppermute(edges[0], both, route(shift, 1)),
            lax.ppermute(edges[1], both, route(shift, -1)),
        ]
    )


def pack(following, pushed, groups):
    points, (fields, rows, columns) = len(pushed), pushed[0].shape
    packet = (groups * points, fields, 1, rows // groups, columns)
    size = points * fields * rows * columns
    return pl.pallas_call(
        functools.partial(pack_kernel, points, groups),
        out_shape=jax.ShapeDtypeStruct(packet, jnp.float32),
        in_specs=[VMEM] * (2 * points),
        out_specs=VMEM,
        scratch_shapes=[pltpu.VMEM((points, fields, rows, columns), jnp.float32)],
        compiler_params=pltpu.CompilerParams(vmem_limit_bytes=24 * 2**20),
        cost_estimate=pl.CostEstimate(flops=size, bytes_accessed=12 * size, transcendentals=0),
    )(*following, *pushed)


def on_device(c_points):
    points = c_points.shape[0]
    groups = lax.axis_size("tm")
    halos = [exchange(edges_of(c_points[k], 2 * FACTOR), 0) for k in range(points)]
    first, carried = head(0, c_points, halos[0])
    ends = [(first, finish(carried, first.shape))]
    ends += [chain(k, c_points, halos[k]) for k in range(1, points)]
    advanced, pushed = zip(*ends)
    next_first = lax.ppermute(advanced[0], ("tm", "space"), route(-1, 0))
    packed = pack([*advanced[1:], next_first], pushed, groups)
    members = [[(groups // 2 + g) % groups for g in range(groups)]]
    coarse = lax.all_to_all(
        packed, "tm", split_axis=0, concat_axis=0, axis_index_groups=members, tiled=True
    )
    split = (groups - groups // 2) * points - 1
    coarse = jnp.concatenate([coarse[split:], coarse[:split]], axis=0)
    incoming = lax.ppermute(advanced[-1], "tm", [(i, i + 1) for i in range(groups - 1)])
    opening = jnp.where(lax.axis_index("tm") == 0, c_points[0], incoming)
    return (jnp.stack([opening, *advanced[:-1]]), coarse)


def solution(mesh):
    in_specs = (P("tm", None, "space", None),)
    out_specs = (P("tm", None, "space", None), P(None, None, "space", "tm", None))
    return jax.shard_map(
        on_device, mesh=mesh, in_specs=in_specs, out_specs=out_specs, check_vma=False
    )
```

```python
import functools

import jax
import jax.numpy as jnp
from jax import lax
from jax.experimental import pallas as pl
from jax.experimental.pallas import tpu as pltpu
from jax.sharding import PartitionSpec as P

FACTOR = 8
LANES = 128
SUB = 8

MOMENTUM = 0.4
PRESSURE = 0.08


def reciprocal(x):
    r = pl.reciprocal(x, approx=True)
    return r * (2.0 - x * r)


def row_terms(read, chunks, factor, lane):
    north, south, east, west = [], [], [], []
    for c in range(chunks):
        h, p, q = read(0, c), read(1, c), read(2, c)
        r = reciprocal(h)
        u = p * r
        pressure = h * h * factor
        a = p * u + pressure
        b = q * u
        d = q * (q * r) + pressure
        east.append((h - p, p - a, q - b))
        west.append((h + p, p + a, q + b))
        north.append((h - q, p - b, q - d))
        south.append((h + q, p + b, q + d))
    level = []
    for c in range(chunks):
        after, before = (c + 1) % chunks, (c - 1) % chunks
        fields = []
        for f in range(3):
            e = jnp.where(lane == 0, east[after][f], east[c][f])
            w = jnp.where(lane == LANES - 1, west[before][f], west[c][f])
            fields.append(pltpu.roll(e, LANES - 1, 1) + pltpu.roll(w, 1, 1))
        level.append(tuple(fields))
    return north, south, level


def step(src, dst, held, first, depth, chunks, factor):
    lane = lax.broadcasted_iota(jnp.int32, (SUB, LANES), 1)
    cells = [(f, c) for f in range(3) for c in range(chunks)]
    partial = south_before = None
    for n in range(depth):
        i, before = (first + n) % depth, (first + n - 1) % depth
        north, south, level = row_terms(lambda f, c: src[f, i, c], chunks, factor, lane)
        if i == 0:
            wrapped = [tuple(pltpu.roll(t, SUB - 1, 0) for t in terms) for terms in north]
        else:
            wrapped = north
        for f, c in cells:
            if n == 0:
                held[f, c] = wrapped[c][f]
            else:
                dst[f, before, c] = partial[c][f] + wrapped[c][f]
        partial = level
        if n > 0:
            partial = [
                tuple(level[c][f] + south_before[c][f] for f in range(3)) for c in range(chunks)
            ]
        south_before = south
        if i == depth - 1:
            south_before = [tuple(pltpu.roll(t, 1, 0) for t in terms) for terms in south]
    last = (first - 1) % depth
    for f, c in cells:
        if depth == 1:
            dst[f, 0, c] = partial[c][f] + held[f, c] + south_before[c][f]
        else:
            dst[f, last, c] = partial[c][f] + held[f, c]
            dst[f, first, c] = dst[f, first, c] + south_before[c][f]


def spans(chunks):
    return [slice(c * LANES, (c + 1) * LANES) for c in range(chunks)]


class Rows:
    def __init__(self, count, chunks):
        self.depth, self.chunks = count // SUB, chunks
        self.pitch = self.depth | 1

    def cells(self):
        return [
            (f, c, i) for f in range(3) for c in range(self.chunks) for i in range(self.depth)
        ]

    def pieces(self, start, count):
        found, at = [], 0
        while at < count:
            block, offset = divmod(start + at, self.depth)
            length = min(count - at, self.depth - offset)
            found.append((at, block * self.pitch + offset, length))
            at += length
        return found

    def fill(self, ext, arrays):
        start = 0
        for array in arrays:
            rows = array.shape[1]
            for at, place, length in self.pieces(start, rows):
                for f in range(3):
                    for c, span in enumerate(spans(self.chunks)):
                        ext[f, c, place : place + length, :] = array[f, at : at + length, span]
            start += rows

    def load(self, ext, state):
        for f, c, i in self.cells():
            value = ext.at[f, c][pl.ds(i, SUB, stride=self.pitch), :]
            state[0, f, i, c] = value if f == 0 else MOMENTUM * value

    def store(self, ext, state, steps):
        shrink = 0.25**steps
        for f, c, i in self.cells():
            value = state[0, f, i, c] * (shrink if f == 0 else shrink / MOMENTUM)
            ext.at[f, c][pl.ds(i, SUB, stride=self.pitch), :] = value

    def propagate(self, state, held, steps):
        depth = self.depth

        def two(_, factor):
            step(state.at[0], state.at[1], held, 0, depth, self.chunks, factor)
            factor = factor * 0.25
            step(state.at[1], state.at[0], held, 1 % depth, depth, self.chunks, factor)
            return factor * 0.25

        lax.fori_loop(0, FACTOR // 2, two, jnp.float32(PRESSURE * 0.25**steps))

    def take(self, ext, start, count, use):
        for at, place, length in self.pieces(start, count):
            for f in range(3):
                for c, span in enumerate(spans(self.chunks)):
                    use(f, span, at, length, ext[f, c, place : place + length, :])


def put(target):
    def use(f, span, at, length, value):
        target[f, at : at + length, span] = value

    return use


def chain_kernel(chunks, point, own, halo, advanced, pushed, ext, state, held):
    rows = own.shape[2]
    wide = Rows(rows + 4 * FACTOR, chunks)
    wide.fill(ext, [halo.at[0], own.at[point], halo.at[1]])
    wide.load(ext, state)
    wide.propagate(state, held, 0)
    wide.store(ext, state, FACTOR)
    wide.take(ext, 2 * FACTOR, rows, put(advanced))
    wide.propagate(state, held, FACTOR)
    wide.store(ext, state, 2 * FACTOR)
    wide.take(ext, 2 * FACTOR, rows, put(pushed))


def cut_kernel(points, own, *refs):
    outs, sems = refs[:-1], refs[-1]
    rows, width = own.shape[2], 2 * FACTOR
    copies = []
    for k in range(points):
        for side, start in enumerate((rows - width, 0)):
            part = own.at[k, :, pl.ds(start, width), :]
            copies.append(pltpu.make_async_copy(part, outs[k].at[side], sems.at[k, side]))
    for copy in copies:
        copy.start()
    for copy in copies:
        copy.wait()


def head_kernel(chunks, point, own, halo, advanced, carried, ext, state, held):
    rows = own.shape[2]
    wide = Rows(rows + 4 * FACTOR, chunks)
    wide.fill(ext, [halo.at[0], own.at[point], halo.at[1]])
    wide.load(ext, state)
    wide.propagate(state, held, 0)
    wide.store(ext, state, FACTOR)
    wide.take(ext, 2 * FACTOR, rows, put(advanced))
    carried[...] = state[0]


def finish_kernel(chunks, carried, pushed, ext, state, held):
    rows = pushed.shape[1]
    wide = Rows(rows + 4 * FACTOR, chunks)
    state[0] = carried[...]
    wide.propagate(state, held, FACTOR)
    wide.store(ext, state, 2 * FACTOR)
    wide.take(ext, 2 * FACTOR, rows, put(pushed))


def pack_kernel(points, groups, *refs):
    following, pushed, (packed, difference) = refs[:points], refs[points:-2], refs[-2:]
    rows = difference.shape[2]
    share = rows // groups
    for k in range(points):
        difference[k] = pushed[k][...] - following[k][...]

    @pl.when(lax.axis_index("tm") == groups - 1)
    def _():
        first = following[points - 1]
        difference[points - 1] = first[...] - first[...]

    for g in range(groups):
        part = slice(g * share, (g + 1) * share)
        for k in range(points):
            for f in range(3):
                packed[(g - groups // 2) % groups * points + k, f, 0] = difference[k, f, part, :]


VMEM = pl.BlockSpec(memory_space=pltpu.VMEM)


def call(kernel, shapes, work, rows, columns, operands):
    chunks = columns // LANES
    extended = rows + 4 * FACTOR
    cost = pl.CostEstimate(
        flops=work * extended * columns * FACTOR * 45,
        bytes_accessed=4 * work * 3 * extended * columns,
        transcendentals=work * extended * columns * FACTOR,
    )
    return pl.pallas_call(
        functools.partial(kernel, chunks),
        out_shape=[jax.ShapeDtypeStruct(shape, jnp.float32) for shape in shapes],
        in_specs=[VMEM] * len(operands),
        out_specs=[VMEM] * len(shapes),
        scratch_shapes=[
            pltpu.VMEM((3, chunks, extended + SUB, LANES), jnp.float32),
            pltpu.VMEM((2, 3, extended // SUB, chunks, SUB, LANES), jnp.float32),
            pltpu.VMEM((3, chunks, SUB, LANES), jnp.float32),
        ],
        compiler_params=pltpu.CompilerParams(vmem_limit_bytes=24 * 2**20),
        cost_estimate=cost,
    )(*operands)


def chain(point, c_points, halo):
    _, fields, rows, columns = c_points.shape
    shape = (fields, rows, columns)
    return call(
        lambda chunks, *refs: chain_kernel(chunks, point, *refs),
        [shape, shape],
        2,
        rows,
        columns,
        (c_points, halo),
    )


def head(point, c_points, halo):
    _, fields, rows, columns = c_points.shape
    vectors = (fields, (rows + 4 * FACTOR) // SUB, columns // LANES, SUB, LANES)
    return call(
        lambda chunks, *refs: head_kernel(chunks, point, *refs),
        [(fields, rows, columns), vectors],
        1,
        rows,
        columns,
        (c_points, halo),
    )


def finish(carried, shape):
    _, rows, columns = shape
    return call(finish_kernel, [shape], 1, rows, columns, (carried,))[0]


def cut(c_points):
    points, fields, _, columns = c_points.shape
    edges = jax.ShapeDtypeStruct((2, fields, 2 * FACTOR, columns), jnp.float32)
    return pl.pallas_call(
        functools.partial(cut_kernel, points),
        out_shape=[edges] * points,
        in_specs=[pl.BlockSpec(memory_space=pltpu.HBM)],
        out_specs=[VMEM] * points,
        scratch_shapes=[pltpu.SemaphoreType.DMA((points, 2))],
    )(c_points)


def route(shift, move):
    groups, strips = lax.axis_size("tm"), lax.axis_size("space")
    return [
        (t * strips + s, (t + shift) % groups * strips + (s + move) % strips)
        for t in range(groups)
        for s in range(strips)
    ]


def exchange(edges, shift):
    both = ("tm", "space")
    if lax.axis_size("space") == 2:
        return lax.ppermute(edges, both, route(shift, 1))
    return jnp.stack(
        [
            lax.ppermute(edges[0], both, route(shift, 1)),
            lax.ppermute(edges[1], both, route(shift, -1)),
        ]
    )


def pack(following, pushed, groups):
    points, (fields, rows, columns) = len(pushed), pushed[0].shape
    packet = (groups * points, fields, 1, rows // groups, columns)
    size = points * fields * rows * columns
    return pl.pallas_call(
        functools.partial(pack_kernel, points, groups),
        out_shape=jax.ShapeDtypeStruct(packet, jnp.float32),
        in_specs=[VMEM] * (2 * points),
        out_specs=VMEM,
        scratch_shapes=[pltpu.VMEM((points, fields, rows, columns), jnp.float32)],
        compiler_params=pltpu.CompilerParams(vmem_limit_bytes=24 * 2**20),
        cost_estimate=pl.CostEstimate(flops=size, bytes_accessed=12 * size, transcendentals=0),
    )(*following, *pushed)


def on_device(c_points):
    points = c_points.shape[0]
    groups = lax.axis_size("tm")
    halos = [exchange(edges, 0) for edges in cut(c_points)]
    first, carried = head(0, c_points, halos[0])
    ends = [(first, finish(carried, first.shape))]
    ends += [chain(k, c_points, halos[k]) for k in range(1, points)]
    advanced, pushed = zip(*ends)
    next_first = lax.ppermute(advanced[0], ("tm", "space"), route(-1, 0))
    packed = pack([*advanced[1:], next_first], pushed, groups)
    members = [[(groups // 2 + g) % groups for g in range(groups)]]
    coarse = lax.all_to_all(
        packed, "tm", split_axis=0, concat_axis=0, axis_index_groups=members, tiled=True
    )
    split = (groups - groups // 2) * points - 1
    coarse = jnp.concatenate([coarse[split:], coarse[:split]], axis=0)
    incoming = lax.ppermute(advanced[-1], "tm", [(i, i + 1) for i in range(groups - 1)])
    coarse, incoming = lax.optimization_barrier((coarse, incoming))
    opening = jnp.where(lax.axis_index("tm") == 0, c_points[0], incoming)
    return (jnp.stack([opening, *advanced[:-1]]), coarse)


def solution(mesh):
    in_specs = (P("tm", None, "space", None),)
    out_specs = (P("tm", None, "space", None), P(None, None, "space", "tm", None))
    return jax.shard_map(
        on_device, mesh=mesh, in_specs=in_specs, out_specs=out_specs, check_vma=False
    )
```

```python
import functools

import jax
import jax.numpy as jnp
from jax import lax
from jax.experimental import pallas as pl
from jax.experimental.pallas import tpu as pltpu
from jax.sharding import PartitionSpec as P

FACTOR = 8
LANES = 128
SUB = 8

MOMENTUM = 0.4
PRESSURE = 0.08


def reciprocal(x):
    r = pl.reciprocal(x, approx=True)
    return r * (2.0 - x * r)


def row_terms(read, chunks, factor, lane):
    north, south, east, west = [], [], [], []
    for c in range(chunks):
        h, p, q = read(0, c), read(1, c), read(2, c)
        r = reciprocal(h)
        u = p * r
        pressure = h * h * factor
        a = p * u + pressure
        b = q * u
        d = q * (q * r) + pressure
        east.append((h - p, p - a, q - b))
        west.append((h + p, p + a, q + b))
        north.append((h - q, p - b, q - d))
        south.append((h + q, p + b, q + d))
    level = []
    for c in range(chunks):
        after, before = (c + 1) % chunks, (c - 1) % chunks
        fields = []
        for f in range(3):
            e = jnp.where(lane == 0, east[after][f], east[c][f])
            w = jnp.where(lane == LANES - 1, west[before][f], west[c][f])
            fields.append(pltpu.roll(e, LANES - 1, 1) + pltpu.roll(w, 1, 1))
        level.append(tuple(fields))
    return north, south, level


def step(src, dst, held, first, depth, chunks, factor):
    lane = lax.broadcasted_iota(jnp.int32, (SUB, LANES), 1)
    cells = [(f, c) for f in range(3) for c in range(chunks)]
    partial = south_before = None
    for n in range(depth):
        i, before = (first + n) % depth, (first + n - 1) % depth
        north, south, level = row_terms(lambda f, c: src[f, i, c], chunks, factor, lane)
        if i == 0:
            wrapped = [tuple(pltpu.roll(t, SUB - 1, 0) for t in terms) for terms in north]
        else:
            wrapped = north
        for f, c in cells:
            if n == 0:
                held[f, c] = wrapped[c][f]
            else:
                dst[f, before, c] = partial[c][f] + wrapped[c][f]
        partial = level
        if n > 0:
            partial = [
                tuple(level[c][f] + south_before[c][f] for f in range(3)) for c in range(chunks)
            ]
        south_before = south
        if i == depth - 1:
            south_before = [tuple(pltpu.roll(t, 1, 0) for t in terms) for terms in south]
    last = (first - 1) % depth
    for f, c in cells:
        if depth == 1:
            dst[f, 0, c] = partial[c][f] + held[f, c] + south_before[c][f]
        else:
            dst[f, last, c] = partial[c][f] + held[f, c]
            dst[f, first, c] = dst[f, first, c] + south_before[c][f]


def spans(chunks):
    return [slice(c * LANES, (c + 1) * LANES) for c in range(chunks)]


class Rows:
    def __init__(self, count, chunks):
        self.depth, self.chunks = count // SUB, chunks
        self.pitch = self.depth | 1

    def cells(self):
        return [
            (f, c, i) for f in range(3) for c in range(self.chunks) for i in range(self.depth)
        ]

    def pieces(self, start, count):
        found, at = [], 0
        while at < count:
            block, offset = divmod(start + at, self.depth)
            length = min(count - at, self.depth - offset)
            found.append((at, block * self.pitch + offset, length))
            at += length
        return found

    def fill(self, ext, arrays):
        start = 0
        for array in arrays:
            rows = array.shape[1]
            for at, place, length in self.pieces(start, rows):
                for f in range(3):
                    for c, span in enumerate(spans(self.chunks)):
                        ext[f, c, place : place + length, :] = array[f, at : at + length, span]
            start += rows

    def load(self, ext, state):
        for f, c, i in self.cells():
            value = ext.at[f, c][pl.ds(i, SUB, stride=self.pitch), :]
            state[0, f, i, c] = value if f == 0 else MOMENTUM * value

    def store(self, ext, state):
        shrink = 0.25**FACTOR
        for f, c, i in self.cells():
            value = state[0, f, i, c] * (shrink if f == 0 else shrink / MOMENTUM)
            ext.at[f, c][pl.ds(i, SUB, stride=self.pitch), :] = value

    def propagate(self, state, held):
        depth = self.depth

        def two(_, factor):
            step(state.at[0], state.at[1], held, 0, depth, self.chunks, factor)
            factor = factor * 0.25
            step(state.at[1], state.at[0], held, 1 % depth, depth, self.chunks, factor)
            return factor * 0.25

        lax.fori_loop(0, FACTOR // 2, two, jnp.float32(PRESSURE))

    def take(self, ext, start, count, use):
        for at, place, length in self.pieces(start, count):
            for f in range(3):
                for c, span in enumerate(spans(self.chunks)):
                    use(f, span, at, length, ext[f, c, place : place + length, :])


def put(target):
    def use(f, span, at, length, value):
        target[f, at : at + length, span] = value

    return use


def first_half(chunks, block, halo, middle, ext, state, held):
    rows = block.shape[1]
    wide = Rows(rows + 4 * FACTOR, chunks)
    wide.fill(ext, [halo.at[0], block, halo.at[1]])
    wide.load(ext, state)
    wide.propagate(state, held)
    wide.store(ext, state)
    wide.take(ext, FACTOR, rows + 2 * FACTOR, put(middle))


def second_half(chunks, middle, pushed, ext, state, held):
    rows = pushed.shape[1]
    narrow = Rows(rows + 2 * FACTOR, chunks)
    narrow.fill(ext, [middle])
    narrow.load(ext, state)
    narrow.propagate(state, held)
    narrow.store(ext, state)
    narrow.take(ext, FACTOR, rows, put(pushed))


def chain_kernel(chunks, point, own, halo, advanced, pushed, middle, *scratch):
    first_half(chunks, own.at[point], halo, middle, *scratch)
    advanced[...] = middle[:, FACTOR : FACTOR + own.shape[2], :]
    second_half(chunks, middle, pushed, *scratch)


def head_kernel(chunks, point, own, halo, advanced, middle, *scratch):
    first_half(chunks, own.at[point], halo, middle, *scratch)
    advanced[...] = middle[:, FACTOR : FACTOR + own.shape[2], :]


def finish_kernel(chunks, middle, pushed, *scratch):
    second_half(chunks, middle, pushed, *scratch)


def pack_kernel(points, groups, *refs):
    following, pushed, (packed, difference) = refs[:points], refs[points:-2], refs[-2:]
    rows = difference.shape[2]
    share = rows // groups
    for k in range(points):
        difference[k] = pushed[k][...] - following[k][...]

    @pl.when(lax.axis_index("tm") == groups - 1)
    def _():
        first = following[points - 1]
        difference[points - 1] = first[...] - first[...]

    for g in range(groups):
        part = slice(g * share, (g + 1) * share)
        for k in range(points):
            for f in range(3):
                packed[(g - groups // 2) % groups * points + k, f, 0] = difference[k, f, part, :]


VMEM = pl.BlockSpec(memory_space=pltpu.VMEM)


def call(kernel, shapes, work, rows, columns, operands, extra=()):
    chunks = columns // LANES
    extended = rows + 4 * FACTOR
    cost = pl.CostEstimate(
        flops=work * extended * columns * FACTOR * 45,
        bytes_accessed=4 * work * 3 * extended * columns,
        transcendentals=work * extended * columns * FACTOR,
    )
    return pl.pallas_call(
        functools.partial(kernel, chunks),
        out_shape=[jax.ShapeDtypeStruct(shape, jnp.float32) for shape in shapes],
        in_specs=[VMEM] * len(operands),
        out_specs=[VMEM] * len(shapes),
        scratch_shapes=[
            *extra,
            pltpu.VMEM((3, chunks, extended + SUB, LANES), jnp.float32),
            pltpu.VMEM((2, 3, extended // SUB, chunks, SUB, LANES), jnp.float32),
            pltpu.VMEM((3, chunks, SUB, LANES), jnp.float32),
        ],
        compiler_params=pltpu.CompilerParams(vmem_limit_bytes=24 * 2**20),
        cost_estimate=cost,
    )(*operands)


def chain(point, c_points, halo):
    _, fields, rows, columns = c_points.shape
    return call(
        lambda chunks, *refs: chain_kernel(chunks, point, *refs),
        [(fields, rows, columns)] * 2,
        2,
        rows,
        columns,
        (c_points, halo),
        extra=[pltpu.VMEM((fields, rows + 2 * FACTOR, columns), jnp.float32)],
    )


def head(point, c_points, halo):
    _, fields, rows, columns = c_points.shape
    return call(
        lambda chunks, *refs: head_kernel(chunks, point, *refs),
        [(fields, rows, columns), (fields, rows + 2 * FACTOR, columns)],
        1,
        rows,
        columns,
        (c_points, halo),
    )


def finish(middle, shape):
    _, rows, columns = shape
    return call(finish_kernel, [shape], 1, rows, columns, (middle,))[0]


def edges_of(block, width):
    return jnp.stack([block[..., -width:, :], block[..., :width, :]])


def route(shift, move):
    groups, strips = lax.axis_size("tm"), lax.axis_size("space")
    return [
        (t * strips + s, (t + shift) % groups * strips + (s + move) % strips)
        for t in range(groups)
        for s in range(strips)
    ]


def exchange(edges, shift):
    both = ("tm", "space")
    if lax.axis_size("space") == 2:
        return lax.ppermute(edges, both, route(shift, 1))
    return jnp.stack(
        [
            lax.ppermute(edges[0], both, route(shift, 1)),
            lax.ppermute(edges[1], both, route(shift, -1)),
        ]
    )


def pack(following, pushed, groups):
    points, (fields, rows, columns) = len(pushed), pushed[0].shape
    packet = (groups * points, fields, 1, rows // groups, columns)
    size = points * fields * rows * columns
    return pl.pallas_call(
        functools.partial(pack_kernel, points, groups),
        out_shape=jax.ShapeDtypeStruct(packet, jnp.float32),
        in_specs=[VMEM] * (2 * points),
        out_specs=VMEM,
        scratch_shapes=[pltpu.VMEM((points, fields, rows, columns), jnp.float32)],
        compiler_params=pltpu.CompilerParams(vmem_limit_bytes=24 * 2**20),
        cost_estimate=pl.CostEstimate(flops=size, bytes_accessed=12 * size, transcendentals=0),
    )(*following, *pushed)


def on_device(c_points):
    points = c_points.shape[0]
    groups = lax.axis_size("tm")
    halos = [exchange(edges_of(c_points[k], 2 * FACTOR), 0) for k in range(points)]
    first, middle = head(0, c_points, halos[0])
    ends = [(first, finish(middle, first.shape))]
    ends += [chain(k, c_points, halos[k]) for k in range(1, points)]
    advanced, pushed = zip(*ends)
    next_first = lax.ppermute(advanced[0], ("tm", "space"), route(-1, 0))
    packed = pack([*advanced[1:], next_first], pushed, groups)
    members = [[(groups // 2 + g) % groups for g in range(groups)]]
    coarse = lax.all_to_all(
        packed, "tm", split_axis=0, concat_axis=0, axis_index_groups=members, tiled=True
    )
    split = (groups - groups // 2) * points - 1
    coarse = jnp.concatenate([coarse[split:], coarse[:split]], axis=0)
    incoming = lax.ppermute(advanced[-1], "tm", [(i, i + 1) for i in range(groups - 1)])
    coarse, incoming = lax.optimization_barrier((coarse, incoming))
    opening = jnp.where(lax.axis_index("tm") == 0, c_points[0], incoming)
    return (jnp.stack([opening, *advanced[:-1]]), coarse)


def solution(mesh):
    in_specs = (P("tm", None, "space", None),)
    out_specs = (P("tm", None, "space", None), P(None, None, "space", "tm", None))
    return jax.shard_map(
        on_device, mesh=mesh, in_specs=in_specs, out_specs=out_specs, check_vma=False
    )
```

```python
import functools

import jax
import jax.numpy as jnp
from jax import lax
from jax.experimental import pallas as pl
from jax.experimental.pallas import tpu as pltpu
from jax.sharding import PartitionSpec as P

FACTOR = 8
LANES = 128
SUB = 8

MOMENTUM = 0.4
PRESSURE = 0.08


def reciprocal(x):
    r = pl.reciprocal(x, approx=True)
    return r * (2.0 - x * r)


def row_terms(read, chunks, factor, lane):
    north, south, east, west = [], [], [], []
    for c in range(chunks):
        h, p, q = read(0, c), read(1, c), read(2, c)
        r = reciprocal(h)
        u = p * r
        pressure = h * h * factor
        a = p * u + pressure
        b = q * u
        d = q * (q * r) + pressure
        east.append((h - p, p - a, q - b))
        west.append((h + p, p + a, q + b))
        north.append((h - q, p - b, q - d))
        south.append((h + q, p + b, q + d))
    level = []
    for c in range(chunks):
        after, before = (c + 1) % chunks, (c - 1) % chunks
        fields = []
        for f in range(3):
            e = jnp.where(lane == 0, east[after][f], east[c][f])
            w = jnp.where(lane == LANES - 1, west[before][f], west[c][f])
            fields.append(pltpu.roll(e, LANES - 1, 1) + pltpu.roll(w, 1, 1))
        level.append(tuple(fields))
    return north, south, level


def step(src, dst, held, first, depth, chunks, factor):
    lane = lax.broadcasted_iota(jnp.int32, (SUB, LANES), 1)
    cells = [(f, c) for f in range(3) for c in range(chunks)]
    partial = south_before = None
    for n in range(depth):
        i, before = (first + n) % depth, (first + n - 1) % depth
        north, south, level = row_terms(lambda f, c: src[f, i, c], chunks, factor, lane)
        if i == 0:
            wrapped = [tuple(pltpu.roll(t, SUB - 1, 0) for t in terms) for terms in north]
        else:
            wrapped = north
        for f, c in cells:
            if n == 0:
                held[f, c] = wrapped[c][f]
            else:
                dst[f, before, c] = partial[c][f] + wrapped[c][f]
        partial = level
        if n > 0:
            partial = [
                tuple(level[c][f] + south_before[c][f] for f in range(3)) for c in range(chunks)
            ]
        south_before = south
        if i == depth - 1:
            south_before = [tuple(pltpu.roll(t, 1, 0) for t in terms) for terms in south]
    last = (first - 1) % depth
    for f, c in cells:
        if depth == 1:
            dst[f, 0, c] = partial[c][f] + held[f, c] + south_before[c][f]
        else:
            dst[f, last, c] = partial[c][f] + held[f, c]
            dst[f, first, c] = dst[f, first, c] + south_before[c][f]


def spans(chunks):
    return [slice(c * LANES, (c + 1) * LANES) for c in range(chunks)]


class Rows:
    def __init__(self, count, chunks):
        self.depth, self.chunks = count // SUB, chunks
        self.pitch = self.depth | 1

    def cells(self):
        return [
            (f, c, i) for f in range(3) for c in range(self.chunks) for i in range(self.depth)
        ]

    def pieces(self, start, count):
        found, at = [], 0
        while at < count:
            block, offset = divmod(start + at, self.depth)
            length = min(count - at, self.depth - offset)
            found.append((at, block * self.pitch + offset, length))
            at += length
        return found

    def fill(self, ext, arrays):
        start = 0
        for array in arrays:
            rows = array.shape[1]
            for at, place, length in self.pieces(start, rows):
                for f in range(3):
                    for c, span in enumerate(spans(self.chunks)):
                        ext[f, c, place : place + length, :] = array[f, at : at + length, span]
            start += rows

    def load(self, ext, state):
        for f, c, i in self.cells():
            value = ext.at[f, c][pl.ds(i, SUB, stride=self.pitch), :]
            state[0, f, i, c] = value if f == 0 else MOMENTUM * value

    def store(self, ext, state):
        shrink = 0.25**FACTOR
        for f, c, i in self.cells():
            value = state[0, f, i, c] * (shrink if f == 0 else shrink / MOMENTUM)
            ext.at[f, c][pl.ds(i, SUB, stride=self.pitch), :] = value

    def propagate(self, state, held):
        depth = self.depth

        def two(_, factor):
            step(state.at[0], state.at[1], held, 0, depth, self.chunks, factor)
            factor = factor * 0.25
            step(state.at[1], state.at[0], held, 1 % depth, depth, self.chunks, factor)
            return factor * 0.25

        lax.fori_loop(0, FACTOR // 2, two, jnp.float32(PRESSURE))

    def take(self, ext, start, count, use):
        for at, place, length in self.pieces(start, count):
            for f in range(3):
                for c, span in enumerate(spans(self.chunks)):
                    use(f, span, at, length, ext[f, c, place : place + length, :])


def put(target):
    def use(f, span, at, length, value):
        target[f, at : at + length, span] = value

    return use


def first_half(chunks, block, halo, middle, ext, state, held):
    rows = block.shape[1]
    wide = Rows(rows + 4 * FACTOR, chunks)
    wide.fill(ext, [halo.at[0], block, halo.at[1]])
    wide.load(ext, state)
    wide.propagate(state, held)
    wide.store(ext, state)
    wide.take(ext, FACTOR, rows + 2 * FACTOR, put(middle))


def second_half(chunks, middle, pushed, ext, state, held):
    rows = pushed.shape[1]
    narrow = Rows(rows + 2 * FACTOR, chunks)
    narrow.fill(ext, [middle])
    narrow.load(ext, state)
    narrow.propagate(state, held)
    narrow.store(ext, state)
    narrow.take(ext, FACTOR, rows, put(pushed))


def chain_kernel(chunks, point, own, halo, advanced, pushed, middle, *scratch):
    first_half(chunks, own.at[point], halo, middle, *scratch)
    advanced[...] = middle[:, FACTOR : FACTOR + own.shape[2], :]
    second_half(chunks, middle, pushed, *scratch)


def head_kernel(chunks, point, own, halo, advanced, middle, *scratch):
    first_half(chunks, own.at[point], halo, middle, *scratch)
    advanced[...] = middle[:, FACTOR : FACTOR + own.shape[2], :]


def finish_kernel(chunks, middle, pushed, *scratch):
    second_half(chunks, middle, pushed, *scratch)


def half_kernel(chunks, block, halo, advanced, *scratch):
    rows = block.shape[1]
    narrow = Rows(rows + 2 * FACTOR, chunks)
    narrow.fill(scratch[0], [halo.at[0], block, halo.at[1]])
    narrow.load(*scratch[:2])
    narrow.propagate(*scratch[1:])
    narrow.store(*scratch[:2])
    narrow.take(scratch[0], FACTOR, rows, put(advanced))


def pack_kernel(points, groups, *refs):
    following, pushed, (packed, difference) = refs[:points], refs[points:-2], refs[-2:]
    rows = difference.shape[2]
    share = rows // groups
    for k in range(points):
        difference[k] = pushed[k][...] - following[k][...]

    @pl.when(lax.axis_index("tm") == groups - 1)
    def _():
        first = following[points - 1]
        difference[points - 1] = first[...] - first[...]

    for g in range(groups):
        part = slice(g * share, (g + 1) * share)
        for k in range(points):
            for f in range(3):
                packed[(g - groups // 2) % groups * points + k, f, 0] = difference[k, f, part, :]


VMEM = pl.BlockSpec(memory_space=pltpu.VMEM)


def call(kernel, shapes, work, rows, columns, operands, extra=()):
    chunks = columns // LANES
    extended = rows + 4 * FACTOR
    cost = pl.CostEstimate(
        flops=work * extended * columns * FACTOR * 45,
        bytes_accessed=4 * work * 3 * extended * columns,
        transcendentals=work * extended * columns * FACTOR,
    )
    return pl.pallas_call(
        functools.partial(kernel, chunks),
        out_shape=[jax.ShapeDtypeStruct(shape, jnp.float32) for shape in shapes],
        in_specs=[VMEM] * len(operands),
        out_specs=[VMEM] * len(shapes),
        scratch_shapes=[
            *extra,
            pltpu.VMEM((3, chunks, extended + SUB, LANES), jnp.float32),
            pltpu.VMEM((2, 3, extended // SUB, chunks, SUB, LANES), jnp.float32),
            pltpu.VMEM((3, chunks, SUB, LANES), jnp.float32),
        ],
        compiler_params=pltpu.CompilerParams(vmem_limit_bytes=24 * 2**20),
        cost_estimate=cost,
    )(*operands)


def chain(point, c_points, halo):
    _, fields, rows, columns = c_points.shape
    return call(
        lambda chunks, *refs: chain_kernel(chunks, point, *refs),
        [(fields, rows, columns)] * 2,
        2,
        rows,
        columns,
        (c_points, halo),
        extra=[pltpu.VMEM((fields, rows + 2 * FACTOR, columns), jnp.float32)],
    )


def head(point, c_points, halo):
    _, fields, rows, columns = c_points.shape
    return call(
        lambda chunks, *refs: head_kernel(chunks, point, *refs),
        [(fields, rows, columns), (fields, rows + 2 * FACTOR, columns)],
        1,
        rows,
        columns,
        (c_points, halo),
    )


def finish(middle, shape):
    _, rows, columns = shape
    return call(finish_kernel, [shape], 1, rows, columns, (middle,))[0]


def half(block, halo):
    return call(half_kernel, [block.shape], 1, *block.shape[1:], (block, halo))[0]


def edges_of(block, width):
    return jnp.stack([block[..., -width:, :], block[..., :width, :]])


def route(shift, move):
    groups, strips = lax.axis_size("tm"), lax.axis_size("space")
    return [
        (t * strips + s, (t + shift) % groups * strips + (s + move) % strips)
        for t in range(groups)
        for s in range(strips)
    ]


def exchange(edges, shift):
    both = ("tm", "space")
    if lax.axis_size("space") == 2:
        return lax.ppermute(edges, both, route(shift, 1))
    return jnp.stack(
        [
            lax.ppermute(edges[0], both, route(shift, 1)),
            lax.ppermute(edges[1], both, route(shift, -1)),
        ]
    )


def pack(following, pushed, groups):
    points, (fields, rows, columns) = len(pushed), pushed[0].shape
    packet = (groups * points, fields, 1, rows // groups, columns)
    size = points * fields * rows * columns
    return pl.pallas_call(
        functools.partial(pack_kernel, points, groups),
        out_shape=jax.ShapeDtypeStruct(packet, jnp.float32),
        in_specs=[VMEM] * (2 * points),
        out_specs=VMEM,
        scratch_shapes=[pltpu.VMEM((points, fields, rows, columns), jnp.float32)],
        compiler_params=pltpu.CompilerParams(vmem_limit_bytes=24 * 2**20),
        cost_estimate=pl.CostEstimate(flops=size, bytes_accessed=12 * size, transcendentals=0),
    )(*following, *pushed)


def on_device(c_points):
    points = c_points.shape[0]
    groups = lax.axis_size("tm")
    halos = [exchange(edges_of(c_points[k], 2 * FACTOR), 0) for k in range(points)]
    behind = lax.ppermute(c_points[-1], "tm", [(i, i + 1) for i in range(groups - 1)])
    halos[0], behind = lax.optimization_barrier((halos[0], behind))
    behind_halo = exchange(edges_of(behind, FACTOR), 0)
    first, middle = head(0, c_points, halos[0])
    ends = [(first, finish(middle, first.shape))]
    ends += [chain(k, c_points, halos[k]) for k in range(1, points)]
    advanced, pushed = zip(*ends)
    next_first = lax.ppermute(advanced[0], ("tm", "space"), route(-1, 0))
    next_first, behind_halo = lax.optimization_barrier((next_first, behind_halo))
    packed = pack([*advanced[1:], next_first], pushed, groups)
    members = [[(groups // 2 + g) % groups for g in range(groups)]]
    coarse = lax.all_to_all(
        packed, "tm", split_axis=0, concat_axis=0, axis_index_groups=members, tiled=True
    )
    split = (groups - groups // 2) * points - 1
    coarse = jnp.concatenate([coarse[split:], coarse[:split]], axis=0)
    behind, behind_halo, _ = lax.optimization_barrier((behind, behind_halo, packed))
    opening = jnp.where(lax.axis_index("tm") == 0, c_points[0], half(behind, behind_halo))
    return (jnp.stack([opening, *advanced[:-1]]), coarse)


def solution(mesh):
    in_specs = (P("tm", None, "space", None),)
    out_specs = (P("tm", None, "space", None), P(None, None, "space", "tm", None))
    return jax.shard_map(
        on_device, mesh=mesh, in_specs=in_specs, out_specs=out_specs, check_vma=False
    )
```

```python
import functools

import jax
import jax.numpy as jnp
from jax import lax
from jax.experimental import pallas as pl
from jax.experimental.pallas import tpu as pltpu
from jax.sharding import PartitionSpec as P

FACTOR = 8
LANES = 128
SUB = 8

MOMENTUM = 0.4
PRESSURE = 0.08


def reciprocal(x):
    r = pl.reciprocal(x, approx=True)
    return r * (2.0 - x * r)


def row_terms(read, chunks, factor, lane):
    north, south, east, west = [], [], [], []
    for c in range(chunks):
        h, p, q = read(0, c), read(1, c), read(2, c)
        r = reciprocal(h)
        u = p * r
        pressure = h * h * factor
        a = p * u + pressure
        b = q * u
        d = q * (q * r) + pressure
        east.append((h - p, p - a, q - b))
        west.append((h + p, p + a, q + b))
        north.append((h - q, p - b, q - d))
        south.append((h + q, p + b, q + d))
    level = []
    for c in range(chunks):
        after, before = (c + 1) % chunks, (c - 1) % chunks
        fields = []
        for f in range(3):
            e = jnp.where(lane == 0, east[after][f], east[c][f])
            w = jnp.where(lane == LANES - 1, west[before][f], west[c][f])
            fields.append(pltpu.roll(e, LANES - 1, 1) + pltpu.roll(w, 1, 1))
        level.append(tuple(fields))
    return north, south, level


def step(src, dst, held, first, depth, chunks, factor):
    lane = lax.broadcasted_iota(jnp.int32, (SUB, LANES), 1)
    cells = [(f, c) for f in range(3) for c in range(chunks)]
    partial = south_before = None
    for n in range(depth):
        i, before = (first + n) % depth, (first + n - 1) % depth
        north, south, level = row_terms(lambda f, c: src[f, i, c], chunks, factor, lane)
        if i == 0:
            wrapped = [tuple(pltpu.roll(t, SUB - 1, 0) for t in terms) for terms in north]
        else:
            wrapped = north
        for f, c in cells:
            if n == 0:
                held[f, c] = wrapped[c][f]
            else:
                dst[f, before, c] = partial[c][f] + wrapped[c][f]
        partial = level
        if n > 0:
            partial = [
                tuple(level[c][f] + south_before[c][f] for f in range(3)) for c in range(chunks)
            ]
        south_before = south
        if i == depth - 1:
            south_before = [tuple(pltpu.roll(t, 1, 0) for t in terms) for terms in south]
    last = (first - 1) % depth
    for f, c in cells:
        if depth == 1:
            dst[f, 0, c] = partial[c][f] + held[f, c] + south_before[c][f]
        else:
            dst[f, last, c] = partial[c][f] + held[f, c]
            dst[f, first, c] = dst[f, first, c] + south_before[c][f]


def spans(chunks):
    return [slice(c * LANES, (c + 1) * LANES) for c in range(chunks)]


class Rows:
    def __init__(self, count, chunks):
        self.depth, self.chunks = count // SUB, chunks
        self.pitch = self.depth | 1

    def cells(self):
        return [
            (f, c, i) for f in range(3) for c in range(self.chunks) for i in range(self.depth)
        ]

    def pieces(self, start, count):
        found, at = [], 0
        while at < count:
            block, offset = divmod(start + at, self.depth)
            length = min(count - at, self.depth - offset)
            found.append((at, block * self.pitch + offset, length))
            at += length
        return found

    def fill(self, ext, arrays):
        start = 0
        for array in arrays:
            rows = array.shape[1]
            for at, place, length in self.pieces(start, rows):
                for f in range(3):
                    for c, span in enumerate(spans(self.chunks)):
                        ext[f, c, place : place + length, :] = array[f, at : at + length, span]
            start += rows

    def load(self, ext, state):
        for f, c, i in self.cells():
            value = ext.at[f, c][pl.ds(i, SUB, stride=self.pitch), :]
            state[0, f, i, c] = value if f == 0 else MOMENTUM * value

    def store(self, ext, state):
        shrink = 0.25**FACTOR
        for f, c, i in self.cells():
            value = state[0, f, i, c] * (shrink if f == 0 else shrink / MOMENTUM)
            ext.at[f, c][pl.ds(i, SUB, stride=self.pitch), :] = value

    def propagate(self, state, held):
        depth = self.depth

        for n in range(FACTOR):
            now, then = state.at[n % 2], state.at[(n + 1) % 2]
            step(now, then, held, n % depth, depth, self.chunks, PRESSURE * 0.25**n)

    def take(self, ext, start, count, use):
        for at, place, length in self.pieces(start, count):
            for f in range(3):
                for c, span in enumerate(spans(self.chunks)):
                    use(f, span, at, length, ext[f, c, place : place + length, :])


def put(target):
    def use(f, span, at, length, value):
        target[f, at : at + length, span] = value

    return use


def first_half(chunks, block, halo, middle, ext, state, held):
    rows = block.shape[1]
    wide = Rows(rows + 4 * FACTOR, chunks)
    wide.fill(ext, [halo.at[0], block, halo.at[1]])
    wide.load(ext, state)
    wide.propagate(state, held)
    wide.store(ext, state)
    wide.take(ext, FACTOR, rows + 2 * FACTOR, put(middle))


def second_half(chunks, middle, pushed, ext, state, held):
    rows = pushed.shape[1]
    narrow = Rows(rows + 2 * FACTOR, chunks)
    narrow.fill(ext, [middle])
    narrow.load(ext, state)
    narrow.propagate(state, held)
    narrow.store(ext, state)
    narrow.take(ext, FACTOR, rows, put(pushed))


def chain_kernel(chunks, point, own, halo, advanced, pushed, middle, *scratch):
    first_half(chunks, own.at[point], halo, middle, *scratch)
    advanced[...] = middle[:, FACTOR : FACTOR + own.shape[2], :]
    second_half(chunks, middle, pushed, *scratch)


def head_kernel(chunks, point, own, halo, advanced, middle, *scratch):
    first_half(chunks, own.at[point], halo, middle, *scratch)
    advanced[...] = middle[:, FACTOR : FACTOR + own.shape[2], :]


def finish_kernel(chunks, middle, pushed, *scratch):
    second_half(chunks, middle, pushed, *scratch)


def pack_kernel(points, groups, *refs):
    following, pushed, (packed, difference) = refs[:points], refs[points:-2], refs[-2:]
    rows = difference.shape[2]
    share = rows // groups
    for k in range(points):
        difference[k] = pushed[k][...] - following[k][...]

    @pl.when(lax.axis_index("tm") == groups - 1)
    def _():
        first = following[points - 1]
        difference[points - 1] = first[...] - first[...]

    for g in range(groups):
        part = slice(g * share, (g + 1) * share)
        for k in range(points):
            for f in range(3):
                packed[(g - groups // 2) % groups * points + k, f, 0] = difference[k, f, part, :]


VMEM = pl.BlockSpec(memory_space=pltpu.VMEM)


def call(kernel, shapes, work, rows, columns, operands, extra=()):
    chunks = columns // LANES
    extended = rows + 4 * FACTOR
    cost = pl.CostEstimate(
        flops=work * extended * columns * FACTOR * 45,
        bytes_accessed=4 * work * 3 * extended * columns,
        transcendentals=work * extended * columns * FACTOR,
    )
    return pl.pallas_call(
        functools.partial(kernel, chunks),
        out_shape=[jax.ShapeDtypeStruct(shape, jnp.float32) for shape in shapes],
        in_specs=[VMEM] * len(operands),
        out_specs=[VMEM] * len(shapes),
        scratch_shapes=[
            *extra,
            pltpu.VMEM((3, chunks, extended + SUB, LANES), jnp.float32),
            pltpu.VMEM((2, 3, extended // SUB, chunks, SUB, LANES), jnp.float32),
            pltpu.VMEM((3, chunks, SUB, LANES), jnp.float32),
        ],
        compiler_params=pltpu.CompilerParams(vmem_limit_bytes=24 * 2**20),
        cost_estimate=cost,
    )(*operands)


def chain(point, c_points, halo):
    _, fields, rows, columns = c_points.shape
    return call(
        lambda chunks, *refs: chain_kernel(chunks, point, *refs),
        [(fields, rows, columns)] * 2,
        2,
        rows,
        columns,
        (c_points, halo),
        extra=[pltpu.VMEM((fields, rows + 2 * FACTOR, columns), jnp.float32)],
    )


def head(point, c_points, halo):
    _, fields, rows, columns = c_points.shape
    return call(
        lambda chunks, *refs: head_kernel(chunks, point, *refs),
        [(fields, rows, columns), (fields, rows + 2 * FACTOR, columns)],
        1,
        rows,
        columns,
        (c_points, halo),
    )


def finish(middle, shape):
    _, rows, columns = shape
    return call(finish_kernel, [shape], 1, rows, columns, (middle,))[0]


def edges_of(block, width):
    return jnp.stack([block[..., -width:, :], block[..., :width, :]])


def route(shift, move):
    groups, strips = lax.axis_size("tm"), lax.axis_size("space")
    return [
        (t * strips + s, (t + shift) % groups * strips + (s + move) % strips)
        for t in range(groups)
        for s in range(strips)
    ]


def exchange(edges, shift):
    both = ("tm", "space")
    if lax.axis_size("space") == 2:
        return lax.ppermute(edges, both, route(shift, 1))
    return jnp.stack(
        [
            lax.ppermute(edges[0], both, route(shift, 1)),
            lax.ppermute(edges[1], both, route(shift, -1)),
        ]
    )


def pack(following, pushed, groups):
    points, (fields, rows, columns) = len(pushed), pushed[0].shape
    packet = (groups * points, fields, 1, rows // groups, columns)
    size = points * fields * rows * columns
    return pl.pallas_call(
        functools.partial(pack_kernel, points, groups),
        out_shape=jax.ShapeDtypeStruct(packet, jnp.float32),
        in_specs=[VMEM] * (2 * points),
        out_specs=VMEM,
        scratch_shapes=[pltpu.VMEM((points, fields, rows, columns), jnp.float32)],
        compiler_params=pltpu.CompilerParams(vmem_limit_bytes=24 * 2**20),
        cost_estimate=pl.CostEstimate(flops=size, bytes_accessed=12 * size, transcendentals=0),
    )(*following, *pushed)


def on_device(c_points):
    points = c_points.shape[0]
    groups = lax.axis_size("tm")
    halos = [exchange(edges_of(c_points[k], 2 * FACTOR), 0) for k in range(points)]
    first, middle = head(0, c_points, halos[0])
    ends = [(first, finish(middle, first.shape))]
    ends += [chain(k, c_points, halos[k]) for k in range(1, points)]
    advanced, pushed = zip(*ends)
    next_first = lax.ppermute(advanced[0], ("tm", "space"), route(-1, 0))
    packed = pack([*advanced[1:], next_first], pushed, groups)
    members = [[(groups // 2 + g) % groups for g in range(groups)]]
    coarse = lax.all_to_all(
        packed, "tm", split_axis=0, concat_axis=0, axis_index_groups=members, tiled=True
    )
    incoming = lax.ppermute(advanced[-1], "tm", [(i, i + 1) for i in range(groups - 1)])
    updated, _ = lax.optimization_barrier((jnp.stack([c_points[0], *advanced[:-1]]), packed))
    coarse, incoming = lax.optimization_barrier((coarse, incoming))
    opening = jnp.where(lax.axis_index("tm") == 0, c_points[0], incoming)
    updated = lax.dynamic_update_slice(updated, opening[None], (0, 0, 0, 0))
    updated, coarse = lax.optimization_barrier((updated, coarse))
    split = (groups - groups // 2) * points - 1
    return (updated, jnp.concatenate([coarse[split:], coarse[:split]], axis=0))


def solution(mesh):
    in_specs = (P("tm", None, "space", None),)
    out_specs = (P("tm", None, "space", None), P(None, None, "space", "tm", None))
    return jax.shard_map(
        on_device, mesh=mesh, in_specs=in_specs, out_specs=out_specs, check_vma=False
    )
```

```python
import functools

import jax
import jax.numpy as jnp
from jax import lax
from jax.experimental import pallas as pl
from jax.experimental.pallas import tpu as pltpu
from jax.sharding import PartitionSpec as P

FACTOR = 8
LANES = 128
SUB = 8

MOMENTUM = 0.4
PRESSURE = 0.08


def reciprocal(x):
    r = pl.reciprocal(x, approx=True)
    return r * (2.0 - x * r)


def row_terms(read, chunks, factor, lane):
    north, south, east, west = [], [], [], []
    for c in range(chunks):
        h, p, q = read(0, c), read(1, c), read(2, c)
        r = reciprocal(h)
        u = p * r
        pressure = h * h * factor
        a = p * u + pressure
        b = q * u
        d = q * (q * r) + pressure
        east.append((h - p, p - a, q - b))
        west.append((h + p, p + a, q + b))
        north.append((h - q, p - b, q - d))
        south.append((h + q, p + b, q + d))
    level = []
    for c in range(chunks):
        after, before = (c + 1) % chunks, (c - 1) % chunks
        fields = []
        for f in range(3):
            e = jnp.where(lane == 0, east[after][f], east[c][f])
            w = jnp.where(lane == LANES - 1, west[before][f], west[c][f])
            fields.append(pltpu.roll(e, LANES - 1, 1) + pltpu.roll(w, 1, 1))
        level.append(tuple(fields))
    return north, south, level


def step(src, dst, held, first, depth, chunks, factor):
    lane = lax.broadcasted_iota(jnp.int32, (SUB, LANES), 1)
    cells = [(f, c) for f in range(3) for c in range(chunks)]
    partial = south_before = None
    for n in range(depth):
        i, before = (first + n) % depth, (first + n - 1) % depth
        north, south, level = row_terms(lambda f, c: src[f, i, c], chunks, factor, lane)
        if i == 0:
            wrapped = [tuple(pltpu.roll(t, SUB - 1, 0) for t in terms) for terms in north]
        else:
            wrapped = north
        for f, c in cells:
            if n == 0:
                held[f, c] = wrapped[c][f]
            else:
                dst[f, before, c] = partial[c][f] + wrapped[c][f]
        partial = level
        if n > 0:
            partial = [
                tuple(level[c][f] + south_before[c][f] for f in range(3)) for c in range(chunks)
            ]
        south_before = south
        if i == depth - 1:
            south_before = [tuple(pltpu.roll(t, 1, 0) for t in terms) for terms in south]
    last = (first - 1) % depth
    for f, c in cells:
        if depth == 1:
            dst[f, 0, c] = partial[c][f] + held[f, c] + south_before[c][f]
        else:
            dst[f, last, c] = partial[c][f] + held[f, c]
            dst[f, first, c] = dst[f, first, c] + south_before[c][f]


def spans(chunks):
    return [slice(c * LANES, (c + 1) * LANES) for c in range(chunks)]


class Rows:
    def __init__(self, count, chunks):
        self.depth, self.chunks = count // SUB, chunks
        self.pitch = self.depth | 1

    def cells(self):
        return [
            (f, c, i) for f in range(3) for c in range(self.chunks) for i in range(self.depth)
        ]

    def pieces(self, start, count):
        found, at = [], 0
        while at < count:
            block, offset = divmod(start + at, self.depth)
            length = min(count - at, self.depth - offset)
            found.append((at, block * self.pitch + offset, length))
            at += length
        return found

    def fill(self, ext, arrays):
        start = 0
        for array in arrays:
            rows = array.shape[1]
            for at, place, length in self.pieces(start, rows):
                for f in range(3):
                    for c, span in enumerate(spans(self.chunks)):
                        ext[f, c, place : place + length, :] = array[f, at : at + length, span]
            start += rows

    def load(self, ext, state):
        for f, c, i in self.cells():
            value = ext.at[f, c][pl.ds(i, SUB, stride=self.pitch), :]
            state[0, f, i, c] = value if f == 0 else MOMENTUM * value

    def store(self, ext, state):
        shrink = 0.25**FACTOR
        for f, c, i in self.cells():
            value = state[0, f, i, c] * (shrink if f == 0 else shrink / MOMENTUM)
            ext.at[f, c][pl.ds(i, SUB, stride=self.pitch), :] = value

    def propagate(self, state, held):
        depth = self.depth

        for n in range(FACTOR):
            now, then = state.at[n % 2], state.at[(n + 1) % 2]
            step(now, then, held, n % depth, depth, self.chunks, PRESSURE * 0.25**n)

    def take(self, ext, start, count, use):
        for at, place, length in self.pieces(start, count):
            for f in range(3):
                for c, span in enumerate(spans(self.chunks)):
                    use(f, span, at, length, ext[f, c, place : place + length, :])


def put(target):
    def use(f, span, at, length, value):
        target[f, at : at + length, span] = value

    return use


def first_half(chunks, block, halo, middle, ext, state, held):
    rows = block.shape[1]
    wide = Rows(rows + 4 * FACTOR, chunks)
    wide.fill(ext, [halo.at[0], block, halo.at[1]])
    wide.load(ext, state)
    wide.propagate(state, held)
    wide.store(ext, state)
    wide.take(ext, FACTOR, rows + 2 * FACTOR, put(middle))


def second_half(chunks, middle, pushed, ext, state, held):
    rows = pushed.shape[1]
    narrow = Rows(rows + 2 * FACTOR, chunks)
    narrow.fill(ext, [middle])
    narrow.load(ext, state)
    narrow.propagate(state, held)
    narrow.store(ext, state)
    narrow.take(ext, FACTOR, rows, put(pushed))


def lay_out(groups, difference, place):
    share = difference.shape[1] // groups
    for g in range(groups):
        part = slice(g * share, (g + 1) * share)
        for f in range(3):
            place((g - groups // 2) % groups)[f, 0] = difference[f, part, :]


def chain_kernel(
    chunks, point, groups, own, halo, before, advanced, pushed, packed, middle, difference, *scratch
):
    rows = own.shape[2]
    first_half(chunks, own.at[point], halo, middle, *scratch)
    advanced[...] = middle[:, FACTOR : FACTOR + rows, :]
    difference[...] = before[...] - middle[:, FACTOR : FACTOR + rows, :]
    lay_out(groups, difference, lambda n: packed.at[n])
    second_half(chunks, middle, pushed, *scratch)


def head_kernel(chunks, point, own, halo, advanced, middle, *scratch):
    first_half(chunks, own.at[point], halo, middle, *scratch)
    advanced[...] = middle[:, FACTOR : FACTOR + own.shape[2], :]


def finish_kernel(chunks, middle, pushed, *scratch):
    second_half(chunks, middle, pushed, *scratch)


def pack_kernel(points, groups, following, pushed, *refs):
    ready, (packed, difference) = refs[: points - 1], refs[points - 1 :]
    for k in range(points - 1):
        for n in range(groups):
            packed[n * points + k] = ready[k][n]
    difference[...] = pushed[...] - following[...]

    @pl.when(lax.axis_index("tm") == groups - 1)
    def _():
        difference[...] = following[...] - following[...]

    lay_out(groups, difference, lambda n: packed.at[n * points + points - 1])


VMEM = pl.BlockSpec(memory_space=pltpu.VMEM)


def call(kernel, shapes, work, rows, columns, operands, extra=()):
    chunks = columns // LANES
    extended = rows + 4 * FACTOR
    cost = pl.CostEstimate(
        flops=work * extended * columns * FACTOR * 45,
        bytes_accessed=4 * work * 3 * extended * columns,
        transcendentals=work * extended * columns * FACTOR,
    )
    return pl.pallas_call(
        functools.partial(kernel, chunks),
        out_shape=[jax.ShapeDtypeStruct(shape, jnp.float32) for shape in shapes],
        in_specs=[VMEM] * len(operands),
        out_specs=[VMEM] * len(shapes),
        scratch_shapes=[
            *extra,
            pltpu.VMEM((3, chunks, extended + SUB, LANES), jnp.float32),
            pltpu.VMEM((2, 3, extended // SUB, chunks, SUB, LANES), jnp.float32),
            pltpu.VMEM((3, chunks, SUB, LANES), jnp.float32),
        ],
        compiler_params=pltpu.CompilerParams(vmem_limit_bytes=24 * 2**20),
        cost_estimate=cost,
    )(*operands)


def chain(point, c_points, halo, before, groups):
    _, fields, rows, columns = c_points.shape
    shape = (fields, rows, columns)
    return call(
        lambda chunks, *refs: chain_kernel(chunks, point, groups, *refs),
        [shape, shape, (groups, fields, 1, rows // groups, columns)],
        2,
        rows,
        columns,
        (c_points, halo, before),
        extra=[
            pltpu.VMEM((fields, rows + 2 * FACTOR, columns), jnp.float32),
            pltpu.VMEM(shape, jnp.float32),
        ],
    )


def head(point, c_points, halo):
    _, fields, rows, columns = c_points.shape
    return call(
        lambda chunks, *refs: head_kernel(chunks, point, *refs),
        [(fields, rows, columns), (fields, rows + 2 * FACTOR, columns)],
        1,
        rows,
        columns,
        (c_points, halo),
    )


def finish(middle, shape):
    _, rows, columns = shape
    return call(finish_kernel, [shape], 1, rows, columns, (middle,))[0]


def edges_of(block, width):
    return jnp.stack([block[..., -width:, :], block[..., :width, :]])


def route(shift, move):
    groups, strips = lax.axis_size("tm"), lax.axis_size("space")
    return [
        (t * strips + s, (t + shift) % groups * strips + (s + move) % strips)
        for t in range(groups)
        for s in range(strips)
    ]


def exchange(edges, shift):
    both = ("tm", "space")
    if lax.axis_size("space") == 2:
        return lax.ppermute(edges, both, route(shift, 1))
    return jnp.stack(
        [
            lax.ppermute(edges[0], both, route(shift, 1)),
            lax.ppermute(edges[1], both, route(shift, -1)),
        ]
    )


def pack(following, pushed, ready, groups):
    points, (fields, rows, columns) = len(ready) + 1, pushed.shape
    packet = (groups * points, fields, 1, rows // groups, columns)
    size = points * fields * rows * columns
    return pl.pallas_call(
        functools.partial(pack_kernel, points, groups),
        out_shape=jax.ShapeDtypeStruct(packet, jnp.float32),
        in_specs=[VMEM] * (points + 1),
        out_specs=VMEM,
        scratch_shapes=[pltpu.VMEM((fields, rows, columns), jnp.float32)],
        compiler_params=pltpu.CompilerParams(vmem_limit_bytes=24 * 2**20),
        cost_estimate=pl.CostEstimate(flops=size, bytes_accessed=12 * size, transcendentals=0),
    )(following, pushed, *ready)


def on_device(c_points):
    points = c_points.shape[0]
    groups = lax.axis_size("tm")
    halos = [exchange(edges_of(c_points[k], 2 * FACTOR), 0) for k in range(points)]
    first, middle = head(0, c_points, halos[0])
    advanced, pushed, ready = [first], finish(middle, first.shape), []
    for k in range(1, points):
        now, pushed, part = chain(k, c_points, halos[k], pushed, groups)
        advanced.append(now)
        ready.append(part)
    next_first = lax.ppermute(advanced[0], ("tm", "space"), route(-1, 0))
    packed = pack(next_first, pushed, ready, groups)
    members = [[(groups // 2 + g) % groups for g in range(groups)]]
    coarse = lax.all_to_all(
        packed, "tm", split_axis=0, concat_axis=0, axis_index_groups=members, tiled=True
    )
    incoming = lax.ppermute(advanced[-1], "tm", [(i, i + 1) for i in range(groups - 1)])
    updated, _ = lax.optimization_barrier((jnp.stack([c_points[0], *advanced[:-1]]), packed))
    coarse, incoming = lax.optimization_barrier((coarse, incoming))
    opening = jnp.where(lax.axis_index("tm") == 0, c_points[0], incoming)
    updated = lax.dynamic_update_slice(updated, opening[None], (0, 0, 0, 0))
    updated, coarse = lax.optimization_barrier((updated, coarse))
    split = (groups - groups // 2) * points - 1
    return (updated, jnp.concatenate([coarse[split:], coarse[:split]], axis=0))


def solution(mesh):
    in_specs = (P("tm", None, "space", None),)
    out_specs = (P("tm", None, "space", None), P(None, None, "space", "tm", None))
    return jax.shard_map(
        on_device, mesh=mesh, in_specs=in_specs, out_specs=out_specs, check_vma=False
    )
```

```python
import functools

import jax
import jax.numpy as jnp
from jax import lax
from jax.experimental import pallas as pl
from jax.experimental.pallas import tpu as pltpu
from jax.sharding import PartitionSpec as P

FACTOR = 8
LANES = 128
SUB = 8

MOMENTUM = 0.4
PRESSURE = 0.08


def reciprocal(x):
    r = pl.reciprocal(x, approx=True)
    return r * (2.0 - x * r)


def row_terms(read, chunks, factor, lane):
    north, south, east, west = [], [], [], []
    for c in range(chunks):
        h, p, q = read(0, c), read(1, c), read(2, c)
        r = reciprocal(h)
        u = p * r
        pressure = h * h * factor
        a = p * u + pressure
        b = q * u
        d = q * (q * r) + pressure
        east.append((h - p, p - a, q - b))
        west.append((h + p, p + a, q + b))
        north.append((h - q, p - b, q - d))
        south.append((h + q, p + b, q + d))
    level = []
    for c in range(chunks):
        after, before = (c + 1) % chunks, (c - 1) % chunks
        fields = []
        for f in range(3):
            e = jnp.where(lane == 0, east[after][f], east[c][f])
            w = jnp.where(lane == LANES - 1, west[before][f], west[c][f])
            fields.append(pltpu.roll(e, LANES - 1, 1) + pltpu.roll(w, 1, 1))
        level.append(tuple(fields))
    return north, south, level


def step(src, dst, held, first, depth, chunks, factor):
    lane = lax.broadcasted_iota(jnp.int32, (SUB, LANES), 1)
    cells = [(f, c) for f in range(3) for c in range(chunks)]
    partial = south_before = None
    for n in range(depth):
        i, before = (first + n) % depth, (first + n - 1) % depth
        north, south, level = row_terms(lambda f, c: src[f, i, c], chunks, factor, lane)
        if i == 0:
            wrapped = [tuple(pltpu.roll(t, SUB - 1, 0) for t in terms) for terms in north]
        else:
            wrapped = north
        for f, c in cells:
            if n == 0:
                held[f, c] = wrapped[c][f]
            else:
                dst[f, before, c] = partial[c][f] + wrapped[c][f]
        partial = level
        if n > 0:
            partial = [
                tuple(level[c][f] + south_before[c][f] for f in range(3)) for c in range(chunks)
            ]
        south_before = south
        if i == depth - 1:
            south_before = [tuple(pltpu.roll(t, 1, 0) for t in terms) for terms in south]
    last = (first - 1) % depth
    for f, c in cells:
        if depth == 1:
            dst[f, 0, c] = partial[c][f] + held[f, c] + south_before[c][f]
        else:
            dst[f, last, c] = partial[c][f] + held[f, c]
            dst[f, first, c] = dst[f, first, c] + south_before[c][f]


def spans(chunks):
    return [slice(c * LANES, (c + 1) * LANES) for c in range(chunks)]


class Rows:
    def __init__(self, count, chunks):
        self.depth, self.chunks = count // SUB, chunks
        self.pitch = self.depth | 1

    def cells(self):
        return [
            (f, c, i) for f in range(3) for c in range(self.chunks) for i in range(self.depth)
        ]

    def pieces(self, start, count):
        found, at = [], 0
        while at < count:
            block, offset = divmod(start + at, self.depth)
            length = min(count - at, self.depth - offset)
            found.append((at, block * self.pitch + offset, length))
            at += length
        return found

    def fill(self, ext, arrays):
        start = 0
        for array in arrays:
            rows = array.shape[1]
            for at, place, length in self.pieces(start, rows):
                for f in range(3):
                    for c, span in enumerate(spans(self.chunks)):
                        ext[f, c, place : place + length, :] = array[f, at : at + length, span]
            start += rows

    def load(self, ext, state):
        for f, c, i in self.cells():
            value = ext.at[f, c][pl.ds(i, SUB, stride=self.pitch), :]
            state[0, f, i, c] = value if f == 0 else MOMENTUM * value

    def store(self, ext, state):
        shrink = 0.25**FACTOR
        for f, c, i in self.cells():
            value = state[0, f, i, c] * (shrink if f == 0 else shrink / MOMENTUM)
            ext.at[f, c][pl.ds(i, SUB, stride=self.pitch), :] = value

    def propagate(self, state, held):
        depth = self.depth

        for n in range(FACTOR):
            now, then = state.at[n % 2], state.at[(n + 1) % 2]
            step(now, then, held, n % depth, depth, self.chunks, PRESSURE * 0.25**n)

    def take(self, ext, start, count, use):
        for at, place, length in self.pieces(start, count):
            for f in range(3):
                for c, span in enumerate(spans(self.chunks)):
                    use(f, span, at, length, ext[f, c, place : place + length, :])


def put(target):
    def use(f, span, at, length, value):
        target[f, at : at + length, span] = value

    return use


def first_half(chunks, block, halo, middle, ext, state, held):
    rows = block.shape[1]
    wide = Rows(rows + 4 * FACTOR, chunks)
    wide.fill(ext, [halo.at[0], block, halo.at[1]])
    wide.load(ext, state)
    wide.propagate(state, held)
    wide.store(ext, state)
    wide.take(ext, FACTOR, rows + 2 * FACTOR, put(middle))


def second_half(chunks, middle, pushed, ext, state, held):
    rows = pushed.shape[1]
    narrow = Rows(rows + 2 * FACTOR, chunks)
    narrow.fill(ext, [middle])
    narrow.load(ext, state)
    narrow.propagate(state, held)
    narrow.store(ext, state)
    narrow.take(ext, FACTOR, rows, put(pushed))


def stride_of(groups):
    return groups // 4 if groups % 4 == 0 else 1


def listed(g, groups):
    turn, rest = divmod((g - groups // 2) % groups, stride_of(groups))
    return rest * (groups // stride_of(groups)) + turn


def lay_out(groups, difference, place):
    share = difference.shape[1] // groups
    for g in range(groups):
        part = slice(g * share, (g + 1) * share)
        for f in range(3):
            place(listed(g, groups))[f, 0] = difference[f, part, :]


def chain_kernel(
    chunks, point, groups, own, halo, before, advanced, pushed, packed, middle, difference, *scratch
):
    rows = own.shape[2]
    first_half(chunks, own.at[point], halo, middle, *scratch)
    advanced[...] = middle[:, FACTOR : FACTOR + rows, :]
    difference[...] = before[...] - middle[:, FACTOR : FACTOR + rows, :]
    lay_out(groups, difference, lambda n: packed.at[n])
    second_half(chunks, middle, pushed, *scratch)


def head_kernel(chunks, point, own, halo, advanced, middle, *scratch):
    first_half(chunks, own.at[point], halo, middle, *scratch)
    advanced[...] = middle[:, FACTOR : FACTOR + own.shape[2], :]


def finish_kernel(chunks, middle, pushed, *scratch):
    second_half(chunks, middle, pushed, *scratch)


def pack_kernel(points, groups, following, pushed, *refs):
    ready, (packed, difference) = refs[: points - 1], refs[points - 1 :]
    for k in range(points - 1):
        for n in range(groups):
            packed[n * points + k] = ready[k][n]
    difference[...] = pushed[...] - following[...]

    @pl.when(lax.axis_index("tm") == groups - 1)
    def _():
        difference[...] = following[...] - following[...]

    lay_out(groups, difference, lambda n: packed.at[n * points + points - 1])


VMEM = pl.BlockSpec(memory_space=pltpu.VMEM)


def call(kernel, shapes, work, rows, columns, operands, extra=()):
    chunks = columns // LANES
    extended = rows + 4 * FACTOR
    cost = pl.CostEstimate(
        flops=work * extended * columns * FACTOR * 45,
        bytes_accessed=4 * work * 3 * extended * columns,
        transcendentals=work * extended * columns * FACTOR,
    )
    return pl.pallas_call(
        functools.partial(kernel, chunks),
        out_shape=[jax.ShapeDtypeStruct(shape, jnp.float32) for shape in shapes],
        in_specs=[VMEM] * len(operands),
        out_specs=[VMEM] * len(shapes),
        scratch_shapes=[
            *extra,
            pltpu.VMEM((3, chunks, extended + SUB, LANES), jnp.float32),
            pltpu.VMEM((2, 3, extended // SUB, chunks, SUB, LANES), jnp.float32),
            pltpu.VMEM((3, chunks, SUB, LANES), jnp.float32),
        ],
        compiler_params=pltpu.CompilerParams(vmem_limit_bytes=24 * 2**20),
        cost_estimate=cost,
    )(*operands)


def chain(point, c_points, halo, before, groups):
    _, fields, rows, columns = c_points.shape
    shape = (fields, rows, columns)
    return call(
        lambda chunks, *refs: chain_kernel(chunks, point, groups, *refs),
        [shape, shape, (groups, fields, 1, rows // groups, columns)],
        2,
        rows,
        columns,
        (c_points, halo, before),
        extra=[
            pltpu.VMEM((fields, rows + 2 * FACTOR, columns), jnp.float32),
            pltpu.VMEM(shape, jnp.float32),
        ],
    )


def head(point, c_points, halo):
    _, fields, rows, columns = c_points.shape
    return call(
        lambda chunks, *refs: head_kernel(chunks, point, *refs),
        [(fields, rows, columns), (fields, rows + 2 * FACTOR, columns)],
        1,
        rows,
        columns,
        (c_points, halo),
    )


def finish(middle, shape):
    _, rows, columns = shape
    return call(finish_kernel, [shape], 1, rows, columns, (middle,))[0]


def edges_of(block, width):
    return jnp.stack([block[..., -width:, :], block[..., :width, :]])


def route(shift, move):
    groups, strips = lax.axis_size("tm"), lax.axis_size("space")
    return [
        (t * strips + s, (t + shift) % groups * strips + (s + move) % strips)
        for t in range(groups)
        for s in range(strips)
    ]


def exchange(edges, shift):
    both = ("tm", "space")
    if lax.axis_size("space") == 2:
        return lax.ppermute(edges, both, route(shift, 1))
    return jnp.stack(
        [
            lax.ppermute(edges[0], both, route(shift, 1)),
            lax.ppermute(edges[1], both, route(shift, -1)),
        ]
    )


def pack(following, pushed, ready, groups):
    points, (fields, rows, columns) = len(ready) + 1, pushed.shape
    packet = (groups * points, fields, 1, rows // groups, columns)
    size = points * fields * rows * columns
    return pl.pallas_call(
        functools.partial(pack_kernel, points, groups),
        out_shape=jax.ShapeDtypeStruct(packet, jnp.float32),
        in_specs=[VMEM] * (points + 1),
        out_specs=VMEM,
        scratch_shapes=[pltpu.VMEM((fields, rows, columns), jnp.float32)],
        compiler_params=pltpu.CompilerParams(vmem_limit_bytes=24 * 2**20),
        cost_estimate=pl.CostEstimate(flops=size, bytes_accessed=12 * size, transcendentals=0),
    )(following, pushed, *ready)


def on_device(c_points):
    points = c_points.shape[0]
    groups = lax.axis_size("tm")
    halos = [exchange(edges_of(c_points[k], 2 * FACTOR), 0) for k in range(points)]
    first, middle = head(0, c_points, halos[0])
    advanced, pushed, ready = [first], finish(middle, first.shape), []
    for k in range(1, points):
        now, pushed, part = chain(k, c_points, halos[k], pushed, groups)
        advanced.append(now)
        ready.append(part)
    next_first = lax.ppermute(advanced[0], ("tm", "space"), route(-1, 0))
    packed = pack(next_first, pushed, ready, groups)
    members = [sorted(range(groups), key=lambda g: listed(g, groups))]
    coarse = lax.all_to_all(
        packed, "tm", split_axis=0, concat_axis=0, axis_index_groups=members, tiled=True
    )
    incoming = lax.ppermute(advanced[-1], "tm", [(i, i + 1) for i in range(groups - 1)])
    updated, _ = lax.optimization_barrier((jnp.stack([c_points[0], *advanced[:-1]]), packed))
    coarse, incoming = lax.optimization_barrier((coarse, incoming))
    opening = jnp.where(lax.axis_index("tm") == 0, c_points[0], incoming)
    updated = lax.dynamic_update_slice(updated, opening[None], (0, 0, 0, 0))
    updated, coarse = lax.optimization_barrier((updated, coarse))
    shape = coarse.shape
    steps = coarse.reshape(stride_of(groups), -1, points, *shape[1:])
    coarse = jnp.swapaxes(steps, 0, 1).reshape(shape)
    split = (groups - groups // 2) * points - 1
    return (updated, jnp.concatenate([coarse[split:], coarse[:split]], axis=0))


def solution(mesh):
    in_specs = (P("tm", None, "space", None),)
    out_specs = (P("tm", None, "space", None), P(None, None, "space", "tm", None))
    return jax.shard_map(
        on_device, mesh=mesh, in_specs=in_specs, out_specs=out_specs, check_vma=False
    )
```

```python
import functools

import jax
import jax.numpy as jnp
from jax import lax
from jax.experimental import pallas as pl
from jax.experimental.pallas import tpu as pltpu
from jax.sharding import PartitionSpec as P

FACTOR = 8
LANES = 128
SUB = 8

MOMENTUM = 0.4
PRESSURE = 0.08


def reciprocal(x):
    r = pl.reciprocal(x, approx=True)
    return r * (2.0 - x * r)


def row_terms(read, chunks, factor, lane):
    north, south, east, west = [], [], [], []
    for c in range(chunks):
        h, p, q = read(0, c), read(1, c), read(2, c)
        r = reciprocal(h)
        u = p * r
        pressure = h * h * factor
        a = p * u + pressure
        b = q * u
        d = q * (q * r) + pressure
        east.append((h - p, p - a, q - b))
        west.append((h + p, p + a, q + b))
        north.append((h - q, p - b, q - d))
        south.append((h + q, p + b, q + d))
    level = []
    for c in range(chunks):
        after, before = (c + 1) % chunks, (c - 1) % chunks
        fields = []
        for f in range(3):
            e = jnp.where(lane == 0, east[after][f], east[c][f])
            w = jnp.where(lane == LANES - 1, west[before][f], west[c][f])
            fields.append(pltpu.roll(e, LANES - 1, 1) + pltpu.roll(w, 1, 1))
        level.append(tuple(fields))
    return north, south, level


def step(src, dst, held, first, depth, chunks, factor):
    lane = lax.broadcasted_iota(jnp.int32, (SUB, LANES), 1)
    cells = [(f, c) for f in range(3) for c in range(chunks)]
    partial = south_before = None
    for n in range(depth):
        i, before = (first + n) % depth, (first + n - 1) % depth
        north, south, level = row_terms(lambda f, c: src[f, i, c], chunks, factor, lane)
        if i == 0:
            wrapped = [tuple(pltpu.roll(t, SUB - 1, 0) for t in terms) for terms in north]
        else:
            wrapped = north
        for f, c in cells:
            if n == 0:
                held[f, c] = wrapped[c][f]
            else:
                dst[f, before, c] = partial[c][f] + wrapped[c][f]
        partial = level
        if n > 0:
            partial = [
                tuple(level[c][f] + south_before[c][f] for f in range(3)) for c in range(chunks)
            ]
        south_before = south
        if i == depth - 1:
            south_before = [tuple(pltpu.roll(t, 1, 0) for t in terms) for terms in south]
    last = (first - 1) % depth
    for f, c in cells:
        if depth == 1:
            dst[f, 0, c] = partial[c][f] + held[f, c] + south_before[c][f]
        else:
            dst[f, last, c] = partial[c][f] + held[f, c]
            dst[f, first, c] = dst[f, first, c] + south_before[c][f]


def spans(chunks):
    return [slice(c * LANES, (c + 1) * LANES) for c in range(chunks)]


class Rows:
    def __init__(self, count, chunks):
        self.depth, self.chunks = count // SUB, chunks
        self.pitch = self.depth | 1

    def cells(self):
        return [
            (f, c, i) for f in range(3) for c in range(self.chunks) for i in range(self.depth)
        ]

    def pieces(self, start, count):
        found, at = [], 0
        while at < count:
            block, offset = divmod(start + at, self.depth)
            length = min(count - at, self.depth - offset)
            found.append((at, block * self.pitch + offset, length))
            at += length
        return found

    def fill(self, ext, arrays):
        start = 0
        for array in arrays:
            rows = array.shape[1]
            for at, place, length in self.pieces(start, rows):
                for f in range(3):
                    for c, span in enumerate(spans(self.chunks)):
                        ext[f, c, place : place + length, :] = array[f, at : at + length, span]
            start += rows

    def load(self, ext, state):
        for f, c, i in self.cells():
            value = ext.at[f, c][pl.ds(i, SUB, stride=self.pitch), :]
            state[0, f, i, c] = value if f == 0 else MOMENTUM * value

    def store(self, ext, state):
        shrink = 0.25**FACTOR
        for f, c, i in self.cells():
            value = state[0, f, i, c] * (shrink if f == 0 else shrink / MOMENTUM)
            ext.at[f, c][pl.ds(i, SUB, stride=self.pitch), :] = value

    def propagate(self, state, held):
        depth = self.depth

        for n in range(FACTOR):
            now, then = state.at[n % 2], state.at[(n + 1) % 2]
            step(now, then, held, n % depth, depth, self.chunks, PRESSURE * 0.25**n)

    def take(self, ext, start, count, use):
        for at, place, length in self.pieces(start, count):
            for f in range(3):
                for c, span in enumerate(spans(self.chunks)):
                    use(f, span, at, length, ext[f, c, place : place + length, :])


def put(target):
    def use(f, span, at, length, value):
        target[f, at : at + length, span] = value

    return use


def first_half(chunks, block, halo, middle, ext, state, held):
    rows = block.shape[1]
    wide = Rows(rows + 4 * FACTOR, chunks)
    wide.fill(ext, [halo.at[0], block, halo.at[1]])
    wide.load(ext, state)
    wide.propagate(state, held)
    wide.store(ext, state)
    wide.take(ext, FACTOR, rows + 2 * FACTOR, put(middle))


def second_half(chunks, middle, pushed, ext, state, held):
    rows = pushed.shape[1]
    narrow = Rows(rows + 2 * FACTOR, chunks)
    narrow.fill(ext, [middle])
    narrow.load(ext, state)
    narrow.propagate(state, held)
    narrow.store(ext, state)
    narrow.take(ext, FACTOR, rows, put(pushed))


def lay_out(groups, difference, place):
    share = difference.shape[1] // groups
    for g in range(groups):
        part = slice(g * share, (g + 1) * share)
        for f in range(3):
            place((g - groups // 2) % groups)[f, 0] = difference[f, part, :]


def chain_kernel(
    chunks, point, groups, own, halo, before, advanced, pushed, packed, middle, difference, *scratch
):
    rows = own.shape[2]
    first_half(chunks, own.at[point], halo, middle, *scratch)
    advanced[...] = middle[:, FACTOR : FACTOR + rows, :]
    difference[...] = before[...] - middle[:, FACTOR : FACTOR + rows, :]
    lay_out(groups, difference, lambda n: packed.at[n])
    second_half(chunks, middle, pushed, *scratch)


def head_kernel(chunks, point, own, halo, advanced, middle, *scratch):
    first_half(chunks, own.at[point], halo, middle, *scratch)
    advanced[...] = middle[:, FACTOR : FACTOR + own.shape[2], :]


def finish_kernel(chunks, middle, pushed, *scratch):
    second_half(chunks, middle, pushed, *scratch)


def pack_kernel(points, groups, following, pushed, *refs):
    ready, (packed, difference) = refs[: points - 1], refs[points - 1 :]
    for k in range(points - 1):
        for n in range(groups):
            packed[n * points + k] = ready[k][n]
    difference[...] = pushed[...] - following[...]

    @pl.when(lax.axis_index("tm") == groups - 1)
    def _():
        difference[...] = following[...] - following[...]

    lay_out(groups, difference, lambda n: packed.at[n * points + points - 1])


VMEM = pl.BlockSpec(memory_space=pltpu.VMEM)


def call(kernel, shapes, work, rows, columns, operands, extra=()):
    chunks = columns // LANES
    extended = rows + 4 * FACTOR
    cost = pl.CostEstimate(
        flops=work * extended * columns * FACTOR * 45,
        bytes_accessed=4 * work * 3 * extended * columns,
        transcendentals=work * extended * columns * FACTOR,
    )
    return pl.pallas_call(
        functools.partial(kernel, chunks),
        out_shape=[jax.ShapeDtypeStruct(shape, jnp.float32) for shape in shapes],
        in_specs=[VMEM] * len(operands),
        out_specs=[VMEM] * len(shapes),
        scratch_shapes=[
            *extra,
            pltpu.VMEM((3, chunks, extended + extended // SUB + SUB, LANES), jnp.float32),
            pltpu.VMEM((2, 3, extended // SUB, chunks, SUB, LANES), jnp.float32),
            pltpu.VMEM((3, chunks, SUB, LANES), jnp.float32),
        ],
        compiler_params=pltpu.CompilerParams(vmem_limit_bytes=24 * 2**20),
        cost_estimate=cost,
    )(*operands)


def chain(point, c_points, halo, before, groups):
    _, fields, rows, columns = c_points.shape
    shape = (fields, rows, columns)
    return call(
        lambda chunks, *refs: chain_kernel(chunks, point, groups, *refs),
        [shape, shape, (groups, fields, 1, rows // groups, columns)],
        2,
        rows,
        columns,
        (c_points, halo, before),
        extra=[
            pltpu.VMEM((fields, rows + 2 * FACTOR, columns), jnp.float32),
            pltpu.VMEM(shape, jnp.float32),
        ],
    )


def head(point, c_points, halo):
    _, fields, rows, columns = c_points.shape
    return call(
        lambda chunks, *refs: head_kernel(chunks, point, *refs),
        [(fields, rows, columns), (fields, rows + 2 * FACTOR, columns)],
        1,
        rows,
        columns,
        (c_points, halo),
    )


def finish(middle, shape):
    _, rows, columns = shape
    return call(finish_kernel, [shape], 1, rows, columns, (middle,))[0]


def edges_of(block, width):
    return jnp.stack([block[..., -width:, :], block[..., :width, :]])


def route(shift, move):
    groups, strips = lax.axis_size("tm"), lax.axis_size("space")
    return [
        (t * strips + s, (t + shift) % groups * strips + (s + move) % strips)
        for t in range(groups)
        for s in range(strips)
    ]


def exchange(edges, shift):
    both = ("tm", "space")
    if lax.axis_size("space") == 2:
        return lax.ppermute(edges, both, route(shift, 1))
    return jnp.stack(
        [
            lax.ppermute(edges[0], both, route(shift, 1)),
            lax.ppermute(edges[1], both, route(shift, -1)),
        ]
    )


def pack(following, pushed, ready, groups):
    points, (fields, rows, columns) = len(ready) + 1, pushed.shape
    packet = (groups * points, fields, 1, rows // groups, columns)
    size = points * fields * rows * columns
    return pl.pallas_call(
        functools.partial(pack_kernel, points, groups),
        out_shape=jax.ShapeDtypeStruct(packet, jnp.float32),
        in_specs=[VMEM] * (points + 1),
        out_specs=VMEM,
        scratch_shapes=[pltpu.VMEM((fields, rows, columns), jnp.float32)],
        compiler_params=pltpu.CompilerParams(vmem_limit_bytes=24 * 2**20),
        cost_estimate=pl.CostEstimate(flops=size, bytes_accessed=12 * size, transcendentals=0),
    )(following, pushed, *ready)


def on_device(c_points):
    points = c_points.shape[0]
    groups = lax.axis_size("tm")
    halos = [exchange(edges_of(c_points[k], 2 * FACTOR), 0) for k in range(points)]
    first, middle = head(0, c_points, halos[0])
    advanced, pushed, ready = [first], finish(middle, first.shape), []
    for k in range(1, points):
        now, pushed, part = chain(k, c_points, halos[k], pushed, groups)
        advanced.append(now)
        ready.append(part)
    next_first = lax.ppermute(advanced[0], ("tm", "space"), route(-1, 0))
    packed = pack(next_first, pushed, ready, groups)
    members = [[(groups // 2 + g) % groups for g in range(groups)]]
    coarse = lax.all_to_all(
        packed, "tm", split_axis=0, concat_axis=0, axis_index_groups=members, tiled=True
    )
    incoming = lax.ppermute(advanced[-1], "tm", [(i, i + 1) for i in range(groups - 1)])
    updated, _ = lax.optimization_barrier((jnp.stack([c_points[0], *advanced[:-1]]), packed))
    coarse, incoming = lax.optimization_barrier((coarse, incoming))
    opening = jnp.where(lax.axis_index("tm") == 0, c_points[0], incoming)
    updated = lax.dynamic_update_slice(updated, opening[None], (0, 0, 0, 0))
    updated, coarse = lax.optimization_barrier((updated, coarse))
    split = (groups - groups // 2) * points - 1
    return (updated, jnp.concatenate([coarse[split:], coarse[:split]], axis=0))


def solution(mesh):
    in_specs = (P("tm", None, "space", None),)
    out_specs = (P("tm", None, "space", None), P(None, None, "space", "tm", None))
    return jax.shard_map(
        on_device, mesh=mesh, in_specs=in_specs, out_specs=out_specs, check_vma=False
    )
```
